32 devices in a mesh: depth: 4 (over x, core), tile: 8 (over z, y).
Axes of the slice: x: 2, y: 2, z: 4, core: 2. Of those that a mesh axis runs over, the one named last changes fastest.
Arguments:
- incident: float32 [2, 3, 256, 512], P(None, None, 'tile'), may hold values from -6 to 6
- delta: float32 [3, 8, 256, 512], P(None, 'depth', 'tile'), may hold values from 0 to 1
- beta: float32 [3, 8, 256, 512], P(None, 'depth', 'tile'), may hold values from 0 to 0.5
- view_order: int32 [3], replicated, may hold values from 0 to 2, each once
Outputs:
- slab_waves: float32 [2, 3, 4, 256, 512], P(None, None, 'depth', 'tile')
The draws below stay inside these ranges and needn't reach their ends.
Inputs may be any that keep to these rules, and one draw needn't show every extreme that they name: `view_order`: each view appears once.
All inputs are finite; a program needn't handle non-finite values.
Results may differ from the reference program's by a relative error of at most 0.0001.
Values sent between devices are 32-bit elements; how exact they have to be, the bound alone decides.
A program may use at most 64 MiB of HBM per device.

```python
import jax
import jax.numpy as jnp
from jax import lax

VIEWS = 3
SLAB = 2
HALF = 32
COLS = 512
NX = 256
SLICES = 8


def block_scale(key, dims, split, least, top_value):
    level = 1.0
    for position, blocks in split:
        heights = jax.random.uniform(jax.random.fold_in(jax.random.fold_in(key, 6), position), (blocks,), jnp.float32, least / len(split), top_value / len(split))
        level = level * jnp.repeat(jnp.exp(heights), dims[position] // blocks).reshape((-1,) + (1,) * (len(dims) - 1 - position))
    return level


def centred(stream_key, shape, scale, bound, pieces=(), held_as=jnp.bfloat16):
    drawn = scale * jax.random.normal(stream_key, shape, jnp.float32)
    if pieces:
        drawn = drawn * block_scale(stream_key, shape, pieces, -0.22, 0.18)
    return jnp.clip(drawn, -bound, bound).astype(held_as)


def setup_inputs(seed: int = 0) -> dict:
    arg_keys = jax.random.split(jax.random.key(seed), 5)
    return {
        "incident": centred(arg_keys[0], (2, VIEWS, NX, COLS), 1.0, 6.0, ((2, 8),), jnp.float32),
        "delta": jnp.clip(1.0 * jax.random.uniform(arg_keys[1], (VIEWS, SLICES, NX, COLS), jnp.float32) ** block_scale(arg_keys[1], (VIEWS, SLICES, NX, COLS), ((1, 4), (2, 8)), -0.2, 0.2), 0.0, 1.0),
        "beta": jnp.clip(0.5 * jax.random.uniform(arg_keys[2], (VIEWS, SLICES, NX, COLS), jnp.float32) ** block_scale(arg_keys[2], (VIEWS, SLICES, NX, COLS), ((1, 4), (2, 8)), -0.2, 0.2), 0.0, 0.5),
        "view_order": jax.random.permutation(arg_keys[3], VIEWS).astype(jnp.int32),
    }


def tap_table(half):
    grid = jnp.arange(-half, half + 1).astype(jnp.float32)
    window = 0.75 + 0.25 * jnp.cos(jnp.pi * grid / (half + 1))
    angle = jnp.pi * grid * grid / (6.25 * half)
    real_part = window * jnp.cos(angle)
    imag_part = window * jnp.sin(angle)
    norm = jnp.sqrt(jnp.sum(real_part) ** 2 + jnp.sum(imag_part) ** 2)
    return (real_part / norm, imag_part / norm)

def convolve(field, taps_re, taps_im, along_rows):
    kernel = jnp.stack([jnp.stack([taps_re, -taps_im]), jnp.stack([taps_im, taps_re])])
    if along_rows:
        kernel = kernel[:, :, :, None]
        padding = ((HALF, HALF), (0, 0))
    else:
        kernel = kernel[:, :, None, :]
        padding = ((0, 0), (HALF, HALF))
    result = lax.conv_general_dilated(field[None], kernel.astype(field.dtype), (1, 1), padding, dimension_numbers=('NCHW', 'OIHW', 'NCHW'), precision=lax.Precision.HIGHEST)
    return result[0]

def reference(incident, delta, beta, view_order):
    taps_re, taps_im = tap_table(HALF)
    stored = []
    for slot in range(VIEWS):
        view = view_order[slot]
        field = jnp.take(incident, view, axis=1)
        slabs = []
        for piece in range(SLICES):
            amp = jnp.exp(-jnp.take(beta, view, axis=0)[piece])
            phase = -jnp.pi * jnp.take(delta, view, axis=0)[piece]
            trans_re = amp * jnp.cos(phase)
            trans_im = amp * jnp.sin(phase)
            field = jnp.stack([field[0] * trans_re - field[1] * trans_im, field[0] * trans_im + field[1] * trans_re])
            field = convolve(field, taps_re, taps_im, True)
            field = convolve(field, taps_re, taps_im, False)
            if piece % SLAB == SLAB - 1:
                slabs.append(field)
        stored.append(jnp.stack(slabs, axis=1))
    return jnp.stack(stored, axis=1)
```

```python
import functools

import jax
import jax.numpy as jnp
import ml_dtypes
import numpy as np
from jax import lax
from jax.experimental import pallas as pl
from jax.experimental.pallas import tpu as pltpu
from jax.sharding import PartitionSpec as P

HALF = 32
LANES = 128
PAIR = 2
MESH = pl.DeviceIdType.MESH

SIN_TERMS = (
    3.1415926535897931,
    -5.1677127800499694,
    2.5501640398773450,
    -0.59926452932079199,
    0.082145886611128236,
    -0.0073704309457143504,
    0.00046630280576761250,
)
COS_TERMS = (
    1.0,
    -4.9348022005446790,
    4.0587121264167676,
    -1.3352627688545893,
    0.23533063035889312,
    -0.025806891390014061,
    0.0019295743094039231,
    -0.00010463810492484570,
)


def series(square, terms):
    total = jnp.full_like(square, terms[-1])
    for term in terms[-2::-1]:
        total = total * square + term
    return total


def taps(offset, half):
    grid = np.arange(-half, half + 1, dtype=np.float64)
    norm = np.abs(
        np.sum((0.75 + 0.25 * np.cos(np.pi * grid / (half + 1))) * np.exp(1j * np.pi * grid**2 / (6.25 * half)))
    )
    place = offset.astype(np.float64)
    value = (0.75 + 0.25 * np.cos(np.pi * place / (half + 1))) * np.exp(1j * np.pi * place**2 / (6.25 * half))
    value = np.where(np.abs(offset) <= half, value / norm, 0.0)
    return value.real, value.imag


def in_two(matrix):
    matrix = matrix.astype(np.float32)
    high = matrix.astype(ml_dtypes.bfloat16)
    low = (matrix - high.astype(np.float32)).astype(ml_dtypes.bfloat16)
    return high, low


def row_matrix(rows, half):
    target, source = np.mgrid[0:rows, 0 : rows + 2 * half]
    real_part, imag_part = taps(source - half - target, half)
    return np.block([[real_part, -imag_part], [imag_part, real_part]])


def column_matrix(block, edge, half):
    source, target = np.mgrid[0 : block + 2 * edge, 0:block]
    real_part, imag_part = taps(source - edge - target, half)
    return np.block([[real_part, imag_part], [-imag_part, real_part]])


def split(value):
    high = value.astype(jnp.bfloat16)
    low = (value - high.astype(jnp.float32)).astype(jnp.bfloat16)
    return high, low


def dot(a, b):
    return jnp.dot(a, b, preferred_element_type=jnp.float32)


def body(
    depths, tiles, views, rows, cols, per_slab,
    incident_ref, delta_ref, beta_ref, rmat_ref, cmat_ref, out_ref,
    start_buf, volume, wave, field, trans, leaving,
    start_send, start_recv, vol_send, vol_recv, rim_send, rim_recv, out_send, out_recv,
):
    half = HALF
    span = PAIR * rows
    slices = depths * per_slab
    blocks = cols // LANES
    edge = LANES // 2
    d = lax.axis_index("depth")
    t = lax.axis_index("tile")
    pair = t // PAIR
    q = t % PAIR
    pairs = tiles // PAIR
    mine = (d // 2) * PAIR + q
    works = (d % 2 == 0) & (mine < views)
    places = [((v // PAIR) * 2, v % PAIR) for v in range(views)]

    barrier = pltpu.get_barrier_semaphore()
    for dd in range(depths):
        for qq in range(PAIR):
            here = (d == dd) & (q == qq)
            peer = (dd, pair * PAIR + qq)
            if (dd, qq) in places:

                @pl.when(jnp.logical_not(here))
                def _():
                    pl.semaphore_signal(barrier, inc=1, device_id=peer, device_id_type=MESH)
            else:

                @pl.when(works)
                def _():
                    pl.semaphore_signal(barrier, inc=1, device_id=peer, device_id_type=MESH)

    has_up = works & (pair > 0)
    has_down = works & (pair < pairs - 1)
    up = (d, jnp.maximum(t - PAIR, 0))
    down = (d, jnp.minimum(t + PAIR, tiles - 1))

    @pl.when(has_up)
    def _():
        pl.semaphore_signal(barrier, inc=1, device_id=up, device_id_type=MESH)

    @pl.when(has_down)
    def _():
        pl.semaphore_signal(barrier, inc=1, device_id=down, device_id_type=MESH)

    peers = jnp.where(works, depths * PAIR - 1, views)
    pl.semaphore_wait(barrier, peers + has_up.astype(jnp.int32) + has_down.astype(jnp.int32))

    def piece_copy(ref, c, i, v, target):
        return pltpu.make_async_remote_copy(
            src_ref=ref.at[v, i],
            dst_ref=volume.at[d * per_slab + i, c, q],
            send_sem=vol_send.at[i, c, v],
            recv_sem=vol_recv.at[d * per_slab + i, c, q],
            device_id=target,
            device_id_type=MESH,
        )

    def start_copy(v, target):
        return pltpu.make_async_remote_copy(
            src_ref=incident_ref.at[:, v],
            dst_ref=start_buf.at[q],
            send_sem=start_send,
            recv_sem=start_recv.at[q],
            device_id=target,
            device_id_type=MESH,
        )

    for v, (dd, qq) in enumerate(places):
        target = (dd, pair * PAIR + qq)

        @pl.when((d == dd) & (q != qq))
        def _():
            start_copy(v, target).start()

        @pl.when((d == dd) & (q == qq))
        def _():
            pltpu.make_async_copy(incident_ref.at[:, v], start_buf.at[q], start_recv.at[q]).start()

    for i in range(per_slab):
        for v, (dd, qq) in enumerate(places):
            target = (dd, pair * PAIR + qq)
            here = (d == dd) & (q == qq)
            for c, ref in enumerate((delta_ref, beta_ref)):

                @pl.when(here)
                def _():
                    pltpu.make_async_copy(
                        ref.at[v, i], volume.at[d * per_slab + i, c, q], vol_recv.at[d * per_slab + i, c, q]
                    ).start()

                @pl.when(jnp.logical_not(here))
                def _():
                    piece_copy(ref, c, i, v, target).start()

    def out_copy(slab, qq):
        return pltpu.make_async_remote_copy(
            src_ref=leaving.at[slab, :, pl.ds(qq * rows, rows)],
            dst_ref=out_ref.at[:, mine, 0],
            send_sem=out_send.at[slab, qq],
            recv_sem=out_recv.at[mine],
            device_id=(slab, pair * PAIR + qq),
            device_id_type=MESH,
        )

    def rim_copy(s, side):
        first = half if side == 0 else span
        land = span + half if side == 0 else 0
        return pltpu.make_async_remote_copy(
            src_ref=wave.at[s, :, pl.ds(first, half)],
            dst_ref=wave.at[s, :, pl.ds(land, half)],
            send_sem=rim_send.at[s, side],
            recv_sem=rim_recv.at[s, 1 - side],
            device_id=up if side == 0 else down,
            device_id_type=MESH,
        )

    def rim_arrival(s, side):
        land = 0 if side == 0 else span + half
        ref = wave.at[s, :, pl.ds(land, half)]
        return pltpu.make_async_copy(ref, ref, rim_recv.at[s, side])

    def transmission(s):
        for c in range(2):
            for qq in range(PAIR):
                ref = volume.at[s, c, qq]
                pltpu.make_async_copy(ref, ref, vol_recv.at[s, c, qq]).wait()
        u = volume[s, 0].reshape(span, cols) - 0.5
        amp = jnp.exp(-volume[s, 1].reshape(span, cols))
        square = u * u
        trans[0] = -amp * (u * series(square, SIN_TERMS))
        trans[1] = -amp * series(square, COS_TERMS)

    @pl.when(works)
    def _():
        @pl.when(pair == 0)
        def _():
            wave[:, :, 0:half] = jnp.zeros((slices, 2, half, cols), jnp.float32)

        @pl.when(pair == pairs - 1)
        def _():
            wave[:, :, span + half :] = jnp.zeros((slices, 2, half, cols), jnp.float32)

        for qq in range(PAIR):
            pltpu.make_async_copy(start_buf.at[qq], start_buf.at[qq], start_recv.at[qq]).wait()
        for qq in range(PAIR):
            field[:, qq * rows : (qq + 1) * rows] = start_buf[qq]
        transmission(0)

        @pl.loop(0, slices)
        def _(s):
            wave[s, 0, half : half + span] = field[0] * trans[0] - field[1] * trans[1]
            wave[s, 1, half : half + span] = field[0] * trans[1] + field[1] * trans[0]

            @pl.when(has_up)
            def _():
                rim_copy(s, 0).start()

            @pl.when(has_down)
            def _():
                rim_copy(s, 1).start()

            @pl.when(s < slices - 1)
            def _():
                transmission(s + 1)

            @pl.when(has_up)
            def _():
                rim_arrival(s, 0).wait()

            @pl.when(has_down)
            def _():
                rim_arrival(s, 1).wait()

            high, low = split(wave[s].reshape(2 * (span + 2 * half), cols))
            both = dot(rmat_ref[...], high)
            count = 2 * span
            wide = both[:count] + both[count:] + dot(rmat_ref[:count], low)
            windows = []
            for part in range(2):
                padded = jnp.concatenate(
                    [wide[part * span : (part + 1) * span], jnp.zeros((span, LANES), jnp.float32)], axis=1
                )
                padded = pltpu.roll(padded, edge, 1)
                windows.append(
                    jnp.concatenate([padded[:, b * LANES : (b + 2) * LANES] for b in range(blocks)], axis=0)
                )
            high, low = split(jnp.concatenate(windows, axis=1))
            result = dot(high, cmat_ref[0]) + dot(low, cmat_ref[0]) + dot(high, cmat_ref[1])
            for part in range(2):
                for b in range(blocks):
                    field[part, :, b * LANES : (b + 1) * LANES] = result[
                        b * span : (b + 1) * span, part * LANES : (part + 1) * LANES
                    ]

            @pl.when(s % per_slab == per_slab - 1)
            def _():
                slab = s // per_slab
                leaving[slab] = field[...]
                for qq in range(PAIR):
                    here = (d == slab) & (q == qq)

                    @pl.when(here)
                    def _():
                        pltpu.make_async_copy(
                            leaving.at[slab, :, pl.ds(qq * rows, rows)], out_ref.at[:, mine, 0], out_recv.at[mine]
                        ).start()

                    @pl.when(jnp.logical_not(here))
                    def _():
                        out_copy(slab, qq).start()

    for v, (dd, qq) in enumerate(places):
        target = (dd, pair * PAIR + qq)
        here = (d == dd) & (q == qq)

        @pl.when((d == dd) & (q != qq))
        def _():
            start_copy(v, target).wait_send()

        @pl.when(jnp.logical_not(here))
        def _():
            for i in range(per_slab):
                for c, ref in enumerate((delta_ref, beta_ref)):
                    piece_copy(ref, c, i, v, target).wait_send()

    for v in range(views):
        ref = out_ref.at[:, v, 0]
        pltpu.make_async_copy(ref, ref, out_recv.at[v]).wait()

    @pl.when(works)
    def _():
        @pl.loop(0, slices)
        def _(s):
            @pl.when(has_up)
            def _():
                rim_copy(s, 0).wait_send()

            @pl.when(has_down)
            def _():
                rim_copy(s, 1).wait_send()

        @pl.loop(0, depths)
        def _(slab):
            for qq in range(PAIR):

                @pl.when(jnp.logical_not((d == slab) & (q == qq)))
                def _():
                    out_copy(slab, qq).wait_send()


def in_order(views, order_ref, value_ref, out_ref):
    for k in range(views):
        out_ref[:, k] = value_ref[:, order_ref[k]]


def per_device(depths, tiles, incident, delta, beta, view_order):
    half = HALF
    _, views, rows, cols = incident.shape
    per_slab = delta.shape[1]
    slices = per_slab * depths
    span = PAIR * rows
    edge = LANES // 2
    rmat = jnp.asarray(np.concatenate(in_two(row_matrix(span, half)), axis=0))
    cmat = jnp.asarray(np.stack(in_two(column_matrix(LANES, edge, half))))
    anywhere = pl.BlockSpec(memory_space=pl.ANY)
    vmem = pl.BlockSpec(memory_space=pltpu.VMEM)
    shape = jax.ShapeDtypeStruct((2, views, 1, rows, cols), jnp.float32)
    f32 = jnp.float32
    dma = pltpu.SemaphoreType.DMA
    by_view = pl.pallas_call(
        functools.partial(body, depths, tiles, views, rows, cols, per_slab),
        out_shape=shape,
        in_specs=[anywhere, anywhere, anywhere, vmem, vmem],
        out_specs=anywhere,
        scratch_shapes=[
            pltpu.VMEM((PAIR, 2, rows, cols), f32),
            pltpu.VMEM((slices, 2, PAIR, rows, cols), f32),
            pltpu.VMEM((slices, 2, span + 2 * half, cols), f32),
            pltpu.VMEM((2, span, cols), f32),
            pltpu.VMEM((2, span, cols), f32),
            pltpu.VMEM((depths, 2, span, cols), f32),
            dma,
            dma((PAIR,)),
            dma((per_slab, 2, views)),
            dma((slices, 2, PAIR)),
            dma((slices, 2)),
            dma((slices, 2)),
            dma((depths, PAIR)),
            dma((views,)),
        ],
        compiler_params=pltpu.CompilerParams(
            collective_id=0, has_side_effects=True, vmem_limit_bytes=40 * 1024 * 1024
        ),
        name="views_by_worker",
    )(incident, delta, beta, rmat, cmat)
    return pl.pallas_call(
        functools.partial(in_order, views),
        out_shape=shape,
        in_specs=[pl.BlockSpec(memory_space=pltpu.SMEM), vmem],
        out_specs=vmem,
        name="stored_order",
    )(view_order, by_view)


def solution(mesh):
    return jax.shard_map(
        functools.partial(per_device, mesh.shape["depth"], mesh.shape["tile"]),
        mesh=mesh,
        in_specs=(
            P(None, None, "tile", None),
            P(None, "depth", "tile", None),
            P(None, "depth", "tile", None),
            P(),
        ),
        out_specs=P(None, None, "depth", "tile", None),
        check_vma=False,
    )
```

```python
import functools

import jax
import jax.numpy as jnp
import ml_dtypes
import numpy as np
from jax import lax
from jax.experimental import pallas as pl
from jax.experimental.pallas import tpu as pltpu
from jax.sharding import PartitionSpec as P

HALF = 32
LANES = 128
PAIR = 2
PARTS = 2
MESH = pl.DeviceIdType.MESH

SIN_TERMS = (
    3.1415926535897931,
    -5.1677127800499694,
    2.5501640398773450,
    -0.59926452932079199,
    0.082145886611128236,
    -0.0073704309457143504,
    0.00046630280576761250,
)
COS_TERMS = (
    1.0,
    -4.9348022005446790,
    4.0587121264167676,
    -1.3352627688545893,
    0.23533063035889312,
    -0.025806891390014061,
    0.0019295743094039231,
    -0.00010463810492484570,
)


def series(square, terms):
    total = jnp.full_like(square, terms[-1])
    for term in terms[-2::-1]:
        total = total * square + term
    return total


def taps(offset, half):
    grid = np.arange(-half, half + 1, dtype=np.float64)
    norm = np.abs(
        np.sum((0.75 + 0.25 * np.cos(np.pi * grid / (half + 1))) * np.exp(1j * np.pi * grid**2 / (6.25 * half)))
    )
    place = offset.astype(np.float64)
    value = (0.75 + 0.25 * np.cos(np.pi * place / (half + 1))) * np.exp(1j * np.pi * place**2 / (6.25 * half))
    value = np.where(np.abs(offset) <= half, value / norm, 0.0)
    return value.real, value.imag


def in_two(matrix):
    matrix = matrix.astype(np.float32)
    high = matrix.astype(ml_dtypes.bfloat16)
    low = (matrix - high.astype(np.float32)).astype(ml_dtypes.bfloat16)
    return high, low


def row_matrix(rows, half):
    target, source = np.mgrid[0:rows, 0 : rows + 2 * half]
    real_part, imag_part = taps(source - half - target, half)
    return np.block([[real_part, -imag_part], [imag_part, real_part]])


def column_matrix(block, edge, half):
    source, target = np.mgrid[0 : block + 2 * edge, 0:block]
    real_part, imag_part = taps(source - edge - target, half)
    return np.block([[real_part, imag_part], [-imag_part, real_part]])


def split(value):
    high = value.astype(jnp.bfloat16)
    low = (value - high.astype(jnp.float32)).astype(jnp.bfloat16)
    return high, low


def dot(a, b):
    return jnp.dot(a, b, preferred_element_type=jnp.float32)


def transmitted(delta, beta):
    u = delta - 0.5
    amp = jnp.exp(-beta)
    square = u * u
    return -amp * (u * series(square, SIN_TERMS)), -amp * series(square, COS_TERMS)


def body(
    depths, tiles, views, rows, cols, per_slab,
    incident_ref, delta_ref, beta_ref, rmat_ref, cmat_ref, out_ref,
    loads, first, volume, wave, trans, leaving, rmat_buf, cmat_buf,
    load_sem, first_send, first_recv, vol_send, vol_recv, rim_send, rim_recv, out_send, out_recv, go,
):
    half = HALF
    span = PAIR * rows
    slices = depths * per_slab
    blocks = cols // LANES
    edge = LANES // 2
    d = lax.axis_index("depth")
    t = lax.axis_index("tile")
    pair = t // PAIR
    q = t % PAIR
    pairs = tiles // PAIR
    mine = (d // 2) * PAIR + q
    works = (d % 2 == 0) & (mine < views)
    places = [((v // PAIR) * 2, v % PAIR) for v in range(views)]

    taps_in = [
        pltpu.make_async_copy(rmat_ref, rmat_buf, load_sem.at[0]),
        pltpu.make_async_copy(cmat_ref, cmat_buf, load_sem.at[1]),
    ]
    first_in = [
        pltpu.make_async_copy(incident_ref.at[0], loads.at[0], load_sem.at[2]),
        pltpu.make_async_copy(incident_ref.at[1], loads.at[1], load_sem.at[3]),
        pltpu.make_async_copy(delta_ref.at[:, 0], loads.at[2], load_sem.at[4]),
        pltpu.make_async_copy(beta_ref.at[:, 0], loads.at[3], load_sem.at[5]),
    ]

    @pl.when(d == 0)
    def _():
        for copy in first_in:
            copy.start()

    @pl.when(works)
    def _():
        for copy in taps_in:
            copy.start()

    barrier = pltpu.get_barrier_semaphore()
    for dd in range(depths):
        for qq in range(PAIR):
            here = (d == dd) & (q == qq)
            peer = (dd, pair * PAIR + qq)
            if (dd, qq) in places:

                @pl.when(jnp.logical_not(here))
                def _():
                    pl.semaphore_signal(barrier, inc=1, device_id=peer, device_id_type=MESH)
            else:

                @pl.when(works)
                def _():
                    pl.semaphore_signal(barrier, inc=1, device_id=peer, device_id_type=MESH)

    has_up = works & (pair > 0)
    has_down = works & (pair < pairs - 1)
    up = (d, jnp.maximum(t - PAIR, 0))
    down = (d, jnp.minimum(t + PAIR, tiles - 1))

    @pl.when(has_up)
    def _():
        pl.semaphore_signal(barrier, inc=1, device_id=up, device_id_type=MESH)

    @pl.when(has_down)
    def _():
        pl.semaphore_signal(barrier, inc=1, device_id=down, device_id_type=MESH)

    peers = jnp.where(works, depths * PAIR - 1, views)
    pl.semaphore_wait(barrier, peers + has_up.astype(jnp.int32) + has_down.astype(jnp.int32))

    def piece_copy(i, c, v, target):
        return pltpu.make_async_remote_copy(
            src_ref=(delta_ref, beta_ref)[c].at[v, i],
            dst_ref=volume.at[d * per_slab + i, c, q],
            send_sem=vol_send.at[i, c, v],
            recv_sem=vol_recv.at[d * per_slab + i, c, q],
            device_id=target,
            device_id_type=MESH,
        )

    def send_pieces(i, v):
        dd, qq = places[v]
        here = (d == dd) & (q == qq)
        for c, ref in enumerate((delta_ref, beta_ref)):

            @pl.when(here)
            def _():
                pltpu.make_async_copy(
                    ref.at[v, i], volume.at[d * per_slab + i, c, q], vol_recv.at[d * per_slab + i, c, q]
                ).start()

            @pl.when(jnp.logical_not(here))
            def _():
                piece_copy(i, c, v, (dd, pair * PAIR + qq)).start()

    def first_copy(v):
        dd, qq = places[v]
        return pltpu.make_async_remote_copy(
            src_ref=first.at[v],
            dst_ref=wave.at[0, :, pl.ds(half + q * rows, rows)],
            send_sem=first_send.at[v],
            recv_sem=first_recv.at[q],
            device_id=(dd, pair * PAIR + qq),
            device_id_type=MESH,
        )

    @pl.when(d == 0)
    def _():
        for copy in first_in:
            copy.wait()
        for v, (dd, qq) in enumerate(places):
            real_part, imag_part = transmitted(loads[2, v], loads[3, v])
            first[v, 0] = loads[0, v] * real_part - loads[1, v] * imag_part
            first[v, 1] = loads[0, v] * imag_part + loads[1, v] * real_part
            here = (d == dd) & (q == qq)

            @pl.when(here)
            def _():
                pltpu.make_async_copy(
                    first.at[v], wave.at[0, :, pl.ds(half + q * rows, rows)], first_recv.at[q]
                ).start()

            @pl.when(jnp.logical_not(here))
            def _():
                first_copy(v).start()

        for v, (dd, qq) in enumerate(places):

            @pl.when(jnp.logical_not((d == dd) & (q == qq)))
            def _():
                first_copy(v).wait_send()

        for i in range(1, per_slab):
            for v in range(views):
                send_pieces(i, v)

    @pl.when((d > 0) & jnp.logical_not(works))
    def _():
        for v in range(views):
            pl.semaphore_wait(go.at[v], 1)
            for i in range(per_slab):
                send_pieces(i, v)

    def out_copy(slab, qq):
        return pltpu.make_async_remote_copy(
            src_ref=leaving.at[slab, :, pl.ds(qq * rows, rows)],
            dst_ref=out_ref.at[:, mine, 0],
            send_sem=out_send.at[slab, qq],
            recv_sem=out_recv.at[mine],
            device_id=(slab, pair * PAIR + qq),
            device_id_type=MESH,
        )

    wide_cols = cols // PARTS

    def rim_copy(s, side, h):
        first_row = half if side == 0 else span
        land = span + half if side == 0 else 0
        columns = pl.ds(h * wide_cols, wide_cols)
        return pltpu.make_async_remote_copy(
            src_ref=wave.at[s, :, pl.ds(first_row, half), columns],
            dst_ref=wave.at[s, :, pl.ds(land, half), columns],
            send_sem=rim_send.at[s, side, h],
            recv_sem=rim_recv.at[s, 1 - side, h],
            device_id=up if side == 0 else down,
            device_id_type=MESH,
        )

    def send_rims(s, h):
        @pl.when(has_up)
        def _():
            rim_copy(s, 0, h).start()

        @pl.when(has_down)
        def _():
            rim_copy(s, 1, h).start()

    def rim_arrival(s, side, h):
        land = 0 if side == 0 else span + half
        ref = wave.at[s, :, pl.ds(land, half), pl.ds(h * wide_cols, wide_cols)]
        return pltpu.make_async_copy(ref, ref, rim_recv.at[s, side, h])

    def transmission(s):
        for c in range(2):
            for qq in range(PAIR):
                ref = volume.at[s, c, qq]
                pltpu.make_async_copy(ref, ref, vol_recv.at[s, c, qq]).wait()
        trans[0], trans[1] = transmitted(volume[s, 0].reshape(span, cols), volume[s, 1].reshape(span, cols))

    @pl.when(works)
    def _():
        @pl.when(pair == 0)
        def _():
            wave[:, :, 0:half] = jnp.zeros((slices, 2, half, cols), jnp.float32)

        @pl.when(pair == pairs - 1)
        def _():
            wave[:, :, span + half :] = jnp.zeros((slices, 2, half, cols), jnp.float32)

        for copy in taps_in:
            copy.wait()
        for qq in range(PAIR):
            ref = wave.at[0, :, pl.ds(half + qq * rows, rows)]
            pltpu.make_async_copy(ref, ref, first_recv.at[qq]).wait()
        for h in range(PARTS):
            send_rims(0, h)

        @pl.loop(0, slices)
        def _(s):
            for dd in range(1, depths):

                @pl.when(s == max(0, (dd - 1) * per_slab - 1))
                def _():
                    for qq in range(PAIR):
                        if (dd, qq) in places:

                            @pl.when((d == dd) & (q == qq))
                            def _():
                                for i in range(per_slab):
                                    for v in range(views):
                                        send_pieces(i, v)
                        else:
                            pl.semaphore_signal(
                                go.at[mine], inc=1, device_id=(dd, pair * PAIR + qq), device_id_type=MESH
                            )

            @pl.when(s < slices - 1)
            def _():
                transmission(s + 1)

            count = 2 * span
            parts = []
            for h in range(PARTS):

                @pl.when(has_up)
                def _():
                    rim_arrival(s, 0, h).wait()

                @pl.when(has_down)
                def _():
                    rim_arrival(s, 1, h).wait()

                columns = slice(h * wide_cols, (h + 1) * wide_cols)
                high, low = split(wave[s, :, :, columns].reshape(2 * (span + 2 * half), wide_cols))
                both = dot(rmat_buf[...], high)
                parts.append(both[:count] + both[count:] + dot(rmat_buf[:count], low))
            padded = jnp.concatenate(parts + [jnp.zeros((count, LANES), jnp.float32)], axis=1)
            high, low = split(pltpu.roll(padded, edge, 1))
            per_part = blocks // PARTS
            for h in range(PARTS):
                mine_blocks = range(h * per_part, (h + 1) * per_part)

                def windows(value):
                    return jnp.concatenate(
                        [
                            jnp.concatenate(
                                [
                                    value[:span, b * LANES : (b + 2) * LANES],
                                    value[span:, b * LANES : (b + 2) * LANES],
                                ],
                                axis=1,
                            )
                            for b in mine_blocks
                        ],
                        axis=0,
                    )

                high_h = windows(high)
                result = dot(high_h, cmat_buf[0]) + dot(windows(low), cmat_buf[0]) + dot(high_h, cmat_buf[1])
                real_part, imag_part = [
                    jnp.concatenate(
                        [
                            result[k * span : (k + 1) * span, part * LANES : (part + 1) * LANES]
                            for k in range(per_part)
                        ],
                        axis=1,
                    )
                    for part in range(2)
                ]
                columns = slice(h * wide_cols, (h + 1) * wide_cols)

                @pl.when(s < slices - 1)
                def _():
                    trans_re, trans_im = trans[0, :, columns], trans[1, :, columns]
                    wave[s + 1, 0, half : half + span, columns] = real_part * trans_re - imag_part * trans_im
                    wave[s + 1, 1, half : half + span, columns] = real_part * trans_im + imag_part * trans_re
                    send_rims(s + 1, h)

                @pl.when(s % per_slab == per_slab - 1)
                def _():
                    leaving[s // per_slab, 0, :, columns] = real_part
                    leaving[s // per_slab, 1, :, columns] = imag_part

            @pl.when(s % per_slab == per_slab - 1)
            def _():
                slab = s // per_slab
                for qq in range(PAIR):
                    here = (d == slab) & (q == qq)

                    @pl.when(here)
                    def _():
                        pltpu.make_async_copy(
                            leaving.at[slab, :, pl.ds(qq * rows, rows)], out_ref.at[:, mine, 0], out_recv.at[mine]
                        ).start()

                    @pl.when(jnp.logical_not(here))
                    def _():
                        out_copy(slab, qq).start()

    for v, (dd, qq) in enumerate(places):
        target = (dd, pair * PAIR + qq)

        @pl.when(jnp.logical_not((d == dd) & (q == qq)))
        def _():
            for i in range(per_slab):
                for c in range(2):
                    if i == 0:

                        @pl.when(d > 0)
                        def _():
                            piece_copy(i, c, v, target).wait_send()
                    else:
                        piece_copy(i, c, v, target).wait_send()

    for v in range(views):
        ref = out_ref.at[:, v, 0]
        pltpu.make_async_copy(ref, ref, out_recv.at[v]).wait()

    @pl.when(works)
    def _():
        @pl.loop(0, slices)
        def _(s):
            for h in range(PARTS):

                @pl.when(has_up)
                def _():
                    rim_copy(s, 0, h).wait_send()

                @pl.when(has_down)
                def _():
                    rim_copy(s, 1, h).wait_send()

        @pl.loop(0, depths)
        def _(slab):
            for qq in range(PAIR):

                @pl.when(jnp.logical_not((d == slab) & (q == qq)))
                def _():
                    out_copy(slab, qq).wait_send()


def in_order(views, order_ref, value_ref, out_ref, sems):
    copies = [
        pltpu.make_async_copy(value_ref.at[:, order_ref[k]], out_ref.at[:, k], sems.at[k]) for k in range(views)
    ]
    for copy in copies:
        copy.start()
    for copy in copies:
        copy.wait()


def per_device(depths, tiles, incident, delta, beta, view_order):
    half = HALF
    _, views, rows, cols = incident.shape
    per_slab = delta.shape[1]
    slices = per_slab * depths
    span = PAIR * rows
    edge = LANES // 2
    rmat = jnp.asarray(np.concatenate(in_two(row_matrix(span, half)), axis=0))
    cmat = jnp.asarray(np.stack(in_two(column_matrix(LANES, edge, half))))
    anywhere = pl.BlockSpec(memory_space=pl.ANY)
    hbm = pl.BlockSpec(memory_space=pltpu.HBM)
    shape = jax.ShapeDtypeStruct((2, views, 1, rows, cols), jnp.float32)
    f32 = jnp.float32
    dma = pltpu.SemaphoreType.DMA
    by_view = pl.pallas_call(
        functools.partial(body, depths, tiles, views, rows, cols, per_slab),
        out_shape=shape,
        in_specs=[hbm] * 5,
        out_specs=anywhere,
        scratch_shapes=[
            pltpu.VMEM((4, views, rows, cols), f32),
            pltpu.VMEM((views, 2, rows, cols), f32),
            pltpu.VMEM((slices, 2, PAIR, rows, cols), f32),
            pltpu.VMEM((slices, 2, span + 2 * half, cols), f32),
            pltpu.VMEM((2, span, cols), f32),
            pltpu.VMEM((depths, 2, span, cols), f32),
            pltpu.VMEM(rmat.shape, rmat.dtype),
            pltpu.VMEM(cmat.shape, cmat.dtype),
            dma((6,)),
            dma((views,)),
            dma((PAIR,)),
            dma((per_slab, 2, views)),
            dma((slices, 2, PAIR)),
            dma((slices, 2, PARTS)),
            dma((slices, 2, PARTS)),
            dma((depths, PAIR)),
            dma((views,)),
            pltpu.SemaphoreType.REGULAR((views,)),
        ],
        compiler_params=pltpu.CompilerParams(
            collective_id=0, has_side_effects=True, vmem_limit_bytes=63 * 1024 * 1024
        ),
        name="views_by_worker",
    )(incident, delta, beta, rmat, cmat)
    return pl.pallas_call(
        functools.partial(in_order, views),
        out_shape=shape,
        in_specs=[pl.BlockSpec(memory_space=pltpu.SMEM), anywhere],
        out_specs=hbm,
        scratch_shapes=[dma((views,))],
        name="stored_order",
    )(view_order, by_view)


def solution(mesh):
    return jax.shard_map(
        functools.partial(per_device, mesh.shape["depth"], mesh.shape["tile"]),
        mesh=mesh,
        in_specs=(
            P(None, None, "tile", None),
            P(None, "depth", "tile", None),
            P(None, "depth", "tile", None),
            P(),
        ),
        out_specs=P(None, None, "depth", "tile", None),
        check_vma=False,
    )
```

```python
import functools

import jax
import jax.numpy as jnp
import ml_dtypes
import numpy as np
from jax import lax
from jax.experimental import pallas as pl
from jax.experimental.pallas import tpu as pltpu
from jax.sharding import PartitionSpec as P

HALF = 32
LANES = 128
PAIR = 2
GROUP = 2
MESH = pl.DeviceIdType.MESH

SIN_TERMS = (
    3.1415926535897931,
    -5.1677127800499694,
    2.5501640398773450,
    -0.59926452932079199,
    0.082145886611128236,
    -0.0073704309457143504,
    0.00046630280576761250,
)
COS_TERMS = (
    1.0,
    -4.9348022005446790,
    4.0587121264167676,
    -1.3352627688545893,
    0.23533063035889312,
    -0.025806891390014061,
    0.0019295743094039231,
    -0.00010463810492484570,
)


def series(square, terms):
    total = jnp.full_like(square, terms[-1])
    for term in terms[-2::-1]:
        total = total * square + term
    return total


def taps(offset, half):
    grid = np.arange(-half, half + 1, dtype=np.float64)
    norm = np.abs(
        np.sum((0.75 + 0.25 * np.cos(np.pi * grid / (half + 1))) * np.exp(1j * np.pi * grid**2 / (6.25 * half)))
    )
    place = offset.astype(np.float64)
    value = (0.75 + 0.25 * np.cos(np.pi * place / (half + 1))) * np.exp(1j * np.pi * place**2 / (6.25 * half))
    value = np.where(np.abs(offset) <= half, value / norm, 0.0)
    return value.real, value.imag


def in_two(matrix):
    matrix = matrix.astype(np.float32)
    high = matrix.astype(ml_dtypes.bfloat16)
    low = (matrix - high.astype(np.float32)).astype(ml_dtypes.bfloat16)
    return high, low


def row_matrix(rows, half):
    target, source = np.mgrid[0:rows, 0 : rows + 2 * half]
    real_part, imag_part = taps(source - half - target, half)
    return np.block([[real_part, -imag_part], [imag_part, real_part]])


def column_matrix(block, edge, half):
    source, target = np.mgrid[0 : block + 2 * edge, 0:block]
    real_part, imag_part = taps(source - edge - target, half)
    return np.block([[real_part, imag_part], [-imag_part, real_part]])


def split(value):
    high = value.astype(jnp.bfloat16)
    low = (value - high.astype(jnp.float32)).astype(jnp.bfloat16)
    return high, low


def dot(a, b):
    return jnp.dot(a, b, preferred_element_type=jnp.float32)


def transmitted(delta, beta):
    u = delta - 0.5
    amp = jnp.exp(-beta)
    square = u * u
    return -amp * (u * series(square, SIN_TERMS)), -amp * series(square, COS_TERMS)


def body(
    depths, tiles, views, rows, cols, per_slab,
    incident_ref, delta_ref, beta_ref, rmat_ref, cmat_ref, out_ref,
    loads, first, volume, wave, trans, leaving, rmat_buf, cmat_buf,
    load_sem, first_send, first_recv, vol_send, vol_recv, rim_send, rim_recv, out_send, out_recv, go,
):
    half = HALF
    span = PAIR * rows
    slices = depths * per_slab
    blocks = cols // LANES
    edge = LANES // 2
    d = lax.axis_index("depth")
    t = lax.axis_index("tile")
    pair = t // PAIR
    q = t % PAIR
    pairs = tiles // PAIR
    mine = (d // 2) * PAIR + q
    works = (d % 2 == 0) & (mine < views)
    places = [((v // PAIR) * 2, v % PAIR) for v in range(views)]

    taps_in = [
        pltpu.make_async_copy(rmat_ref, rmat_buf, load_sem.at[0]),
        pltpu.make_async_copy(cmat_ref, cmat_buf, load_sem.at[1]),
    ]
    first_in = [
        pltpu.make_async_copy(incident_ref.at[0], loads.at[0], load_sem.at[2]),
        pltpu.make_async_copy(incident_ref.at[1], loads.at[1], load_sem.at[3]),
        pltpu.make_async_copy(delta_ref.at[:, 0], loads.at[2], load_sem.at[4]),
        pltpu.make_async_copy(beta_ref.at[:, 0], loads.at[3], load_sem.at[5]),
    ]

    @pl.when(d == 0)
    def _():
        for copy in first_in:
            copy.start()

    @pl.when(works)
    def _():
        for copy in taps_in:
            copy.start()

    barrier = pltpu.get_barrier_semaphore()
    for dd in range(depths):
        for qq in range(PAIR):
            here = (d == dd) & (q == qq)
            peer = (dd, pair * PAIR + qq)
            if (dd, qq) in places:

                @pl.when(jnp.logical_not(here))
                def _():
                    pl.semaphore_signal(barrier, inc=1, device_id=peer, device_id_type=MESH)
            else:

                @pl.when(works)
                def _():
                    pl.semaphore_signal(barrier, inc=1, device_id=peer, device_id_type=MESH)

    has_up = works & (pair > 0)
    has_down = works & (pair < pairs - 1)
    up = (d, jnp.maximum(t - PAIR, 0))
    down = (d, jnp.minimum(t + PAIR, tiles - 1))

    @pl.when(has_up)
    def _():
        pl.semaphore_signal(barrier, inc=1, device_id=up, device_id_type=MESH)

    @pl.when(has_down)
    def _():
        pl.semaphore_signal(barrier, inc=1, device_id=down, device_id_type=MESH)

    @pl.when(d == 0)
    def _():
        for copy in first_in:
            copy.wait()
        for v in range(views):
            real_part, imag_part = transmitted(loads[2, v], loads[3, v])
            first[v, 0] = loads[0, v] * real_part - loads[1, v] * imag_part
            first[v, 1] = loads[0, v] * imag_part + loads[1, v] * real_part

    peers = jnp.where(works, depths * PAIR - 1, views)
    pl.semaphore_wait(barrier, peers + has_up.astype(jnp.int32) + has_down.astype(jnp.int32))

    def piece_copy(i, c, v, target):
        return pltpu.make_async_remote_copy(
            src_ref=(delta_ref, beta_ref)[c].at[v, i],
            dst_ref=volume.at[d * per_slab + i, c, q],
            send_sem=vol_send.at[i, c, v],
            recv_sem=vol_recv.at[d * per_slab + i, c, q],
            device_id=target,
            device_id_type=MESH,
        )

    def send_pieces(i, v):
        dd, qq = places[v]
        here = (d == dd) & (q == qq)
        for c, ref in enumerate((delta_ref, beta_ref)):

            @pl.when(here)
            def _():
                pltpu.make_async_copy(
                    ref.at[v, i], volume.at[d * per_slab + i, c, q], vol_recv.at[d * per_slab + i, c, q]
                ).start()

            @pl.when(jnp.logical_not(here))
            def _():
                piece_copy(i, c, v, (dd, pair * PAIR + qq)).start()

    def first_copy(v):
        dd, qq = places[v]
        return pltpu.make_async_remote_copy(
            src_ref=first.at[v],
            dst_ref=wave.at[0, :, pl.ds(half + q * rows, rows)],
            send_sem=first_send.at[v],
            recv_sem=first_recv.at[q],
            device_id=(dd, pair * PAIR + qq),
            device_id_type=MESH,
        )

    @pl.when(d == 0)
    def _():
        for v, (dd, qq) in enumerate(places):
            here = (d == dd) & (q == qq)

            @pl.when(here)
            def _():
                pltpu.make_async_copy(
                    first.at[v], wave.at[0, :, pl.ds(half + q * rows, rows)], first_recv.at[q]
                ).start()

            @pl.when(jnp.logical_not(here))
            def _():
                first_copy(v).start()

        for v, (dd, qq) in enumerate(places):

            @pl.when(jnp.logical_not((d == dd) & (q == qq)))
            def _():
                first_copy(v).wait_send()

        for i in range(1, per_slab):
            for v in range(views):
                send_pieces(i, v)

    @pl.when((d > 0) & jnp.logical_not(works))
    def _():
        for v in range(views):
            pl.semaphore_wait(go.at[v], 1)
            for i in range(per_slab):
                send_pieces(i, v)

    def out_copy(slab, qq):
        return pltpu.make_async_remote_copy(
            src_ref=leaving.at[slab, :, pl.ds(qq * rows, rows)],
            dst_ref=out_ref.at[:, mine, 0],
            send_sem=out_send.at[slab, qq],
            recv_sem=out_recv.at[mine],
            device_id=(slab, pair * PAIR + qq),
            device_id_type=MESH,
        )


    def rim_copy(s, side, h):
        first_row = half if side == 0 else span
        land = span + half if side == 0 else 0
        columns = pl.ds(h * LANES, LANES)
        return pltpu.make_async_remote_copy(
            src_ref=wave.at[s, :, pl.ds(first_row, half), columns],
            dst_ref=wave.at[s, :, pl.ds(land, half), columns],
            send_sem=rim_send.at[s, side, h],
            recv_sem=rim_recv.at[s, 1 - side, h],
            device_id=up if side == 0 else down,
            device_id_type=MESH,
        )

    def send_rims(s, h):
        @pl.when(has_up)
        def _():
            rim_copy(s, 0, h).start()

        @pl.when(has_down)
        def _():
            rim_copy(s, 1, h).start()

    def rim_arrival(s, side, h):
        land = 0 if side == 0 else span + half
        ref = wave.at[s, :, pl.ds(land, half), pl.ds(h * LANES, LANES)]
        return pltpu.make_async_copy(ref, ref, rim_recv.at[s, side, h])

    def transmission(s):
        for c in range(2):
            for qq in range(PAIR):
                ref = volume.at[s, c, qq]
                pltpu.make_async_copy(ref, ref, vol_recv.at[s, c, qq]).wait()
        trans[0], trans[1] = transmitted(volume[s, 0].reshape(span, cols), volume[s, 1].reshape(span, cols))

    @pl.when(works)
    def _():
        @pl.when(pair == 0)
        def _():
            wave[:, :, 0:half] = jnp.zeros((slices, 2, half, cols), jnp.float32)

        @pl.when(pair == pairs - 1)
        def _():
            wave[:, :, span + half :] = jnp.zeros((slices, 2, half, cols), jnp.float32)

        for copy in taps_in:
            copy.wait()
        for qq in range(PAIR):
            ref = wave.at[0, :, pl.ds(half + qq * rows, rows)]
            pltpu.make_async_copy(ref, ref, first_recv.at[qq]).wait()
        for h in range(blocks):
            send_rims(0, h)

        @pl.loop(0, slices)
        def _(s):
            for dd in range(1, depths):

                @pl.when(s == max(0, (dd - 1) * per_slab - 1))
                def _():
                    for qq in range(PAIR):
                        if (dd, qq) in places:

                            @pl.when((d == dd) & (q == qq))
                            def _():
                                for i in range(per_slab):
                                    for v in range(views):
                                        send_pieces(i, v)
                        else:
                            pl.semaphore_signal(
                                go.at[mine], inc=1, device_id=(dd, pair * PAIR + qq), device_id_type=MESH
                            )

            @pl.when(s < slices - 1)
            def _():
                transmission(s + 1)

            count = 2 * span

            def rows_done(first_block, last_block):
                for h in range(first_block, last_block):

                    @pl.when(has_up)
                    def _():
                        rim_arrival(s, 0, h).wait()

                    @pl.when(has_down)
                    def _():
                        rim_arrival(s, 1, h).wait()

                width = (last_block - first_block) * LANES
                columns = slice(first_block * LANES, last_block * LANES)
                high, low = split(wave[s, :, :, columns].reshape(2 * (span + 2 * half), width))
                both = dot(rmat_buf[...], high)
                return both[:count] + both[count:] + dot(rmat_buf[:count], low)

            def columns_done(first_block, last_block, pieces):
                high, low = split(pltpu.roll(pieces, pieces.shape[1] - edge, 1))

                def windows(value):
                    return [
                        jnp.concatenate(
                            [
                                value[:span, k * LANES : (k + 2) * LANES],
                                value[span:, k * LANES : (k + 2) * LANES],
                            ],
                            axis=1,
                        )
                        for k in range(last_block - first_block)
                    ]

                high, low = windows(high), windows(low)
                height = span * len(high)
                both = dot(jnp.concatenate(high + low, axis=0), cmat_buf[0])
                result = both[:height] + both[height:] + dot(jnp.concatenate(high, axis=0), cmat_buf[1])
                for k, block in enumerate(range(first_block, last_block)):
                    real_part, imag_part = [
                        result[k * span : (k + 1) * span, part * LANES : (part + 1) * LANES] for part in range(2)
                    ]
                    columns = slice(block * LANES, (block + 1) * LANES)

                    @pl.when(s < slices - 1)
                    def _():
                        trans_re, trans_im = trans[0, :, columns], trans[1, :, columns]
                        wave[s + 1, 0, half : half + span, columns] = real_part * trans_re - imag_part * trans_im
                        wave[s + 1, 1, half : half + span, columns] = real_part * trans_im + imag_part * trans_re
                        send_rims(s + 1, block)

                    @pl.when(s % per_slab == per_slab - 1)
                    def _():
                        leaving[s // per_slab, 0, :, columns] = real_part
                        leaving[s // per_slab, 1, :, columns] = imag_part

            outside = jnp.zeros((count, LANES), jnp.float32)
            made = []
            for first_block in range(0, blocks, GROUP):
                last_block = min(first_block + GROUP, blocks)
                if len(made) < last_block:
                    width = last_block - len(made)
                    joined = rows_done(len(made), last_block)
                    made += [joined[:, k * LANES : (k + 1) * LANES] for k in range(width)]
                if len(made) < min(last_block + 1, blocks):
                    made.append(rows_done(last_block, last_block + 1))
                pieces = [
                    made[k] if 0 <= k < blocks else outside for k in range(first_block - 1, last_block + 1)
                ]
                columns_done(first_block, last_block, jnp.concatenate(pieces, axis=1))

            @pl.when(s % per_slab == per_slab - 1)
            def _():
                slab = s // per_slab
                for qq in range(PAIR):
                    here = (d == slab) & (q == qq)

                    @pl.when(here)
                    def _():
                        pltpu.make_async_copy(
                            leaving.at[slab, :, pl.ds(qq * rows, rows)], out_ref.at[:, mine, 0], out_recv.at[mine]
                        ).start()

                    @pl.when(jnp.logical_not(here))
                    def _():
                        out_copy(slab, qq).start()

    for v, (dd, qq) in enumerate(places):
        target = (dd, pair * PAIR + qq)

        @pl.when(jnp.logical_not((d == dd) & (q == qq)))
        def _():
            for i in range(per_slab):
                for c in range(2):
                    if i == 0:

                        @pl.when(d > 0)
                        def _():
                            piece_copy(i, c, v, target).wait_send()
                    else:
                        piece_copy(i, c, v, target).wait_send()

    for v in range(views):
        ref = out_ref.at[:, v, 0]
        pltpu.make_async_copy(ref, ref, out_recv.at[v]).wait()

    @pl.when(works)
    def _():
        @pl.loop(0, slices)
        def _(s):
            for h in range(blocks):

                @pl.when(has_up)
                def _():
                    rim_copy(s, 0, h).wait_send()

                @pl.when(has_down)
                def _():
                    rim_copy(s, 1, h).wait_send()

        @pl.loop(0, depths)
        def _(slab):
            for qq in range(PAIR):

                @pl.when(jnp.logical_not((d == slab) & (q == qq)))
                def _():
                    out_copy(slab, qq).wait_send()


def in_order(views, order_ref, value_ref, out_ref):
    for k in range(views):
        out_ref[:, k] = value_ref[:, order_ref[k]]


def per_device(depths, tiles, incident, delta, beta, view_order):
    half = HALF
    _, views, rows, cols = incident.shape
    per_slab = delta.shape[1]
    slices = per_slab * depths
    span = PAIR * rows
    edge = LANES // 2
    rmat = jnp.asarray(np.concatenate(in_two(row_matrix(span, half)), axis=0))
    cmat = jnp.asarray(np.stack(in_two(column_matrix(LANES, edge, half))))
    anywhere = pl.BlockSpec(memory_space=pl.ANY)
    hbm = pl.BlockSpec(memory_space=pltpu.HBM)
    vmem = pl.BlockSpec(memory_space=pltpu.VMEM)
    shape = jax.ShapeDtypeStruct((2, views, 1, rows, cols), jnp.float32)
    f32 = jnp.float32
    dma = pltpu.SemaphoreType.DMA
    by_view = pl.pallas_call(
        functools.partial(body, depths, tiles, views, rows, cols, per_slab),
        out_shape=shape,
        in_specs=[hbm] * 5,
        out_specs=anywhere,
        scratch_shapes=[
            pltpu.VMEM((4, views, rows, cols), f32),
            pltpu.VMEM((views, 2, rows, cols), f32),
            pltpu.VMEM((slices, 2, PAIR, rows, cols), f32),
            pltpu.VMEM((slices, 2, span + 2 * half, cols), f32),
            pltpu.VMEM((2, span, cols), f32),
            pltpu.VMEM((depths, 2, span, cols), f32),
            pltpu.VMEM(rmat.shape, rmat.dtype),
            pltpu.VMEM(cmat.shape, cmat.dtype),
            dma((6,)),
            dma((views,)),
            dma((PAIR,)),
            dma((per_slab, 2, views)),
            dma((slices, 2, PAIR)),
            dma((slices, 2, cols // LANES)),
            dma((slices, 2, cols // LANES)),
            dma((depths, PAIR)),
            dma((views,)),
            pltpu.SemaphoreType.REGULAR((views,)),
        ],
        compiler_params=pltpu.CompilerParams(
            collective_id=0, has_side_effects=True, vmem_limit_bytes=63 * 1024 * 1024
        ),
        name="views_by_worker",
    )(incident, delta, beta, rmat, cmat)
    return pl.pallas_call(
        functools.partial(in_order, views),
        out_shape=shape,
        in_specs=[pl.BlockSpec(memory_space=pltpu.SMEM), vmem],
        out_specs=vmem,
        name="stored_order",
    )(view_order, by_view)


def solution(mesh):
    return jax.shard_map(
        functools.partial(per_device, mesh.shape["depth"], mesh.shape["tile"]),
        mesh=mesh,
        in_specs=(
            P(None, None, "tile", None),
            P(None, "depth", "tile", None),
            P(None, "depth", "tile", None),
            P(),
        ),
        out_specs=P(None, None, "depth", "tile", None),
        check_vma=False,
    )
```

```python
import functools

import jax
import jax.numpy as jnp
import ml_dtypes
import numpy as np
from jax import lax
from jax.experimental import pallas as pl
from jax.experimental.pallas import tpu as pltpu
from jax.sharding import PartitionSpec as P

HALF = 32
LANES = 128
PAIR = 2
GROUP = 2
STRIP = 8
MESH = pl.DeviceIdType.MESH

SIN_TERMS = (
    3.1415926535897931,
    -5.1677127800499694,
    2.5501640398773450,
    -0.59926452932079199,
    0.082145886611128236,
    -0.0073704309457143504,
    0.00046630280576761250,
)
COS_TERMS = (
    1.0,
    -4.9348022005446790,
    4.0587121264167676,
    -1.3352627688545893,
    0.23533063035889312,
    -0.025806891390014061,
    0.0019295743094039231,
    -0.00010463810492484570,
)


def series(square, terms):
    total = jnp.full_like(square, terms[-1])
    for term in terms[-2::-1]:
        total = total * square + term
    return total


def taps(offset, half):
    grid = np.arange(-half, half + 1, dtype=np.float64)
    norm = np.abs(
        np.sum((0.75 + 0.25 * np.cos(np.pi * grid / (half + 1))) * np.exp(1j * np.pi * grid**2 / (6.25 * half)))
    )
    place = offset.astype(np.float64)
    value = (0.75 + 0.25 * np.cos(np.pi * place / (half + 1))) * np.exp(1j * np.pi * place**2 / (6.25 * half))
    value = np.where(np.abs(offset) <= half, value / norm, 0.0)
    return value.real, value.imag


def in_two(matrix):
    matrix = matrix.astype(np.float32)
    high = matrix.astype(ml_dtypes.bfloat16)
    low = (matrix - high.astype(np.float32)).astype(ml_dtypes.bfloat16)
    return high, low


def row_matrix(rows, half):
    target, source = np.mgrid[0:rows, 0 : rows + 2 * half]
    real_part, imag_part = taps(source - half - target, half)
    return np.block([[real_part, -imag_part], [imag_part, real_part]])


def column_matrix(block, edge, half):
    source, target = np.mgrid[0 : block + 2 * edge, 0:block]
    real_part, imag_part = taps(source - edge - target, half)
    return np.block([[real_part, imag_part], [-imag_part, real_part]])


def split(value):
    high = value.astype(jnp.bfloat16)
    low = (value - high.astype(jnp.float32)).astype(jnp.bfloat16)
    return high, low


def dot(a, b):
    return jnp.dot(a, b, preferred_element_type=jnp.float32)


def transmitted(delta, beta):
    u = delta - 0.5
    amp = jnp.exp(-beta)
    square = u * u
    return -amp * (u * series(square, SIN_TERMS)), -amp * series(square, COS_TERMS)


def body(
    depths, tiles, views, rows, cols, per_slab,
    incident_ref, delta_ref, beta_ref, rmat_ref, cmat_ref, out_ref,
    loads, first, volume, wave, trans, leaving, rmat_buf, cmat_buf,
    load_sem, first_send, first_recv, vol_send, vol_recv, rim_send, rim_recv, out_send, out_recv, go,
):
    half = HALF
    span = PAIR * rows
    slices = depths * per_slab
    blocks = cols // LANES
    edge = LANES // 2
    d = lax.axis_index("depth")
    t = lax.axis_index("tile")
    pair = t // PAIR
    q = t % PAIR
    pairs = tiles // PAIR
    mine = (d // 2) * PAIR + q
    works = (d % 2 == 0) & (mine < views)
    places = [((v // PAIR) * 2, v % PAIR) for v in range(views)]

    def at_worker(v):
        return (d == (v // PAIR) * 2) & (q == v % PAIR)

    def worker(v):
        return ((v // PAIR) * 2, pair * PAIR + v % PAIR)


    taps_in = [
        pltpu.make_async_copy(rmat_ref, rmat_buf, load_sem.at[0]),
        pltpu.make_async_copy(cmat_ref, cmat_buf, load_sem.at[1]),
    ]
    first_in = [
        pltpu.make_async_copy(incident_ref.at[0], loads.at[0], load_sem.at[2]),
        pltpu.make_async_copy(incident_ref.at[1], loads.at[1], load_sem.at[3]),
        pltpu.make_async_copy(delta_ref.at[:, 0], loads.at[2], load_sem.at[4]),
        pltpu.make_async_copy(beta_ref.at[:, 0], loads.at[3], load_sem.at[5]),
    ]

    @pl.when(d == 0)
    def _():
        for copy in first_in:
            copy.start()

    @pl.when(works)
    def _():
        for copy in taps_in:
            copy.start()

    barrier = pltpu.get_barrier_semaphore()
    for dd in range(depths):
        for qq in range(PAIR):
            here = (d == dd) & (q == qq)
            peer = (dd, pair * PAIR + qq)
            if (dd, qq) in places:

                @pl.when(jnp.logical_not(here))
                def _():
                    pl.semaphore_signal(barrier, inc=1, device_id=peer, device_id_type=MESH)
            else:

                @pl.when(works)
                def _():
                    pl.semaphore_signal(barrier, inc=1, device_id=peer, device_id_type=MESH)

    has_up = works & (pair > 0)
    has_down = works & (pair < pairs - 1)
    up = (d, jnp.maximum(t - PAIR, 0))
    down = (d, jnp.minimum(t + PAIR, tiles - 1))

    @pl.when(has_up)
    def _():
        pl.semaphore_signal(barrier, inc=1, device_id=up, device_id_type=MESH)

    @pl.when(has_down)
    def _():
        pl.semaphore_signal(barrier, inc=1, device_id=down, device_id_type=MESH)

    @pl.when(d == 0)
    def _():
        for copy in first_in:
            copy.wait()

        @pl.loop(0, views)
        def _(v):
            @pl.loop(0, rows // STRIP)
            def _(r):
                strip = pl.ds(pl.multiple_of(r * STRIP, STRIP), STRIP)
                real_part, imag_part = transmitted(loads[2, v, strip], loads[3, v, strip])
                wave_re, wave_im = loads[0, v, strip], loads[1, v, strip]
                first[v, 0, strip] = wave_re * real_part - wave_im * imag_part
                first[v, 1, strip] = wave_re * imag_part + wave_im * real_part

    peers = jnp.where(works, depths * PAIR - 1, views)
    pl.semaphore_wait(barrier, peers + has_up.astype(jnp.int32) + has_down.astype(jnp.int32))

    def piece_copy(i, c, v):
        return pltpu.make_async_remote_copy(
            src_ref=(delta_ref, beta_ref)[c].at[v, i],
            dst_ref=volume.at[d * per_slab + i, c, q],
            send_sem=vol_send.at[i, c, v],
            recv_sem=vol_recv.at[d * per_slab + i, c, q],
            device_id=worker(v),
            device_id_type=MESH,
        )

    def send_pieces(i, v):
        here = at_worker(v)

        @pl.when(here)
        def _():
            for c, ref in enumerate((delta_ref, beta_ref)):
                pltpu.make_async_copy(
                    ref.at[v, i], volume.at[d * per_slab + i, c, q], vol_recv.at[d * per_slab + i, c, q]
                ).start()

        @pl.when(jnp.logical_not(here))
        def _():
            for c in range(2):
                piece_copy(i, c, v).start()

    def first_copy(v):
        return pltpu.make_async_remote_copy(
            src_ref=first.at[v],
            dst_ref=wave.at[0, :, pl.ds(half + q * rows, rows)],
            send_sem=first_send.at[v],
            recv_sem=first_recv.at[q],
            device_id=worker(v),
            device_id_type=MESH,
        )

    @pl.when(d == 0)
    def _():
        @pl.loop(0, views)
        def _(v):
            here = at_worker(v)

            @pl.when(here)
            def _():
                pltpu.make_async_copy(
                    first.at[v], wave.at[0, :, pl.ds(half + q * rows, rows)], first_recv.at[q]
                ).start()

            @pl.when(jnp.logical_not(here))
            def _():
                first_copy(v).start()

        @pl.loop(0, views)
        def _(v):
            @pl.when(jnp.logical_not(at_worker(v)))
            def _():
                first_copy(v).wait_send()

        @pl.loop(0, (per_slab - 1) * views)
        def _(k):
            send_pieces(1 + k // views, k % views)

    @pl.when((d > 0) & jnp.logical_not(works))
    def _():
        @pl.loop(0, views)
        def _(v):
            pl.semaphore_wait(go.at[v], 1)

            @pl.loop(0, per_slab)
            def _(i):
                send_pieces(i, v)

    def out_copy(slab, qq):
        return pltpu.make_async_remote_copy(
            src_ref=leaving.at[slab, :, pl.ds(qq * rows, rows)],
            dst_ref=out_ref.at[:, mine, 0],
            send_sem=out_send.at[slab, qq],
            recv_sem=out_recv.at[mine],
            device_id=(slab, pair * PAIR + qq),
            device_id_type=MESH,
        )


    def rim_copy(s, side, h):
        first_row = half if side == 0 else span
        land = span + half if side == 0 else 0
        columns = pl.ds(h * LANES, LANES)
        return pltpu.make_async_remote_copy(
            src_ref=wave.at[s, :, pl.ds(first_row, half), columns],
            dst_ref=wave.at[s, :, pl.ds(land, half), columns],
            send_sem=rim_send.at[s, side, h],
            recv_sem=rim_recv.at[s, 1 - side, h],
            device_id=up if side == 0 else down,
            device_id_type=MESH,
        )

    def send_rims(s, h):
        @pl.when(has_up)
        def _():
            rim_copy(s, 0, h).start()

        @pl.when(has_down)
        def _():
            rim_copy(s, 1, h).start()

    def rim_arrival(s, side, h):
        land = 0 if side == 0 else span + half
        ref = wave.at[s, :, pl.ds(land, half), pl.ds(h * LANES, LANES)]
        return pltpu.make_async_copy(ref, ref, rim_recv.at[s, side, h])

    def transmission(s):
        for c in range(2):
            for qq in range(PAIR):
                ref = volume.at[s, c, qq]
                pltpu.make_async_copy(ref, ref, vol_recv.at[s, c, qq]).wait()
        for qq in range(PAIR):

            @pl.loop(0, rows // STRIP)
            def _(r):
                strip = pl.ds(pl.multiple_of(r * STRIP, STRIP), STRIP)
                land = pl.ds(pl.multiple_of(qq * rows + r * STRIP, STRIP), STRIP)
                real_part, imag_part = transmitted(volume[s, 0, qq, strip], volume[s, 1, qq, strip])
                trans[0, land] = real_part
                trans[1, land] = imag_part

    @pl.when(works)
    def _():
        def clear(first_row):
            @pl.loop(0, slices)
            def _(s):
                wave[s, :, first_row : first_row + half] = jnp.zeros((2, half, cols), jnp.float32)

        @pl.when(pair == 0)
        def _():
            clear(0)

        @pl.when(pair == pairs - 1)
        def _():
            clear(span + half)

        for copy in taps_in:
            copy.wait()
        for qq in range(PAIR):
            ref = wave.at[0, :, pl.ds(half + qq * rows, rows)]
            pltpu.make_async_copy(ref, ref, first_recv.at[qq]).wait()
        for h in range(blocks):
            send_rims(0, h)

        @pl.loop(0, slices)
        def _(s):
            for dd in range(1, depths):

                @pl.when(s == max(0, (dd - 1) * per_slab - 1))
                def _():
                    for qq in range(PAIR):
                        if (dd, qq) in places:

                            @pl.when((d == dd) & (q == qq))
                            def _():
                                @pl.loop(0, per_slab * views)
                                def _(k):
                                    send_pieces(k // views, k % views)
                        else:
                            pl.semaphore_signal(
                                go.at[mine], inc=1, device_id=(dd, pair * PAIR + qq), device_id_type=MESH
                            )

            @pl.when(s < slices - 1)
            def _():
                transmission(s + 1)

            count = 2 * span

            def rows_done(first_block, last_block):
                for h in range(first_block, last_block):

                    @pl.when(has_up)
                    def _():
                        rim_arrival(s, 0, h).wait()

                    @pl.when(has_down)
                    def _():
                        rim_arrival(s, 1, h).wait()

                width = (last_block - first_block) * LANES
                columns = slice(first_block * LANES, last_block * LANES)
                high, low = split(wave[s, :, :, columns].reshape(2 * (span + 2 * half), width))
                both = dot(rmat_buf[...], high)
                return both[:count] + both[count:] + dot(rmat_buf[:count], low)

            def columns_done(first_block, last_block, pieces):
                high, low = split(pltpu.roll(pieces, pieces.shape[1] - edge, 1))

                def windows(value):
                    return [
                        jnp.concatenate(
                            [
                                value[:span, k * LANES : (k + 2) * LANES],
                                value[span:, k * LANES : (k + 2) * LANES],
                            ],
                            axis=1,
                        )
                        for k in range(last_block - first_block)
                    ]

                high, low = windows(high), windows(low)
                height = span * len(high)
                both = dot(jnp.concatenate(high + low, axis=0), cmat_buf[0])
                result = both[:height] + both[height:] + dot(jnp.concatenate(high, axis=0), cmat_buf[1])
                for k, block in enumerate(range(first_block, last_block)):
                    real_part, imag_part = [
                        result[k * span : (k + 1) * span, part * LANES : (part + 1) * LANES] for part in range(2)
                    ]
                    columns = slice(block * LANES, (block + 1) * LANES)

                    @pl.when(s < slices - 1)
                    def _():
                        trans_re, trans_im = trans[0, :, columns], trans[1, :, columns]
                        wave[s + 1, 0, half : half + span, columns] = real_part * trans_re - imag_part * trans_im
                        wave[s + 1, 1, half : half + span, columns] = real_part * trans_im + imag_part * trans_re
                        send_rims(s + 1, block)

                    @pl.when(s % per_slab == per_slab - 1)
                    def _():
                        leaving[s // per_slab, 0, :, columns] = real_part
                        leaving[s // per_slab, 1, :, columns] = imag_part

            outside = jnp.zeros((count, LANES), jnp.float32)
            made = []
            for first_block in range(0, blocks, GROUP):
                last_block = min(first_block + GROUP, blocks)
                if len(made) < last_block:
                    width = last_block - len(made)
                    joined = rows_done(len(made), last_block)
                    made += [joined[:, k * LANES : (k + 1) * LANES] for k in range(width)]
                if len(made) < min(last_block + 1, blocks):
                    made.append(rows_done(last_block, last_block + 1))
                pieces = [
                    made[k] if 0 <= k < blocks else outside for k in range(first_block - 1, last_block + 1)
                ]
                columns_done(first_block, last_block, jnp.concatenate(pieces, axis=1))

            @pl.when(s % per_slab == per_slab - 1)
            def _():
                slab = s // per_slab
                for qq in range(PAIR):
                    here = (d == slab) & (q == qq)

                    @pl.when(here)
                    def _():
                        pltpu.make_async_copy(
                            leaving.at[slab, :, pl.ds(qq * rows, rows)], out_ref.at[:, mine, 0], out_recv.at[mine]
                        ).start()

                    @pl.when(jnp.logical_not(here))
                    def _():
                        out_copy(slab, qq).start()

    @pl.loop(0, per_slab * views)
    def _(k):
        i, v = k // views, k % views

        @pl.when(jnp.logical_not(at_worker(v)) & ((d > 0) | (i > 0)))
        def _():
            for c in range(2):
                piece_copy(i, c, v).wait_send()

    for v in range(views):
        ref = out_ref.at[:, v, 0]
        pltpu.make_async_copy(ref, ref, out_recv.at[v]).wait()

    @pl.when(works)
    def _():
        @pl.loop(0, slices)
        def _(s):
            @pl.loop(0, blocks)
            def _(h):
                @pl.when(has_up)
                def _():
                    rim_copy(s, 0, h).wait_send()

                @pl.when(has_down)
                def _():
                    rim_copy(s, 1, h).wait_send()

        @pl.loop(0, depths)
        def _(slab):
            for qq in range(PAIR):

                @pl.when(jnp.logical_not((d == slab) & (q == qq)))
                def _():
                    out_copy(slab, qq).wait_send()


def in_order(views, order_ref, value_ref, out_ref):
    for k in range(views):
        out_ref[:, k] = value_ref[:, order_ref[k]]


def per_device(depths, tiles, incident, delta, beta, view_order):
    half = HALF
    _, views, rows, cols = incident.shape
    per_slab = delta.shape[1]
    slices = per_slab * depths
    span = PAIR * rows
    edge = LANES // 2
    rmat = jnp.asarray(np.concatenate(in_two(row_matrix(span, half)), axis=0))
    cmat = jnp.asarray(np.stack(in_two(column_matrix(LANES, edge, half))))
    anywhere = pl.BlockSpec(memory_space=pl.ANY)
    hbm = pl.BlockSpec(memory_space=pltpu.HBM)
    vmem = pl.BlockSpec(memory_space=pltpu.VMEM)
    shape = jax.ShapeDtypeStruct((2, views, 1, rows, cols), jnp.float32)
    f32 = jnp.float32
    dma = pltpu.SemaphoreType.DMA
    by_view = pl.pallas_call(
        functools.partial(body, depths, tiles, views, rows, cols, per_slab),
        out_shape=shape,
        in_specs=[hbm] * 5,
        out_specs=anywhere,
        scratch_shapes=[
            pltpu.VMEM((4, views, rows, cols), f32),
            pltpu.VMEM((views, 2, rows, cols), f32),
            pltpu.VMEM((slices, 2, PAIR, rows, cols), f32),
            pltpu.VMEM((slices, 2, span + 2 * half, cols), f32),
            pltpu.VMEM((2, span, cols), f32),
            pltpu.VMEM((depths, 2, span, cols), f32),
            pltpu.VMEM(rmat.shape, rmat.dtype),
            pltpu.VMEM(cmat.shape, cmat.dtype),
            dma((6,)),
            dma((views,)),
            dma((PAIR,)),
            dma((per_slab, 2, views)),
            dma((slices, 2, PAIR)),
            dma((slices, 2, cols // LANES)),
            dma((slices, 2, cols // LANES)),
            dma((depths, PAIR)),
            dma((views,)),
            pltpu.SemaphoreType.REGULAR((views,)),
        ],
        compiler_params=pltpu.CompilerParams(
            collective_id=0, has_side_effects=True, vmem_limit_bytes=63 * 1024 * 1024
        ),
        name="views_by_worker",
    )(incident, delta, beta, rmat, cmat)
    return pl.pallas_call(
        functools.partial(in_order, views),
        out_shape=shape,
        in_specs=[pl.BlockSpec(memory_space=pltpu.SMEM), vmem],
        out_specs=vmem,
        name="stored_order",
    )(view_order, by_view)


def solution(mesh):
    return jax.shard_map(
        functools.partial(per_device, mesh.shape["depth"], mesh.shape["tile"]),
        mesh=mesh,
        in_specs=(
            P(None, None, "tile", None),
            P(None, "depth", "tile", None),
            P(None, "depth", "tile", None),
            P(),
        ),
        out_specs=P(None, None, "depth", "tile", None),
        check_vma=False,
    )
```

```python
import functools

import jax
import jax.numpy as jnp
import ml_dtypes
import numpy as np
from jax import lax
from jax.experimental import pallas as pl
from jax.experimental.pallas import tpu as pltpu
from jax.sharding import PartitionSpec as P

HALF = 32
LANES = 128
PAIR = 2
GROUP = 2
STRIP = 8
MESH = pl.DeviceIdType.MESH

SIN_TERMS = (
    3.1415926535897931,
    -5.1677127800499694,
    2.5501640398773450,
    -0.59926452932079199,
    0.082145886611128236,
    -0.0073704309457143504,
    0.00046630280576761250,
)
COS_TERMS = (
    1.0,
    -4.9348022005446790,
    4.0587121264167676,
    -1.3352627688545893,
    0.23533063035889312,
    -0.025806891390014061,
    0.0019295743094039231,
    -0.00010463810492484570,
)


def series(square, terms):
    total = jnp.full_like(square, terms[-1])
    for term in terms[-2::-1]:
        total = total * square + term
    return total


def taps(offset, half):
    grid = np.arange(-half, half + 1, dtype=np.float64)
    norm = np.abs(
        np.sum((0.75 + 0.25 * np.cos(np.pi * grid / (half + 1))) * np.exp(1j * np.pi * grid**2 / (6.25 * half)))
    )
    place = offset.astype(np.float64)
    value = (0.75 + 0.25 * np.cos(np.pi * place / (half + 1))) * np.exp(1j * np.pi * place**2 / (6.25 * half))
    value = np.where(np.abs(offset) <= half, value / norm, 0.0)
    return value.real, value.imag


def in_two(matrix):
    matrix = matrix.astype(np.float32)
    high = matrix.astype(ml_dtypes.bfloat16)
    low = (matrix - high.astype(np.float32)).astype(ml_dtypes.bfloat16)
    return high, low


def row_matrix(rows, half):
    target, source = np.mgrid[0:rows, 0 : rows + 2 * half]
    real_part, imag_part = taps(source - half - target, half)
    return np.block([[real_part, -imag_part], [imag_part, real_part]])


def column_matrix(block, edge, half):
    source, target = np.mgrid[0 : block + 2 * edge, 0:block]
    real_part, imag_part = taps(source - edge - target, half)
    return np.block([[real_part, imag_part], [-imag_part, real_part]])


def split(value):
    high = value.astype(jnp.bfloat16)
    low = (value - high.astype(jnp.float32)).astype(jnp.bfloat16)
    return high, low


def dot(a, b):
    return jnp.dot(a, b, preferred_element_type=jnp.float32)


def transmitted(delta, beta):
    u = delta - 0.5
    amp = jnp.exp(-beta)
    square = u * u
    return -amp * (u * series(square, SIN_TERMS)), -amp * series(square, COS_TERMS)


def body(
    depths, tiles, views, rows, cols, per_slab,
    incident_ref, delta_ref, beta_ref, rmat_ref, cmat_ref, out_ref,
    loads, first, volume, wave, trans, leaving, rmat_buf, cmat_buf,
    load_sem, first_send, first_recv, vol_send, vol_recv, rim_send, rim_recv, out_send, out_recv, go,
):
    half = HALF
    span = PAIR * rows
    slices = depths * per_slab
    blocks = cols // LANES
    edge = LANES // 2
    d = lax.axis_index("depth")
    t = lax.axis_index("tile")
    pair = t // PAIR
    q = t % PAIR
    pairs = tiles // PAIR
    mine = (d // 2) * PAIR + q
    works = (d % 2 == 0) & (mine < views)
    places = [((v // PAIR) * 2, v % PAIR) for v in range(views)]

    def at_worker(v):
        return (d == (v // PAIR) * 2) & (q == v % PAIR)

    def worker(v):
        return ((v // PAIR) * 2, pair * PAIR + v % PAIR)


    taps_in = [
        pltpu.make_async_copy(rmat_ref, rmat_buf, load_sem.at[0]),
        pltpu.make_async_copy(cmat_ref, cmat_buf, load_sem.at[1]),
    ]
    first_in = [
        pltpu.make_async_copy(incident_ref.at[0], loads.at[0], load_sem.at[2]),
        pltpu.make_async_copy(incident_ref.at[1], loads.at[1], load_sem.at[3]),
        pltpu.make_async_copy(delta_ref.at[:, 0], loads.at[2], load_sem.at[4]),
        pltpu.make_async_copy(beta_ref.at[:, 0], loads.at[3], load_sem.at[5]),
    ]

    @pl.when(d == 0)
    def _():
        for copy in first_in:
            copy.start()

    @pl.when(works)
    def _():
        for copy in taps_in:
            copy.start()

    barrier = pltpu.get_barrier_semaphore()
    for dd in range(depths):
        for qq in range(PAIR):
            here = (d == dd) & (q == qq)
            peer = (dd, pair * PAIR + qq)
            if (dd, qq) in places:

                @pl.when(jnp.logical_not(here))
                def _():
                    pl.semaphore_signal(barrier, inc=1, device_id=peer, device_id_type=MESH)
            else:

                @pl.when(works)
                def _():
                    pl.semaphore_signal(barrier, inc=1, device_id=peer, device_id_type=MESH)

    has_up = works & (pair > 0)
    has_down = works & (pair < pairs - 1)
    up = (d, jnp.maximum(t - PAIR, 0))
    down = (d, jnp.minimum(t + PAIR, tiles - 1))

    @pl.when(has_up)
    def _():
        pl.semaphore_signal(barrier, inc=1, device_id=up, device_id_type=MESH)

    @pl.when(has_down)
    def _():
        pl.semaphore_signal(barrier, inc=1, device_id=down, device_id_type=MESH)

    @pl.when(d == 0)
    def _():
        for copy in first_in:
            copy.wait()

        @pl.loop(0, views)
        def _(v):
            @pl.loop(0, rows // STRIP)
            def _(r):
                strip = pl.ds(pl.multiple_of(r * STRIP, STRIP), STRIP)
                real_part, imag_part = transmitted(loads[2, v, strip], loads[3, v, strip])
                wave_re, wave_im = loads[0, v, strip], loads[1, v, strip]
                first[v, 0, strip] = wave_re * real_part - wave_im * imag_part
                first[v, 1, strip] = wave_re * imag_part + wave_im * real_part

    peers = jnp.where(works, depths * PAIR - 1, views)
    pl.semaphore_wait(barrier, peers + has_up.astype(jnp.int32) + has_down.astype(jnp.int32))

    def piece_copy(i, c, v):
        return pltpu.make_async_remote_copy(
            src_ref=(delta_ref, beta_ref)[c].at[v, i],
            dst_ref=volume.at[d * per_slab + i, c, q],
            send_sem=vol_send.at[i, c, v],
            recv_sem=vol_recv.at[d * per_slab + i, c, q],
            device_id=worker(v),
            device_id_type=MESH,
        )

    def send_pieces(i, v):
        here = at_worker(v)

        @pl.when(here)
        def _():
            for c, ref in enumerate((delta_ref, beta_ref)):
                pltpu.make_async_copy(
                    ref.at[v, i], volume.at[d * per_slab + i, c, q], vol_recv.at[d * per_slab + i, c, q]
                ).start()

        @pl.when(jnp.logical_not(here))
        def _():
            for c in range(2):
                piece_copy(i, c, v).start()

    def first_copy(v):
        return pltpu.make_async_remote_copy(
            src_ref=first.at[v],
            dst_ref=wave.at[0, :, pl.ds(half + q * rows, rows)],
            send_sem=first_send.at[v],
            recv_sem=first_recv.at[q],
            device_id=worker(v),
            device_id_type=MESH,
        )

    @pl.when(d == 0)
    def _():
        @pl.loop(0, views)
        def _(v):
            here = at_worker(v)

            @pl.when(here)
            def _():
                pltpu.make_async_copy(
                    first.at[v], wave.at[0, :, pl.ds(half + q * rows, rows)], first_recv.at[q]
                ).start()

            @pl.when(jnp.logical_not(here))
            def _():
                first_copy(v).start()

        @pl.loop(0, views)
        def _(v):
            @pl.when(jnp.logical_not(at_worker(v)))
            def _():
                first_copy(v).wait_send()

        pl.semaphore_signal(go.at[0], inc=1, device_id=(1, t), device_id_type=MESH)

        @pl.loop(0, (per_slab - 1) * views)
        def _(k):
            send_pieces(1 + k // views, k % views)

    @pl.when(d == 1)
    def _():
        pl.semaphore_wait(go.at[0], 1)

        @pl.loop(0, per_slab * views)
        def _(k):
            send_pieces(k // views, k % views)

    @pl.when((d > 1) & jnp.logical_not(works))
    def _():
        @pl.loop(0, views)
        def _(v):
            pl.semaphore_wait(go.at[v], 1)

            @pl.loop(0, per_slab)
            def _(i):
                send_pieces(i, v)

    def out_copy(slab, qq):
        return pltpu.make_async_remote_copy(
            src_ref=leaving.at[slab, :, pl.ds(qq * rows, rows)],
            dst_ref=out_ref.at[:, mine, 0],
            send_sem=out_send.at[slab, qq],
            recv_sem=out_recv.at[mine],
            device_id=(slab, pair * PAIR + qq),
            device_id_type=MESH,
        )


    def rim_copy(s, side, h):
        first_row = half if side == 0 else span
        land = span + half if side == 0 else 0
        columns = pl.ds(h * LANES, LANES)
        return pltpu.make_async_remote_copy(
            src_ref=wave.at[s, :, pl.ds(first_row, half), columns],
            dst_ref=wave.at[s, :, pl.ds(land, half), columns],
            send_sem=rim_send.at[s, side, h],
            recv_sem=rim_recv.at[s, 1 - side, h],
            device_id=up if side == 0 else down,
            device_id_type=MESH,
        )

    def send_rims(s, h):
        @pl.when(has_up)
        def _():
            rim_copy(s, 0, h).start()

        @pl.when(has_down)
        def _():
            rim_copy(s, 1, h).start()

    def rim_arrival(s, side, h):
        land = 0 if side == 0 else span + half
        ref = wave.at[s, :, pl.ds(land, half), pl.ds(h * LANES, LANES)]
        return pltpu.make_async_copy(ref, ref, rim_recv.at[s, side, h])

    def transmission(s):
        for c in range(2):
            for qq in range(PAIR):
                ref = volume.at[s, c, qq]
                pltpu.make_async_copy(ref, ref, vol_recv.at[s, c, qq]).wait()
        for qq in range(PAIR):

            @pl.loop(0, rows // STRIP)
            def _(r):
                strip = pl.ds(pl.multiple_of(r * STRIP, STRIP), STRIP)
                land = pl.ds(pl.multiple_of(qq * rows + r * STRIP, STRIP), STRIP)
                real_part, imag_part = transmitted(volume[s, 0, qq, strip], volume[s, 1, qq, strip])
                trans[0, land] = real_part
                trans[1, land] = imag_part

    @pl.when(works)
    def _():
        def clear(first_row):
            @pl.loop(0, slices)
            def _(s):
                wave[s, :, first_row : first_row + half] = jnp.zeros((2, half, cols), jnp.float32)

        @pl.when(pair == 0)
        def _():
            clear(0)

        @pl.when(pair == pairs - 1)
        def _():
            clear(span + half)

        for copy in taps_in:
            copy.wait()
        for qq in range(PAIR):
            ref = wave.at[0, :, pl.ds(half + qq * rows, rows)]
            pltpu.make_async_copy(ref, ref, first_recv.at[qq]).wait()
        for h in range(blocks):
            send_rims(0, h)

        @pl.loop(0, slices)
        def _(s):
            for dd in range(2, depths):

                @pl.when(s == (dd - 2) * per_slab)
                def _():
                    for qq in range(PAIR):
                        if (dd, qq) in places:

                            @pl.when((d == dd) & (q == qq))
                            def _():
                                @pl.loop(0, per_slab * views)
                                def _(k):
                                    send_pieces(k // views, k % views)
                        else:
                            pl.semaphore_signal(
                                go.at[mine], inc=1, device_id=(dd, pair * PAIR + qq), device_id_type=MESH
                            )

            @pl.when(s < slices - 1)
            def _():
                transmission(s + 1)

            count = 2 * span

            def rows_done(first_block, last_block):
                for h in range(first_block, last_block):

                    @pl.when(has_up)
                    def _():
                        rim_arrival(s, 0, h).wait()

                    @pl.when(has_down)
                    def _():
                        rim_arrival(s, 1, h).wait()

                width = (last_block - first_block) * LANES
                columns = slice(first_block * LANES, last_block * LANES)
                high, low = split(wave[s, :, :, columns].reshape(2 * (span + 2 * half), width))
                both = dot(rmat_buf[...], high)
                return both[:count] + both[count:] + dot(rmat_buf[:count], low)

            def columns_done(first_block, last_block, pieces):
                high, low = split(pltpu.roll(pieces, pieces.shape[1] - edge, 1))

                def windows(value):
                    return [
                        jnp.concatenate(
                            [
                                value[:span, k * LANES : (k + 2) * LANES],
                                value[span:, k * LANES : (k + 2) * LANES],
                            ],
                            axis=1,
                        )
                        for k in range(last_block - first_block)
                    ]

                high, low = windows(high), windows(low)
                height = span * len(high)
                both = dot(jnp.concatenate(high + low, axis=0), cmat_buf[0])
                result = both[:height] + both[height:] + dot(jnp.concatenate(high, axis=0), cmat_buf[1])
                for k, block in enumerate(range(first_block, last_block)):
                    real_part, imag_part = [
                        result[k * span : (k + 1) * span, part * LANES : (part + 1) * LANES] for part in range(2)
                    ]
                    columns = slice(block * LANES, (block + 1) * LANES)

                    @pl.when(s < slices - 1)
                    def _():
                        trans_re, trans_im = trans[0, :, columns], trans[1, :, columns]
                        wave[s + 1, 0, half : half + span, columns] = real_part * trans_re - imag_part * trans_im
                        wave[s + 1, 1, half : half + span, columns] = real_part * trans_im + imag_part * trans_re
                        send_rims(s + 1, block)

                    @pl.when(s % per_slab == per_slab - 1)
                    def _():
                        leaving[s // per_slab, 0, :, columns] = real_part
                        leaving[s // per_slab, 1, :, columns] = imag_part

            outside = jnp.zeros((count, LANES), jnp.float32)
            made = []
            for first_block in range(0, blocks, GROUP):
                last_block = min(first_block + GROUP, blocks)
                if len(made) < last_block:
                    width = last_block - len(made)
                    joined = rows_done(len(made), last_block)
                    made += [joined[:, k * LANES : (k + 1) * LANES] for k in range(width)]
                if len(made) < min(last_block + 1, blocks):
                    made.append(rows_done(last_block, last_block + 1))
                pieces = [
                    made[k] if 0 <= k < blocks else outside for k in range(first_block - 1, last_block + 1)
                ]
                columns_done(first_block, last_block, jnp.concatenate(pieces, axis=1))

            @pl.when(s % per_slab == per_slab - 1)
            def _():
                slab = s // per_slab
                for qq in range(PAIR):
                    here = (d == slab) & (q == qq)

                    @pl.when(here)
                    def _():
                        pltpu.make_async_copy(
                            leaving.at[slab, :, pl.ds(qq * rows, rows)], out_ref.at[:, mine, 0], out_recv.at[mine]
                        ).start()

                    @pl.when(jnp.logical_not(here))
                    def _():
                        out_copy(slab, qq).start()

    @pl.loop(0, per_slab * views)
    def _(k):
        i, v = k // views, k % views

        @pl.when(jnp.logical_not(at_worker(v)) & ((d > 0) | (i > 0)))
        def _():
            for c in range(2):
                piece_copy(i, c, v).wait_send()

    for v in range(views):
        ref = out_ref.at[:, v, 0]
        pltpu.make_async_copy(ref, ref, out_recv.at[v]).wait()

    @pl.when(works)
    def _():
        @pl.loop(0, slices)
        def _(s):
            @pl.loop(0, blocks)
            def _(h):
                @pl.when(has_up)
                def _():
                    rim_copy(s, 0, h).wait_send()

                @pl.when(has_down)
                def _():
                    rim_copy(s, 1, h).wait_send()

        @pl.loop(0, depths)
        def _(slab):
            for qq in range(PAIR):

                @pl.when(jnp.logical_not((d == slab) & (q == qq)))
                def _():
                    out_copy(slab, qq).wait_send()


def in_order(views, order_ref, value_ref, out_ref):
    for k in range(views):
        out_ref[:, k] = value_ref[:, order_ref[k]]


def per_device(depths, tiles, incident, delta, beta, view_order):
    half = HALF
    _, views, rows, cols = incident.shape
    per_slab = delta.shape[1]
    slices = per_slab * depths
    span = PAIR * rows
    edge = LANES // 2
    rmat = jnp.asarray(np.concatenate(in_two(row_matrix(span, half)), axis=0))
    cmat = jnp.asarray(np.stack(in_two(column_matrix(LANES, edge, half))))
    anywhere = pl.BlockSpec(memory_space=pl.ANY)
    hbm = pl.BlockSpec(memory_space=pltpu.HBM)
    vmem = pl.BlockSpec(memory_space=pltpu.VMEM)
    shape = jax.ShapeDtypeStruct((2, views, 1, rows, cols), jnp.float32)
    f32 = jnp.float32
    dma = pltpu.SemaphoreType.DMA
    by_view = pl.pallas_call(
        functools.partial(body, depths, tiles, views, rows, cols, per_slab),
        out_shape=shape,
        in_specs=[hbm] * 5,
        out_specs=anywhere,
        scratch_shapes=[
            pltpu.VMEM((4, views, rows, cols), f32),
            pltpu.VMEM((views, 2, rows, cols), f32),
            pltpu.VMEM((slices, 2, PAIR, rows, cols), f32),
            pltpu.VMEM((slices, 2, span + 2 * half, cols), f32),
            pltpu.VMEM((2, span, cols), f32),
            pltpu.VMEM((depths, 2, span, cols), f32),
            pltpu.VMEM(rmat.shape, rmat.dtype),
            pltpu.VMEM(cmat.shape, cmat.dtype),
            dma((6,)),
            dma((views,)),
            dma((PAIR,)),
            dma((per_slab, 2, views)),
            dma((slices, 2, PAIR)),
            dma((slices, 2, cols // LANES)),
            dma((slices, 2, cols // LANES)),
            dma((depths, PAIR)),
            dma((views,)),
            pltpu.SemaphoreType.REGULAR((views,)),
        ],
        compiler_params=pltpu.CompilerParams(
            collective_id=0, has_side_effects=True, vmem_limit_bytes=63 * 1024 * 1024
        ),
        name="views_by_worker",
    )(incident, delta, beta, rmat, cmat)
    return pl.pallas_call(
        functools.partial(in_order, views),
        out_shape=shape,
        in_specs=[pl.BlockSpec(memory_space=pltpu.SMEM), vmem],
        out_specs=vmem,
        name="stored_order",
    )(view_order, by_view)


def solution(mesh):
    return jax.shard_map(
        functools.partial(per_device, mesh.shape["depth"], mesh.shape["tile"]),
        mesh=mesh,
        in_specs=(
            P(None, None, "tile", None),
            P(None, "depth", "tile", None),
            P(None, "depth", "tile", None),
            P(),
        ),
        out_specs=P(None, None, "depth", "tile", None),
        check_vma=False,
    )
```

```python
import functools

import jax
import jax.numpy as jnp
import ml_dtypes
import numpy as np
from jax import lax
from jax.experimental import pallas as pl
from jax.experimental.pallas import tpu as pltpu
from jax.sharding import PartitionSpec as P

HALF = 32
LANES = 128
PAIR = 2
GROUP = 2
STRIP = 8
MESH = pl.DeviceIdType.MESH

SIN_TERMS = (
    3.1415926535897931,
    -5.1677127800499694,
    2.5501640398773450,
    -0.59926452932079199,
    0.082145886611128236,
    -0.0073704309457143504,
    0.00046630280576761250,
)
COS_TERMS = (
    1.0,
    -4.9348022005446790,
    4.0587121264167676,
    -1.3352627688545893,
    0.23533063035889312,
    -0.025806891390014061,
    0.0019295743094039231,
    -0.00010463810492484570,
)


def series(square, terms):
    total = jnp.full_like(square, terms[-1])
    for term in terms[-2::-1]:
        total = total * square + term
    return total


def taps(offset, half):
    grid = np.arange(-half, half + 1, dtype=np.float64)
    norm = np.abs(
        np.sum((0.75 + 0.25 * np.cos(np.pi * grid / (half + 1))) * np.exp(1j * np.pi * grid**2 / (6.25 * half)))
    )
    place = offset.astype(np.float64)
    value = (0.75 + 0.25 * np.cos(np.pi * place / (half + 1))) * np.exp(1j * np.pi * place**2 / (6.25 * half))
    value = np.where(np.abs(offset) <= half, value / norm, 0.0)
    return value.real, value.imag


def in_two(matrix):
    matrix = matrix.astype(np.float32)
    high = matrix.astype(ml_dtypes.bfloat16)
    low = (matrix - high.astype(np.float32)).astype(ml_dtypes.bfloat16)
    return high, low


def row_matrix(rows, half):
    target, source = np.mgrid[0:rows, 0 : rows + 2 * half]
    real_part, imag_part = taps(source - half - target, half)
    return np.block([[real_part, -imag_part], [imag_part, real_part]])


def column_matrix(block, edge, half):
    source, target = np.mgrid[0 : block + 2 * edge, 0:block]
    real_part, imag_part = taps(source - edge - target, half)
    return np.block([[real_part, imag_part], [-imag_part, real_part]])


def split(value):
    high = value.astype(jnp.bfloat16)
    low = (value - high.astype(jnp.float32)).astype(jnp.bfloat16)
    return high, low


def dot(a, b):
    return jnp.dot(a, b, preferred_element_type=jnp.float32)


def transmitted(delta, beta):
    u = delta - 0.5
    amp = jnp.exp(-beta)
    square = u * u
    return -amp * (u * series(square, SIN_TERMS)), -amp * series(square, COS_TERMS)


def body(
    depths, tiles, views, rows, cols, per_slab,
    incident_ref, delta_ref, beta_ref, rmat_ref, cmat_ref, out_ref,
    loads, first, volume, wave, trans, leaving, rmat_buf, cmat_buf,
    load_sem, first_send, first_recv, vol_send, vol_recv, rim_send, rim_recv, out_send, out_recv, go,
):
    half = HALF
    span = PAIR * rows
    slices = depths * per_slab
    blocks = cols // LANES
    groups = blocks // GROUP
    wide_cols = GROUP * LANES
    edge = LANES // 2
    d = lax.axis_index("depth")
    t = lax.axis_index("tile")
    pair = t // PAIR
    q = t % PAIR
    pairs = tiles // PAIR
    mine = (d // 2) * PAIR + q
    works = (d % 2 == 0) & (mine < views)
    places = [((v // PAIR) * 2, v % PAIR) for v in range(views)]

    def at_worker(v):
        return (d == (v // PAIR) * 2) & (q == v % PAIR)

    def worker(v):
        return ((v // PAIR) * 2, pair * PAIR + v % PAIR)


    taps_in = [
        pltpu.make_async_copy(rmat_ref, rmat_buf, load_sem.at[0]),
        pltpu.make_async_copy(cmat_ref, cmat_buf, load_sem.at[1]),
    ]
    first_in = [
        pltpu.make_async_copy(incident_ref.at[0], loads.at[0], load_sem.at[2]),
        pltpu.make_async_copy(incident_ref.at[1], loads.at[1], load_sem.at[3]),
        pltpu.make_async_copy(delta_ref.at[:, 0], loads.at[2], load_sem.at[4]),
        pltpu.make_async_copy(beta_ref.at[:, 0], loads.at[3], load_sem.at[5]),
    ]

    @pl.when(d == 0)
    def _():
        for copy in first_in:
            copy.start()

    @pl.when(works)
    def _():
        for copy in taps_in:
            copy.start()

    barrier = pltpu.get_barrier_semaphore()
    for dd in range(depths):
        for qq in range(PAIR):
            here = (d == dd) & (q == qq)
            peer = (dd, pair * PAIR + qq)
            if (dd, qq) in places:

                @pl.when(jnp.logical_not(here))
                def _():
                    pl.semaphore_signal(barrier, inc=1, device_id=peer, device_id_type=MESH)
            else:

                @pl.when(works)
                def _():
                    pl.semaphore_signal(barrier, inc=1, device_id=peer, device_id_type=MESH)

    has_up = works & (pair > 0)
    has_down = works & (pair < pairs - 1)
    up = (d, jnp.maximum(t - PAIR, 0))
    down = (d, jnp.minimum(t + PAIR, tiles - 1))

    @pl.when(has_up)
    def _():
        pl.semaphore_signal(barrier, inc=1, device_id=up, device_id_type=MESH)

    @pl.when(has_down)
    def _():
        pl.semaphore_signal(barrier, inc=1, device_id=down, device_id_type=MESH)

    @pl.when(d == 0)
    def _():
        for copy in first_in:
            copy.wait()

        @pl.loop(0, views)
        def _(v):
            @pl.loop(0, rows // STRIP)
            def _(r):
                strip = pl.ds(pl.multiple_of(r * STRIP, STRIP), STRIP)
                real_part, imag_part = transmitted(loads[2, v, strip], loads[3, v, strip])
                wave_re, wave_im = loads[0, v, strip], loads[1, v, strip]
                first[v, 0, strip] = wave_re * real_part - wave_im * imag_part
                first[v, 1, strip] = wave_re * imag_part + wave_im * real_part

    peers = jnp.where(works, depths * PAIR - 1, views)
    pl.semaphore_wait(barrier, peers + has_up.astype(jnp.int32) + has_down.astype(jnp.int32))

    def piece_copy(i, c, v):
        return pltpu.make_async_remote_copy(
            src_ref=(delta_ref, beta_ref)[c].at[v, i],
            dst_ref=volume.at[d * per_slab + i, c, q],
            send_sem=vol_send.at[i, c, v],
            recv_sem=vol_recv.at[d * per_slab + i, c, q],
            device_id=worker(v),
            device_id_type=MESH,
        )

    def send_pieces(i, v):
        here = at_worker(v)

        @pl.when(here)
        def _():
            for c, ref in enumerate((delta_ref, beta_ref)):
                pltpu.make_async_copy(
                    ref.at[v, i], volume.at[d * per_slab + i, c, q], vol_recv.at[d * per_slab + i, c, q]
                ).start()

        @pl.when(jnp.logical_not(here))
        def _():
            for c in range(2):
                piece_copy(i, c, v).start()

    def first_copy(v):
        return pltpu.make_async_remote_copy(
            src_ref=first.at[v],
            dst_ref=wave.at[0, :, pl.ds(half + q * rows, rows)],
            send_sem=first_send.at[v],
            recv_sem=first_recv.at[q],
            device_id=worker(v),
            device_id_type=MESH,
        )

    @pl.when(d == 0)
    def _():
        @pl.loop(0, views)
        def _(v):
            here = at_worker(v)

            @pl.when(here)
            def _():
                pltpu.make_async_copy(
                    first.at[v], wave.at[0, :, pl.ds(half + q * rows, rows)], first_recv.at[q]
                ).start()

            @pl.when(jnp.logical_not(here))
            def _():
                first_copy(v).start()

        @pl.loop(0, views)
        def _(v):
            @pl.when(jnp.logical_not(at_worker(v)))
            def _():
                first_copy(v).wait_send()

        @pl.loop(0, (per_slab - 1) * views)
        def _(k):
            send_pieces(1 + k // views, k % views)

    @pl.when((d > 0) & jnp.logical_not(works))
    def _():
        @pl.loop(0, views)
        def _(v):
            pl.semaphore_wait(go.at[v], 1)

            @pl.loop(0, per_slab)
            def _(i):
                send_pieces(i, v)

    def out_copy(slab, qq):
        return pltpu.make_async_remote_copy(
            src_ref=leaving.at[slab, :, pl.ds(qq * rows, rows)],
            dst_ref=out_ref.at[:, mine, 0],
            send_sem=out_send.at[slab, qq],
            recv_sem=out_recv.at[mine],
            device_id=(slab, pair * PAIR + qq),
            device_id_type=MESH,
        )


    def rim_copy(s, side, h):
        first_row = half if side == 0 else span
        land = span + half if side == 0 else 0
        columns = pl.ds(h * wide_cols, wide_cols)
        return pltpu.make_async_remote_copy(
            src_ref=wave.at[s, :, pl.ds(first_row, half), columns],
            dst_ref=wave.at[s, :, pl.ds(land, half), columns],
            send_sem=rim_send.at[s, side, h],
            recv_sem=rim_recv.at[s, 1 - side, h],
            device_id=up if side == 0 else down,
            device_id_type=MESH,
        )

    def send_rims(s, h):
        @pl.when(has_up & (s < slices))
        def _():
            rim_copy(s, 0, h).start()

        @pl.when(has_down & (s < slices))
        def _():
            rim_copy(s, 1, h).start()

    def rim_arrival(s, side, h):
        land = 0 if side == 0 else span + half
        ref = wave.at[s, :, pl.ds(land, half), pl.ds(h * wide_cols, wide_cols)]
        return pltpu.make_async_copy(ref, ref, rim_recv.at[s, side, h])

    def transmission(s):
        for c in range(2):
            for qq in range(PAIR):
                ref = volume.at[s, c, qq]
                pltpu.make_async_copy(ref, ref, vol_recv.at[s, c, qq]).wait()
        for qq in range(PAIR):

            @pl.loop(0, rows // STRIP)
            def _(r):
                strip = pl.ds(pl.multiple_of(r * STRIP, STRIP), STRIP)
                land = pl.ds(pl.multiple_of(qq * rows + r * STRIP, STRIP), STRIP)
                real_part, imag_part = transmitted(volume[s, 0, qq, strip], volume[s, 1, qq, strip])
                trans[0, land] = real_part
                trans[1, land] = imag_part

    @pl.when(works)
    def _():
        def clear(first_row):
            @pl.loop(0, slices)
            def _(s):
                wave[s, :, first_row : first_row + half] = jnp.zeros((2, half, cols), jnp.float32)

        @pl.when(pair == 0)
        def _():
            clear(0)

        @pl.when(pair == pairs - 1)
        def _():
            clear(span + half)

        for copy in taps_in:
            copy.wait()
        for qq in range(PAIR):
            ref = wave.at[0, :, pl.ds(half + qq * rows, rows)]
            pltpu.make_async_copy(ref, ref, first_recv.at[qq]).wait()
        for h in range(groups):
            send_rims(0, h)

        @pl.loop(0, slices)
        def _(s):
            for dd in range(1, depths):

                @pl.when(s == max(0, (dd - 1) * per_slab - 1))
                def _():
                    for qq in range(PAIR):
                        if (dd, qq) in places:

                            @pl.when((d == dd) & (q == qq))
                            def _():
                                @pl.loop(0, per_slab * views)
                                def _(k):
                                    send_pieces(k // views, k % views)
                        else:
                            pl.semaphore_signal(
                                go.at[mine], inc=1, device_id=(dd, pair * PAIR + qq), device_id_type=MESH
                            )

            @pl.when(s < slices - 1)
            def _():
                transmission(s + 1)

            count = 2 * span

            def rows_done(h):
                @pl.when(has_up)
                def _():
                    rim_arrival(s, 0, h).wait()

                @pl.when(has_down)
                def _():
                    rim_arrival(s, 1, h).wait()

                columns = slice(h * wide_cols, (h + 1) * wide_cols)
                high, low = split(wave[s, :, :, columns].reshape(2 * (span + 2 * half), wide_cols))
                both = dot(rmat_buf[...], high)
                return both[:count] + both[count:] + dot(rmat_buf[:count], low)

            def columns_done(first_block, last_block, pieces):
                high, low = split(pltpu.roll(pieces, pieces.shape[1] - edge, 1))

                def windows(value):
                    return [
                        jnp.concatenate(
                            [
                                value[:span, k * LANES : (k + 2) * LANES],
                                value[span:, k * LANES : (k + 2) * LANES],
                            ],
                            axis=1,
                        )
                        for k in range(last_block - first_block)
                    ]

                high, low = windows(high), windows(low)
                height = span * len(high)
                both = dot(jnp.concatenate(high + low, axis=0), cmat_buf[0])
                result = both[:height] + both[height:] + dot(jnp.concatenate(high, axis=0), cmat_buf[1])
                for k, block in enumerate(range(first_block, last_block)):
                    real_part, imag_part = [
                        result[k * span : (k + 1) * span, part * LANES : (part + 1) * LANES] for part in range(2)
                    ]
                    columns = slice(block * LANES, (block + 1) * LANES)
                    trans_re, trans_im = trans[0, :, columns], trans[1, :, columns]
                    wave[s + 1, 0, half : half + span, columns] = real_part * trans_re - imag_part * trans_im
                    wave[s + 1, 1, half : half + span, columns] = real_part * trans_im + imag_part * trans_re
                    leaving[s // per_slab, 0, :, columns] = real_part
                    leaving[s // per_slab, 1, :, columns] = imag_part

            outside = jnp.zeros((count, LANES), jnp.float32)
            made = []
            for h in range(groups):
                while len(made) < min((h + 1) * GROUP + 1, blocks):
                    joined = rows_done(len(made) // GROUP)
                    made += [joined[:, k * LANES : (k + 1) * LANES] for k in range(GROUP)]
                first_block, last_block = h * GROUP, (h + 1) * GROUP
                pieces = [
                    made[k] if 0 <= k < blocks else outside for k in range(first_block - 1, last_block + 1)
                ]
                columns_done(first_block, last_block, jnp.concatenate(pieces, axis=1))
                send_rims(s + 1, h)

            @pl.when(s % per_slab == per_slab - 1)
            def _():
                slab = s // per_slab
                for qq in range(PAIR):
                    here = (d == slab) & (q == qq)

                    @pl.when(here)
                    def _():
                        pltpu.make_async_copy(
                            leaving.at[slab, :, pl.ds(qq * rows, rows)], out_ref.at[:, mine, 0], out_recv.at[mine]
                        ).start()

                    @pl.when(jnp.logical_not(here))
                    def _():
                        out_copy(slab, qq).start()

    @pl.loop(0, per_slab * views)
    def _(k):
        i, v = k // views, k % views

        @pl.when(jnp.logical_not(at_worker(v)) & ((d > 0) | (i > 0)))
        def _():
            for c in range(2):
                piece_copy(i, c, v).wait_send()

    for v in range(views):
        ref = out_ref.at[:, v, 0]
        pltpu.make_async_copy(ref, ref, out_recv.at[v]).wait()

    @pl.when(works)
    def _():
        @pl.loop(0, slices)
        def _(s):
            @pl.loop(0, groups)
            def _(h):
                @pl.when(has_up)
                def _():
                    rim_copy(s, 0, h).wait_send()

                @pl.when(has_down)
                def _():
                    rim_copy(s, 1, h).wait_send()

        @pl.loop(0, depths)
        def _(slab):
            for qq in range(PAIR):

                @pl.when(jnp.logical_not((d == slab) & (q == qq)))
                def _():
                    out_copy(slab, qq).wait_send()


def in_order(views, order_ref, value_ref, out_ref):
    for k in range(views):
        out_ref[:, k] = value_ref[:, order_ref[k]]


def per_device(depths, tiles, incident, delta, beta, view_order):
    half = HALF
    _, views, rows, cols = incident.shape
    per_slab = delta.shape[1]
    slices = per_slab * depths
    span = PAIR * rows
    edge = LANES // 2
    rmat = jnp.asarray(np.concatenate(in_two(row_matrix(span, half)), axis=0))
    cmat = jnp.asarray(np.stack(in_two(column_matrix(LANES, edge, half))))
    anywhere = pl.BlockSpec(memory_space=pl.ANY)
    hbm = pl.BlockSpec(memory_space=pltpu.HBM)
    vmem = pl.BlockSpec(memory_space=pltpu.VMEM)
    shape = jax.ShapeDtypeStruct((2, views, 1, rows, cols), jnp.float32)
    f32 = jnp.float32
    dma = pltpu.SemaphoreType.DMA
    by_view = pl.pallas_call(
        functools.partial(body, depths, tiles, views, rows, cols, per_slab),
        out_shape=shape,
        in_specs=[hbm] * 5,
        out_specs=anywhere,
        scratch_shapes=[
            pltpu.VMEM((4, views, rows, cols), f32),
            pltpu.VMEM((views, 2, rows, cols), f32),
            pltpu.VMEM((slices, 2, PAIR, rows, cols), f32),
            pltpu.VMEM((slices + 1, 2, span + 2 * half, cols), f32),
            pltpu.VMEM((2, span, cols), f32),
            pltpu.VMEM((depths, 2, span, cols), f32),
            pltpu.VMEM(rmat.shape, rmat.dtype),
            pltpu.VMEM(cmat.shape, cmat.dtype),
            dma((6,)),
            dma((views,)),
            dma((PAIR,)),
            dma((per_slab, 2, views)),
            dma((slices, 2, PAIR)),
            dma((slices, 2, cols // (GROUP * LANES))),
            dma((slices, 2, cols // (GROUP * LANES))),
            dma((depths, PAIR)),
            dma((views,)),
            pltpu.SemaphoreType.REGULAR((views,)),
        ],
        compiler_params=pltpu.CompilerParams(
            collective_id=0, has_side_effects=True, vmem_limit_bytes=63 * 1024 * 1024
        ),
        name="views_by_worker",
    )(incident, delta, beta, rmat, cmat)
    return pl.pallas_call(
        functools.partial(in_order, views),
        out_shape=shape,
        in_specs=[pl.BlockSpec(memory_space=pltpu.SMEM), vmem],
        out_specs=vmem,
        name="stored_order",
    )(view_order, by_view)


def solution(mesh):
    return jax.shard_map(
        functools.partial(per_device, mesh.shape["depth"], mesh.shape["tile"]),
        mesh=mesh,
        in_specs=(
            P(None, None, "tile", None),
            P(None, "depth", "tile", None),
            P(None, "depth", "tile", None),
            P(),
        ),
        out_specs=P(None, None, "depth", "tile", None),
        check_vma=False,
    )
```

```python
import functools

import jax
import jax.numpy as jnp
import ml_dtypes
import numpy as np
from jax import lax
from jax.experimental import pallas as pl
from jax.experimental.pallas import tpu as pltpu
from jax.sharding import PartitionSpec as P

HALF = 32
LANES = 128
PAIR = 2
GROUP = 1
STRIP = 8
MESH = pl.DeviceIdType.MESH

SIN_TERMS = (
    3.1415926535897931,
    -5.1677127800499694,
    2.5501640398773450,
    -0.59926452932079199,
    0.082145886611128236,
    -0.0073704309457143504,
    0.00046630280576761250,
)
COS_TERMS = (
    1.0,
    -4.9348022005446790,
    4.0587121264167676,
    -1.3352627688545893,
    0.23533063035889312,
    -0.025806891390014061,
    0.0019295743094039231,
    -0.00010463810492484570,
)


def series(square, terms):
    total = jnp.full_like(square, terms[-1])
    for term in terms[-2::-1]:
        total = total * square + term
    return total


def taps(offset, half):
    grid = np.arange(-half, half + 1, dtype=np.float64)
    norm = np.abs(
        np.sum((0.75 + 0.25 * np.cos(np.pi * grid / (half + 1))) * np.exp(1j * np.pi * grid**2 / (6.25 * half)))
    )
    place = offset.astype(np.float64)
    value = (0.75 + 0.25 * np.cos(np.pi * place / (half + 1))) * np.exp(1j * np.pi * place**2 / (6.25 * half))
    value = np.where(np.abs(offset) <= half, value / norm, 0.0)
    return value.real, value.imag


def in_two(matrix):
    matrix = matrix.astype(np.float32)
    high = matrix.astype(ml_dtypes.bfloat16)
    low = (matrix - high.astype(np.float32)).astype(ml_dtypes.bfloat16)
    return high, low


def row_matrix(rows, half):
    target, source = np.mgrid[0:rows, 0 : rows + 2 * half]
    real_part, imag_part = taps(source - half - target, half)
    return np.block([[real_part, -imag_part], [imag_part, real_part]])


def column_matrix(block, edge, half):
    source, target = np.mgrid[0 : block + 2 * edge, 0:block]
    real_part, imag_part = taps(source - edge - target, half)
    return np.block([[real_part, imag_part], [-imag_part, real_part]])


def split(value):
    high = value.astype(jnp.bfloat16)
    low = (value - high.astype(jnp.float32)).astype(jnp.bfloat16)
    return high, low


def dot(a, b):
    return jnp.dot(a, b, preferred_element_type=jnp.float32)


def transmitted(delta, beta):
    u = delta - 0.5
    amp = jnp.exp(-beta)
    square = u * u
    return -amp * (u * series(square, SIN_TERMS)), -amp * series(square, COS_TERMS)


def body(
    depths, tiles, views, rows, cols, per_slab,
    incident_ref, delta_ref, beta_ref, rmat_ref, cmat_ref, out_ref,
    loads, first, volume, wave, trans, leaving, rmat_buf, cmat_buf,
    load_sem, first_send, first_recv, vol_send, vol_recv, rim_send, rim_recv, out_send, out_recv, go,
):
    half = HALF
    span = PAIR * rows
    slices = depths * per_slab
    blocks = cols // LANES
    edge = LANES // 2
    d = lax.axis_index("depth")
    t = lax.axis_index("tile")
    pair = t // PAIR
    q = t % PAIR
    pairs = tiles // PAIR
    mine = (d // 2) * PAIR + q
    works = (d % 2 == 0) & (mine < views)
    places = [((v // PAIR) * 2, v % PAIR) for v in range(views)]

    def at_worker(v):
        return (d == (v // PAIR) * 2) & (q == v % PAIR)

    def worker(v):
        return ((v // PAIR) * 2, pair * PAIR + v % PAIR)


    taps_in = [
        pltpu.make_async_copy(rmat_ref, rmat_buf, load_sem.at[0]),
        pltpu.make_async_copy(cmat_ref, cmat_buf, load_sem.at[1]),
    ]
    first_in = [
        pltpu.make_async_copy(incident_ref.at[0], loads.at[0], load_sem.at[2]),
        pltpu.make_async_copy(incident_ref.at[1], loads.at[1], load_sem.at[3]),
        pltpu.make_async_copy(delta_ref.at[:, 0], loads.at[2], load_sem.at[4]),
        pltpu.make_async_copy(beta_ref.at[:, 0], loads.at[3], load_sem.at[5]),
    ]

    @pl.when(d == 0)
    def _():
        for copy in first_in:
            copy.start()

    @pl.when(works)
    def _():
        for copy in taps_in:
            copy.start()

    barrier = pltpu.get_barrier_semaphore()
    for dd in range(depths):
        for qq in range(PAIR):
            here = (d == dd) & (q == qq)
            peer = (dd, pair * PAIR + qq)
            if (dd, qq) in places:

                @pl.when(jnp.logical_not(here))
                def _():
                    pl.semaphore_signal(barrier, inc=1, device_id=peer, device_id_type=MESH)
            else:

                @pl.when(works)
                def _():
                    pl.semaphore_signal(barrier, inc=1, device_id=peer, device_id_type=MESH)

    has_up = works & (pair > 0)
    has_down = works & (pair < pairs - 1)
    up = (d, jnp.maximum(t - PAIR, 0))
    down = (d, jnp.minimum(t + PAIR, tiles - 1))

    @pl.when(has_up)
    def _():
        pl.semaphore_signal(barrier, inc=1, device_id=up, device_id_type=MESH)

    @pl.when(has_down)
    def _():
        pl.semaphore_signal(barrier, inc=1, device_id=down, device_id_type=MESH)

    @pl.when(d == 0)
    def _():
        for copy in first_in:
            copy.wait()

        @pl.loop(0, views)
        def _(v):
            @pl.loop(0, rows // STRIP)
            def _(r):
                strip = pl.ds(pl.multiple_of(r * STRIP, STRIP), STRIP)
                real_part, imag_part = transmitted(loads[2, v, strip], loads[3, v, strip])
                wave_re, wave_im = loads[0, v, strip], loads[1, v, strip]
                first[v, 0, strip] = wave_re * real_part - wave_im * imag_part
                first[v, 1, strip] = wave_re * imag_part + wave_im * real_part

    peers = jnp.where(works, depths * PAIR - 1, views)
    pl.semaphore_wait(barrier, peers + has_up.astype(jnp.int32) + has_down.astype(jnp.int32))

    def piece_copy(i, c, v):
        return pltpu.make_async_remote_copy(
            src_ref=(delta_ref, beta_ref)[c].at[v, i],
            dst_ref=volume.at[d * per_slab + i, c, q],
            send_sem=vol_send.at[i, c, v],
            recv_sem=vol_recv.at[d * per_slab + i, c, q],
            device_id=worker(v),
            device_id_type=MESH,
        )

    def send_pieces(i, v):
        here = at_worker(v)

        @pl.when(here)
        def _():
            for c, ref in enumerate((delta_ref, beta_ref)):
                pltpu.make_async_copy(
                    ref.at[v, i], volume.at[d * per_slab + i, c, q], vol_recv.at[d * per_slab + i, c, q]
                ).start()

        @pl.when(jnp.logical_not(here))
        def _():
            for c in range(2):
                piece_copy(i, c, v).start()

    def first_copy(v):
        return pltpu.make_async_remote_copy(
            src_ref=first.at[v],
            dst_ref=wave.at[0, :, pl.ds(half + q * rows, rows)],
            send_sem=first_send.at[v],
            recv_sem=first_recv.at[q],
            device_id=worker(v),
            device_id_type=MESH,
        )

    @pl.when(d == 0)
    def _():
        @pl.loop(0, views)
        def _(v):
            here = at_worker(v)

            @pl.when(here)
            def _():
                pltpu.make_async_copy(
                    first.at[v], wave.at[0, :, pl.ds(half + q * rows, rows)], first_recv.at[q]
                ).start()

            @pl.when(jnp.logical_not(here))
            def _():
                first_copy(v).start()

        @pl.loop(0, views)
        def _(v):
            @pl.when(jnp.logical_not(at_worker(v)))
            def _():
                first_copy(v).wait_send()

        @pl.loop(0, (per_slab - 1) * views)
        def _(k):
            send_pieces(1 + k // views, k % views)

    @pl.when((d > 0) & jnp.logical_not(works))
    def _():
        @pl.loop(0, views)
        def _(v):
            pl.semaphore_wait(go.at[v], 1)

            @pl.loop(0, per_slab)
            def _(i):
                send_pieces(i, v)

    def out_copy(slab, qq):
        return pltpu.make_async_remote_copy(
            src_ref=leaving.at[slab, :, pl.ds(qq * rows, rows)],
            dst_ref=out_ref.at[:, mine, 0],
            send_sem=out_send.at[slab, qq],
            recv_sem=out_recv.at[mine],
            device_id=(slab, pair * PAIR + qq),
            device_id_type=MESH,
        )


    def rim_copy(s, side, h):
        first_row = half if side == 0 else span
        land = span + half if side == 0 else 0
        columns = pl.ds(h * LANES, LANES)
        return pltpu.make_async_remote_copy(
            src_ref=wave.at[s, :, pl.ds(first_row, half), columns],
            dst_ref=wave.at[s, :, pl.ds(land, half), columns],
            send_sem=rim_send.at[s, side, h],
            recv_sem=rim_recv.at[s, 1 - side, h],
            device_id=up if side == 0 else down,
            device_id_type=MESH,
        )

    def send_rims(s, first_block, last_block):
        @pl.when(has_up & (s < slices))
        def _():
            for h in range(first_block, last_block):
                rim_copy(s, 0, h).start()

        @pl.when(has_down & (s < slices))
        def _():
            for h in range(first_block, last_block):
                rim_copy(s, 1, h).start()

    def rim_arrival(s, side, h):
        land = 0 if side == 0 else span + half
        ref = wave.at[s, :, pl.ds(land, half), pl.ds(h * LANES, LANES)]
        return pltpu.make_async_copy(ref, ref, rim_recv.at[s, side, h])

    def transmission(s):
        for c in range(2):
            for qq in range(PAIR):
                ref = volume.at[s, c, qq]
                pltpu.make_async_copy(ref, ref, vol_recv.at[s, c, qq]).wait()
        for qq in range(PAIR):

            @pl.loop(0, rows // STRIP)
            def _(r):
                strip = pl.ds(pl.multiple_of(r * STRIP, STRIP), STRIP)
                land = pl.ds(pl.multiple_of(qq * rows + r * STRIP, STRIP), STRIP)
                real_part, imag_part = transmitted(volume[s, 0, qq, strip], volume[s, 1, qq, strip])
                trans[0, land] = real_part
                trans[1, land] = imag_part

    @pl.when(works)
    def _():
        def clear(first_row):
            @pl.loop(0, slices)
            def _(s):
                wave[s, :, first_row : first_row + half] = jnp.zeros((2, half, cols), jnp.float32)

        @pl.when(pair == 0)
        def _():
            clear(0)

        @pl.when(pair == pairs - 1)
        def _():
            clear(span + half)

        for copy in taps_in:
            copy.wait()
        for qq in range(PAIR):
            ref = wave.at[0, :, pl.ds(half + qq * rows, rows)]
            pltpu.make_async_copy(ref, ref, first_recv.at[qq]).wait()
        send_rims(0, 0, blocks)

        @pl.loop(0, slices)
        def _(s):
            for dd in range(1, depths):

                @pl.when(s == max(0, (dd - 1) * per_slab - 1))
                def _():
                    for qq in range(PAIR):
                        if (dd, qq) in places:

                            @pl.when((d == dd) & (q == qq))
                            def _():
                                @pl.loop(0, per_slab * views)
                                def _(k):
                                    send_pieces(k // views, k % views)
                        else:
                            pl.semaphore_signal(
                                go.at[mine], inc=1, device_id=(dd, pair * PAIR + qq), device_id_type=MESH
                            )

            @pl.when(s < slices - 1)
            def _():
                transmission(s + 1)

            count = 2 * span

            def rows_done(first_block, last_block):
                @pl.when(has_up)
                def _():
                    for h in range(first_block, last_block):
                        rim_arrival(s, 0, h).wait()

                @pl.when(has_down)
                def _():
                    for h in range(first_block, last_block):
                        rim_arrival(s, 1, h).wait()

                columns = slice(first_block * LANES, last_block * LANES)
                width = (last_block - first_block) * LANES
                high, low = split(wave[s, :, :, columns].reshape(2 * (span + 2 * half), width))
                both = dot(rmat_buf[...], high)
                return both[:count] + both[count:] + dot(rmat_buf[:count], low)

            def columns_done(first_block, last_block, pieces):
                high, low = split(pltpu.roll(pieces, pieces.shape[1] - edge, 1))

                def windows(value):
                    return [
                        jnp.concatenate(
                            [
                                value[:span, k * LANES : (k + 2) * LANES],
                                value[span:, k * LANES : (k + 2) * LANES],
                            ],
                            axis=1,
                        )
                        for k in range(last_block - first_block)
                    ]

                high, low = windows(high), windows(low)
                height = span * len(high)
                both = dot(jnp.concatenate(high + low, axis=0), cmat_buf[0])
                result = both[:height] + both[height:] + dot(jnp.concatenate(high, axis=0), cmat_buf[1])
                for k, block in enumerate(range(first_block, last_block)):
                    real_part, imag_part = [
                        result[k * span : (k + 1) * span, part * LANES : (part + 1) * LANES] for part in range(2)
                    ]
                    columns = slice(block * LANES, (block + 1) * LANES)
                    trans_re, trans_im = trans[0, :, columns], trans[1, :, columns]
                    wave[s + 1, 0, half : half + span, columns] = real_part * trans_re - imag_part * trans_im
                    wave[s + 1, 1, half : half + span, columns] = real_part * trans_im + imag_part * trans_re
                    leaving[s // per_slab, 0, :, columns] = real_part
                    leaving[s // per_slab, 1, :, columns] = imag_part

            outside = jnp.zeros((count, LANES), jnp.float32)
            made = []
            for first_block in range(0, blocks, GROUP):
                last_block = min(first_block + GROUP, blocks)
                for wanted in (last_block, min(last_block + 1, blocks)):
                    if len(made) < wanted:
                        joined = rows_done(len(made), wanted)
                        made += [joined[:, k : k + LANES] for k in range(0, joined.shape[1], LANES)]
                pieces = [
                    made[k] if 0 <= k < blocks else outside for k in range(first_block - 1, last_block + 1)
                ]
                columns_done(first_block, last_block, jnp.concatenate(pieces, axis=1))
                send_rims(s + 1, first_block, last_block)

            @pl.when(s % per_slab == per_slab - 1)
            def _():
                slab = s // per_slab
                for qq in range(PAIR):
                    here = (d == slab) & (q == qq)

                    @pl.when(here)
                    def _():
                        pltpu.make_async_copy(
                            leaving.at[slab, :, pl.ds(qq * rows, rows)], out_ref.at[:, mine, 0], out_recv.at[mine]
                        ).start()

                    @pl.when(jnp.logical_not(here))
                    def _():
                        out_copy(slab, qq).start()

    @pl.loop(0, per_slab * views)
    def _(k):
        i, v = k // views, k % views

        @pl.when(jnp.logical_not(at_worker(v)) & ((d > 0) | (i > 0)))
        def _():
            for c in range(2):
                piece_copy(i, c, v).wait_send()

    for v in range(views):
        ref = out_ref.at[:, v, 0]
        pltpu.make_async_copy(ref, ref, out_recv.at[v]).wait()

    @pl.when(works)
    def _():
        @pl.loop(0, slices)
        def _(s):
            @pl.loop(0, blocks)
            def _(h):
                @pl.when(has_up)
                def _():
                    rim_copy(s, 0, h).wait_send()

                @pl.when(has_down)
                def _():
                    rim_copy(s, 1, h).wait_send()

        @pl.loop(0, depths)
        def _(slab):
            for qq in range(PAIR):

                @pl.when(jnp.logical_not((d == slab) & (q == qq)))
                def _():
                    out_copy(slab, qq).wait_send()


def in_order(views, order_ref, value_ref, out_ref):
    for k in range(views):
        out_ref[:, k] = value_ref[:, order_ref[k]]


def per_device(depths, tiles, incident, delta, beta, view_order):
    half = HALF
    _, views, rows, cols = incident.shape
    per_slab = delta.shape[1]
    slices = per_slab * depths
    span = PAIR * rows
    edge = LANES // 2
    rmat = jnp.asarray(np.concatenate(in_two(row_matrix(span, half)), axis=0))
    cmat = jnp.asarray(np.stack(in_two(column_matrix(LANES, edge, half))))
    anywhere = pl.BlockSpec(memory_space=pl.ANY)
    hbm = pl.BlockSpec(memory_space=pltpu.HBM)
    vmem = pl.BlockSpec(memory_space=pltpu.VMEM)
    shape = jax.ShapeDtypeStruct((2, views, 1, rows, cols), jnp.float32)
    f32 = jnp.float32
    dma = pltpu.SemaphoreType.DMA
    by_view = pl.pallas_call(
        functools.partial(body, depths, tiles, views, rows, cols, per_slab),
        out_shape=shape,
        in_specs=[hbm] * 5,
        out_specs=anywhere,
        scratch_shapes=[
            pltpu.VMEM((4, views, rows, cols), f32),
            pltpu.VMEM((views, 2, rows, cols), f32),
            pltpu.VMEM((slices, 2, PAIR, rows, cols), f32),
            pltpu.VMEM((slices + 1, 2, span + 2 * half, cols), f32),
            pltpu.VMEM((2, span, cols), f32),
            pltpu.VMEM((depths, 2, span, cols), f32),
            pltpu.VMEM(rmat.shape, rmat.dtype),
            pltpu.VMEM(cmat.shape, cmat.dtype),
            dma((6,)),
            dma((views,)),
            dma((PAIR,)),
            dma((per_slab, 2, views)),
            dma((slices, 2, PAIR)),
            dma((slices, 2, cols // LANES)),
            dma((slices, 2, cols // LANES)),
            dma((depths, PAIR)),
            dma((views,)),
            pltpu.SemaphoreType.REGULAR((views,)),
        ],
        compiler_params=pltpu.CompilerParams(
            collective_id=0, has_side_effects=True, vmem_limit_bytes=63 * 1024 * 1024
        ),
        name="views_by_worker",
    )(incident, delta, beta, rmat, cmat)
    return pl.pallas_call(
        functools.partial(in_order, views),
        out_shape=shape,
        in_specs=[pl.BlockSpec(memory_space=pltpu.SMEM), vmem],
        out_specs=vmem,
        name="stored_order",
    )(view_order, by_view)


def solution(mesh):
    return jax.shard_map(
        functools.partial(per_device, mesh.shape["depth"], mesh.shape["tile"]),
        mesh=mesh,
        in_specs=(
            P(None, None, "tile", None),
            P(None, "depth", "tile", None),
            P(None, "depth", "tile", None),
            P(),
        ),
        out_specs=P(None, None, "depth", "tile", None),
        check_vma=False,
    )
```

```python
import functools

import jax
import jax.numpy as jnp
import ml_dtypes
import numpy as np
from jax import lax
from jax.experimental import pallas as pl
from jax.experimental.pallas import tpu as pltpu
from jax.sharding import PartitionSpec as P

HALF = 32
LANES = 128
PAIR = 2
GROUP = 1
STRIP = 8
MESH = pl.DeviceIdType.MESH

SIN_TERMS = (
    3.1415926535897931,
    -5.1677127800499694,
    2.5501640398773450,
    -0.59926452932079199,
    0.082145886611128236,
    -0.0073704309457143504,
    0.00046630280576761250,
)
COS_TERMS = (
    1.0,
    -4.9348022005446790,
    4.0587121264167676,
    -1.3352627688545893,
    0.23533063035889312,
    -0.025806891390014061,
    0.0019295743094039231,
    -0.00010463810492484570,
)


def series(square, terms):
    total = jnp.full_like(square, terms[-1])
    for term in terms[-2::-1]:
        total = total * square + term
    return total


def taps(offset, half):
    grid = np.arange(-half, half + 1, dtype=np.float64)
    norm = np.abs(
        np.sum((0.75 + 0.25 * np.cos(np.pi * grid / (half + 1))) * np.exp(1j * np.pi * grid**2 / (6.25 * half)))
    )
    place = offset.astype(np.float64)
    value = (0.75 + 0.25 * np.cos(np.pi * place / (half + 1))) * np.exp(1j * np.pi * place**2 / (6.25 * half))
    value = np.where(np.abs(offset) <= half, value / norm, 0.0)
    return value.real, value.imag


def in_two(matrix):
    matrix = matrix.astype(np.float32)
    high = matrix.astype(ml_dtypes.bfloat16)
    low = (matrix - high.astype(np.float32)).astype(ml_dtypes.bfloat16)
    return high, low


def row_matrix(rows, half):
    target, source = np.mgrid[0:rows, 0 : rows + 2 * half]
    real_part, imag_part = taps(source - half - target, half)
    return np.block([[real_part, -imag_part], [imag_part, real_part]])


def column_matrix(block, edge, half):
    source, target = np.mgrid[0 : block + 2 * edge, 0:block]
    real_part, imag_part = taps(source - edge - target, half)
    return np.block([[real_part, imag_part], [-imag_part, real_part]])


def split(value):
    high = value.astype(jnp.bfloat16)
    low = (value - high.astype(jnp.float32)).astype(jnp.bfloat16)
    return high, low


def dot(a, b):
    return jnp.dot(a, b, preferred_element_type=jnp.float32)


def transmitted(delta, beta):
    u = delta - 0.5
    amp = jnp.exp(-beta)
    square = u * u
    return -amp * (u * series(square, SIN_TERMS)), -amp * series(square, COS_TERMS)


def body(
    depths, tiles, views, rows, cols, per_slab,
    incident_ref, delta_ref, beta_ref, rmat_ref, cmat_ref, out_ref,
    loads, first, volume, wave, trans, leaving, rmat_buf, cmat_buf,
    load_sem, first_send, first_recv, vol_send, vol_recv, rim_send, rim_recv, out_send, out_recv, go,
    passing, passing_first, pass_send, pass_recv, pass_first_send, pass_first_recv,
):
    half = HALF
    span = PAIR * rows
    slices = depths * per_slab
    blocks = cols // LANES
    edge = LANES // 2
    d = lax.axis_index("depth")
    t = lax.axis_index("tile")
    pair = t // PAIR
    q = t % PAIR
    pairs = tiles // PAIR
    mine = (d // 2) * PAIR + q
    works = (d % 2 == 0) & (mine < views)
    places = [((v // PAIR) * 2, v % PAIR) for v in range(views)]

    def at_worker(v):
        return (d == (v // PAIR) * 2) & (q == v % PAIR)

    def worker(v):
        return ((v // PAIR) * 2, pair * PAIR + v % PAIR)


    taps_in = [
        pltpu.make_async_copy(rmat_ref, rmat_buf, load_sem.at[0]),
        pltpu.make_async_copy(cmat_ref, cmat_buf, load_sem.at[1]),
    ]
    first_in = [
        pltpu.make_async_copy(incident_ref.at[0], loads.at[0], load_sem.at[2]),
        pltpu.make_async_copy(incident_ref.at[1], loads.at[1], load_sem.at[3]),
        pltpu.make_async_copy(delta_ref.at[:, 0], loads.at[2], load_sem.at[4]),
        pltpu.make_async_copy(beta_ref.at[:, 0], loads.at[3], load_sem.at[5]),
    ]

    @pl.when(d == 0)
    def _():
        for copy in first_in:
            copy.start()

    @pl.when(works)
    def _():
        for copy in taps_in:
            copy.start()

    relayed = None
    for v, (dd, qq) in enumerate(places):
        if dd >= 2 and PAIR == 2 and not any((dd + core, 1 - qq) in places for core in range(2)):
            relayed = v
            break
    if relayed is None:
        gives = passes = partners = jnp.bool_(False)
        there = 0
    else:
        there, side = places[relayed]
        gives = (d < 2) & (q != side)
        passes = (d >= there) & (d < there + 2) & (q != side)
        partners = (gives | passes) & (d % 2 == 1)

    barrier = pltpu.get_barrier_semaphore()

    @pl.when(partners)
    def _():
        other = jnp.where(gives, d + there, d - there)
        pl.semaphore_signal(barrier, inc=1, device_id=(other, t), device_id_type=MESH)

    for dd in range(depths):
        for qq in range(PAIR):
            here = (d == dd) & (q == qq)
            peer = (dd, pair * PAIR + qq)
            if (dd, qq) in places:

                @pl.when(jnp.logical_not(here))
                def _():
                    pl.semaphore_signal(barrier, inc=1, device_id=peer, device_id_type=MESH)
            else:

                @pl.when(works)
                def _():
                    pl.semaphore_signal(barrier, inc=1, device_id=peer, device_id_type=MESH)

    has_up = works & (pair > 0)
    has_down = works & (pair < pairs - 1)
    up = (d, jnp.maximum(t - PAIR, 0))
    down = (d, jnp.minimum(t + PAIR, tiles - 1))

    @pl.when(has_up)
    def _():
        pl.semaphore_signal(barrier, inc=1, device_id=up, device_id_type=MESH)

    @pl.when(has_down)
    def _():
        pl.semaphore_signal(barrier, inc=1, device_id=down, device_id_type=MESH)

    @pl.when(d == 0)
    def _():
        for copy in first_in:
            copy.wait()

        @pl.loop(0, views)
        def _(v):
            @pl.loop(0, rows // STRIP)
            def _(r):
                strip = pl.ds(pl.multiple_of(r * STRIP, STRIP), STRIP)
                real_part, imag_part = transmitted(loads[2, v, strip], loads[3, v, strip])
                wave_re, wave_im = loads[0, v, strip], loads[1, v, strip]
                first[v, 0, strip] = wave_re * real_part - wave_im * imag_part
                first[v, 1, strip] = wave_re * imag_part + wave_im * real_part

    peers = jnp.where(works, depths * PAIR - 1, views) + partners.astype(jnp.int32)
    pl.semaphore_wait(barrier, peers + has_up.astype(jnp.int32) + has_down.astype(jnp.int32))

    def piece_copy(i, c, v):
        return pltpu.make_async_remote_copy(
            src_ref=(delta_ref, beta_ref)[c].at[v, i],
            dst_ref=volume.at[d * per_slab + i, c, q],
            send_sem=vol_send.at[i, c, v],
            recv_sem=vol_recv.at[d * per_slab + i, c, q],
            device_id=worker(v),
            device_id_type=MESH,
        )

    def by_relay(v):
        return gives & (v == (-1 if relayed is None else relayed))

    def piece_to_relay(i, c):
        return pltpu.make_async_remote_copy(
            src_ref=(delta_ref, beta_ref)[c].at[relayed or 0, i],
            dst_ref=passing.at[i, c],
            send_sem=vol_send.at[i, c, relayed or 0],
            recv_sem=pass_recv.at[i, c],
            device_id=(d + there, t),
            device_id_type=MESH,
        )

    def piece_from_relay(i, c):
        return pltpu.make_async_remote_copy(
            src_ref=passing.at[i, c],
            dst_ref=volume.at[(d - there) * per_slab + i, c, q],
            send_sem=pass_send.at[i, c],
            recv_sem=vol_recv.at[(d - there) * per_slab + i, c, q],
            device_id=worker(relayed or 0),
            device_id_type=MESH,
        )

    def first_to_relay():
        return pltpu.make_async_remote_copy(
            src_ref=first.at[relayed or 0],
            dst_ref=passing_first,
            send_sem=first_send.at[relayed or 0],
            recv_sem=pass_first_recv,
            device_id=(d + there, t),
            device_id_type=MESH,
        )

    def first_from_relay():
        return pltpu.make_async_remote_copy(
            src_ref=passing_first,
            dst_ref=wave.at[0, :, pl.ds(half + q * rows, rows)],
            send_sem=pass_first_send,
            recv_sem=first_recv.at[q],
            device_id=worker(relayed or 0),
            device_id_type=MESH,
        )

    def send_pieces(i, v):
        here = at_worker(v)

        @pl.when(by_relay(v))
        def _():
            for c in range(2):
                piece_to_relay(i, c).start()

        @pl.when(here)
        def _():
            for c, ref in enumerate((delta_ref, beta_ref)):
                pltpu.make_async_copy(
                    ref.at[v, i], volume.at[d * per_slab + i, c, q], vol_recv.at[d * per_slab + i, c, q]
                ).start()

        @pl.when(jnp.logical_not(here | by_relay(v)))
        def _():
            for c in range(2):
                piece_copy(i, c, v).start()

    def first_copy(v):
        return pltpu.make_async_remote_copy(
            src_ref=first.at[v],
            dst_ref=wave.at[0, :, pl.ds(half + q * rows, rows)],
            send_sem=first_send.at[v],
            recv_sem=first_recv.at[q],
            device_id=worker(v),
            device_id_type=MESH,
        )

    @pl.when(d == 0)
    def _():
        @pl.loop(0, views)
        def _(v):
            here = at_worker(v)

            @pl.when(here)
            def _():
                pltpu.make_async_copy(
                    first.at[v], wave.at[0, :, pl.ds(half + q * rows, rows)], first_recv.at[q]
                ).start()

            @pl.when(by_relay(v))
            def _():
                first_to_relay().start()

            @pl.when(jnp.logical_not(here | by_relay(v)))
            def _():
                first_copy(v).start()

        @pl.loop(0, views)
        def _(v):
            @pl.when(jnp.logical_not(at_worker(v)))
            def _():
                first_copy(v).wait_send()

        @pl.loop(0, (per_slab - 1) * views)
        def _(k):
            send_pieces(1 + k // views, k % views)

    @pl.when(passes)
    def _():
        @pl.when(d == there)
        def _():
            pltpu.make_async_copy(passing_first, passing_first, pass_first_recv).wait()
            first_from_relay().start()

        @pl.loop(jnp.where(d == there, 1, 0), per_slab)
        def _(i):
            for c in range(2):
                pltpu.make_async_copy(passing.at[i, c], passing.at[i, c], pass_recv.at[i, c]).wait()
                piece_from_relay(i, c).start()

    @pl.when((d > 0) & jnp.logical_not(works))
    def _():
        @pl.loop(0, views)
        def _(v):
            pl.semaphore_wait(go.at[v], 1)

            @pl.loop(0, per_slab)
            def _(i):
                send_pieces(i, v)

    def out_copy(slab, qq):
        return pltpu.make_async_remote_copy(
            src_ref=leaving.at[slab, :, pl.ds(qq * rows, rows)],
            dst_ref=out_ref.at[:, mine, 0],
            send_sem=out_send.at[slab, qq],
            recv_sem=out_recv.at[mine],
            device_id=(slab, pair * PAIR + qq),
            device_id_type=MESH,
        )


    def rim_copy(s, side, h):
        first_row = half if side == 0 else span
        land = span + half if side == 0 else 0
        columns = pl.ds(h * LANES, LANES)
        return pltpu.make_async_remote_copy(
            src_ref=wave.at[s, :, pl.ds(first_row, half), columns],
            dst_ref=wave.at[s, :, pl.ds(land, half), columns],
            send_sem=rim_send.at[s, side, h],
            recv_sem=rim_recv.at[s, 1 - side, h],
            device_id=up if side == 0 else down,
            device_id_type=MESH,
        )

    def send_rims(s, first_block, last_block):
        @pl.when(has_up & (s < slices))
        def _():
            for h in range(first_block, last_block):
                rim_copy(s, 0, h).start()

        @pl.when(has_down & (s < slices))
        def _():
            for h in range(first_block, last_block):
                rim_copy(s, 1, h).start()

    def rim_arrival(s, side, h):
        land = 0 if side == 0 else span + half
        ref = wave.at[s, :, pl.ds(land, half), pl.ds(h * LANES, LANES)]
        return pltpu.make_async_copy(ref, ref, rim_recv.at[s, side, h])

    def transmission(s):
        for c in range(2):
            for qq in range(PAIR):
                ref = volume.at[s, c, qq]
                pltpu.make_async_copy(ref, ref, vol_recv.at[s, c, qq]).wait()
        for qq in range(PAIR):

            @pl.loop(0, rows // STRIP)
            def _(r):
                strip = pl.ds(pl.multiple_of(r * STRIP, STRIP), STRIP)
                land = pl.ds(pl.multiple_of(qq * rows + r * STRIP, STRIP), STRIP)
                real_part, imag_part = transmitted(volume[s, 0, qq, strip], volume[s, 1, qq, strip])
                trans[0, land] = real_part
                trans[1, land] = imag_part

    @pl.when(works)
    def _():
        def clear(first_row):
            @pl.loop(0, slices)
            def _(s):
                wave[s, :, first_row : first_row + half] = jnp.zeros((2, half, cols), jnp.float32)

        @pl.when(pair == 0)
        def _():
            clear(0)

        @pl.when(pair == pairs - 1)
        def _():
            clear(span + half)

        for copy in taps_in:
            copy.wait()
        for qq in range(PAIR):
            ref = wave.at[0, :, pl.ds(half + qq * rows, rows)]
            pltpu.make_async_copy(ref, ref, first_recv.at[qq]).wait()
        send_rims(0, 0, blocks)

        @pl.loop(0, slices)
        def _(s):
            for dd in range(1, depths):

                @pl.when(s == max(0, (dd - 1) * per_slab - 1))
                def _():
                    for qq in range(PAIR):
                        if (dd, qq) in places:

                            @pl.when((d == dd) & (q == qq))
                            def _():
                                @pl.loop(0, per_slab * views)
                                def _(k):
                                    send_pieces(k // views, k % views)
                        else:
                            pl.semaphore_signal(
                                go.at[mine], inc=1, device_id=(dd, pair * PAIR + qq), device_id_type=MESH
                            )

            @pl.when(s < slices - 1)
            def _():
                transmission(s + 1)

            count = 2 * span

            def rows_done(first_block, last_block):
                @pl.when(has_up)
                def _():
                    for h in range(first_block, last_block):
                        rim_arrival(s, 0, h).wait()

                @pl.when(has_down)
                def _():
                    for h in range(first_block, last_block):
                        rim_arrival(s, 1, h).wait()

                columns = slice(first_block * LANES, last_block * LANES)
                width = (last_block - first_block) * LANES
                high, low = split(wave[s, :, :, columns].reshape(2 * (span + 2 * half), width))
                both = dot(rmat_buf[...], high)
                return both[:count] + both[count:] + dot(rmat_buf[:count], low)

            def columns_done(first_block, last_block, pieces):
                high, low = split(pltpu.roll(pieces, pieces.shape[1] - edge, 1))

                def windows(value):
                    return [
                        jnp.concatenate(
                            [
                                value[:span, k * LANES : (k + 2) * LANES],
                                value[span:, k * LANES : (k + 2) * LANES],
                            ],
                            axis=1,
                        )
                        for k in range(last_block - first_block)
                    ]

                high, low = windows(high), windows(low)
                height = span * len(high)
                both = dot(jnp.concatenate(high + low, axis=0), cmat_buf[0])
                result = both[:height] + both[height:] + dot(jnp.concatenate(high, axis=0), cmat_buf[1])
                for k, block in enumerate(range(first_block, last_block)):
                    real_part, imag_part = [
                        result[k * span : (k + 1) * span, part * LANES : (part + 1) * LANES] for part in range(2)
                    ]
                    columns = slice(block * LANES, (block + 1) * LANES)
                    trans_re, trans_im = trans[0, :, columns], trans[1, :, columns]
                    wave[s + 1, 0, half : half + span, columns] = real_part * trans_re - imag_part * trans_im
                    wave[s + 1, 1, half : half + span, columns] = real_part * trans_im + imag_part * trans_re
                    leaving[s // per_slab, 0, :, columns] = real_part
                    leaving[s // per_slab, 1, :, columns] = imag_part

            outside = jnp.zeros((count, LANES), jnp.float32)
            made = []
            for first_block in range(0, blocks, GROUP):
                last_block = min(first_block + GROUP, blocks)
                for wanted in (last_block, min(last_block + 1, blocks)):
                    if len(made) < wanted:
                        joined = rows_done(len(made), wanted)
                        made += [joined[:, k : k + LANES] for k in range(0, joined.shape[1], LANES)]
                pieces = [
                    made[k] if 0 <= k < blocks else outside for k in range(first_block - 1, last_block + 1)
                ]
                columns_done(first_block, last_block, jnp.concatenate(pieces, axis=1))
                send_rims(s + 1, first_block, last_block)

            @pl.when(s % per_slab == per_slab - 1)
            def _():
                slab = s // per_slab
                for qq in range(PAIR):
                    here = (d == slab) & (q == qq)

                    @pl.when(here)
                    def _():
                        pltpu.make_async_copy(
                            leaving.at[slab, :, pl.ds(qq * rows, rows)], out_ref.at[:, mine, 0], out_recv.at[mine]
                        ).start()

                    @pl.when(jnp.logical_not(here))
                    def _():
                        out_copy(slab, qq).start()

    @pl.loop(0, per_slab * views)
    def _(k):
        i, v = k // views, k % views

        @pl.when(jnp.logical_not(at_worker(v)) & ((d > 0) | (i > 0)))
        def _():
            for c in range(2):
                piece_copy(i, c, v).wait_send()

    @pl.when(passes)
    def _():
        @pl.when(d == there)
        def _():
            first_from_relay().wait_send()

        @pl.loop(jnp.where(d == there, 1, 0), per_slab)
        def _(i):
            for c in range(2):
                piece_from_relay(i, c).wait_send()

    for v in range(views):
        ref = out_ref.at[:, v, 0]
        pltpu.make_async_copy(ref, ref, out_recv.at[v]).wait()

    @pl.when(works)
    def _():
        @pl.loop(0, slices)
        def _(s):
            @pl.loop(0, blocks)
            def _(h):
                @pl.when(has_up)
                def _():
                    rim_copy(s, 0, h).wait_send()

                @pl.when(has_down)
                def _():
                    rim_copy(s, 1, h).wait_send()

        @pl.loop(0, depths)
        def _(slab):
            for qq in range(PAIR):

                @pl.when(jnp.logical_not((d == slab) & (q == qq)))
                def _():
                    out_copy(slab, qq).wait_send()


def in_order(views, order_ref, value_ref, out_ref):
    for k in range(views):
        out_ref[:, k] = value_ref[:, order_ref[k]]


def per_device(depths, tiles, incident, delta, beta, view_order):
    half = HALF
    _, views, rows, cols = incident.shape
    per_slab = delta.shape[1]
    slices = per_slab * depths
    span = PAIR * rows
    edge = LANES // 2
    rmat = jnp.asarray(np.concatenate(in_two(row_matrix(span, half)), axis=0))
    cmat = jnp.asarray(np.stack(in_two(column_matrix(LANES, edge, half))))
    anywhere = pl.BlockSpec(memory_space=pl.ANY)
    hbm = pl.BlockSpec(memory_space=pltpu.HBM)
    vmem = pl.BlockSpec(memory_space=pltpu.VMEM)
    shape = jax.ShapeDtypeStruct((2, views, 1, rows, cols), jnp.float32)
    f32 = jnp.float32
    dma = pltpu.SemaphoreType.DMA
    by_view = pl.pallas_call(
        functools.partial(body, depths, tiles, views, rows, cols, per_slab),
        out_shape=shape,
        in_specs=[hbm] * 5,
        out_specs=anywhere,
        scratch_shapes=[
            pltpu.VMEM((4, views, rows, cols), f32),
            pltpu.VMEM((views, 2, rows, cols), f32),
            pltpu.VMEM((slices, 2, PAIR, rows, cols), f32),
            pltpu.VMEM((slices + 1, 2, span + 2 * half, cols), f32),
            pltpu.VMEM((2, span, cols), f32),
            pltpu.VMEM((depths, 2, span, cols), f32),
            pltpu.VMEM(rmat.shape, rmat.dtype),
            pltpu.VMEM(cmat.shape, cmat.dtype),
            dma((6,)),
            dma((views,)),
            dma((PAIR,)),
            dma((per_slab, 2, views)),
            dma((slices, 2, PAIR)),
            dma((slices, 2, cols // LANES)),
            dma((slices, 2, cols // LANES)),
            dma((depths, PAIR)),
            dma((views,)),
            pltpu.SemaphoreType.REGULAR((views,)),
            pltpu.VMEM((per_slab, 2, rows, cols), f32),
            pltpu.VMEM((2, rows, cols), f32),
            dma((per_slab, 2)),
            dma((per_slab, 2)),
            dma,
            dma,
        ],
        compiler_params=pltpu.CompilerParams(
            collective_id=0, has_side_effects=True, vmem_limit_bytes=63 * 1024 * 1024
        ),
        name="views_by_worker",
    )(incident, delta, beta, rmat, cmat)
    return pl.pallas_call(
        functools.partial(in_order, views),
        out_shape=shape,
        in_specs=[pl.BlockSpec(memory_space=pltpu.SMEM), vmem],
        out_specs=vmem,
        name="stored_order",
    )(view_order, by_view)


def solution(mesh):
    return jax.shard_map(
        functools.partial(per_device, mesh.shape["depth"], mesh.shape["tile"]),
        mesh=mesh,
        in_specs=(
            P(None, None, "tile", None),
            P(None, "depth", "tile", None),
            P(None, "depth", "tile", None),
            P(),
        ),
        out_specs=P(None, None, "depth", "tile", None),
        check_vma=False,
    )
```

```python
import functools

import jax
import jax.numpy as jnp
import ml_dtypes
import numpy as np
from jax import lax
from jax.experimental import pallas as pl
from jax.experimental.pallas import tpu as pltpu
from jax.sharding import PartitionSpec as P

HALF = 32
LANES = 128
PAIR = 2
GROUP = 2
STRIP = 8
MESH = pl.DeviceIdType.MESH

SIN_TERMS = (
    3.1415926535897931,
    -5.1677127800499694,
    2.5501640398773450,
    -0.59926452932079199,
    0.082145886611128236,
    -0.0073704309457143504,
    0.00046630280576761250,
)
COS_TERMS = (
    1.0,
    -4.9348022005446790,
    4.0587121264167676,
    -1.3352627688545893,
    0.23533063035889312,
    -0.025806891390014061,
    0.0019295743094039231,
    -0.00010463810492484570,
)


def series(square, terms):
    total = jnp.full_like(square, terms[-1])
    for term in terms[-2::-1]:
        total = total * square + term
    return total


def taps(offset, half):
    grid = np.arange(-half, half + 1, dtype=np.float64)
    norm = np.abs(
        np.sum((0.75 + 0.25 * np.cos(np.pi * grid / (half + 1))) * np.exp(1j * np.pi * grid**2 / (6.25 * half)))
    )
    place = offset.astype(np.float64)
    value = (0.75 + 0.25 * np.cos(np.pi * place / (half + 1))) * np.exp(1j * np.pi * place**2 / (6.25 * half))
    value = np.where(np.abs(offset) <= half, value / norm, 0.0)
    return value.real, value.imag


def in_two(matrix):
    matrix = matrix.astype(np.float32)
    high = matrix.astype(ml_dtypes.bfloat16)
    low = (matrix - high.astype(np.float32)).astype(ml_dtypes.bfloat16)
    return high, low


def row_matrix(rows, half):
    target, source = np.mgrid[0:rows, 0 : rows + 2 * half]
    real_part, imag_part = taps(source - half - target, half)
    return np.block([[real_part, -imag_part], [imag_part, real_part]])


def column_matrix(block, edge, half):
    source, target = np.mgrid[0 : block + 2 * edge, 0:block]
    real_part, imag_part = taps(source - edge - target, half)
    return np.block([[real_part, imag_part], [-imag_part, real_part]])


def split(value):
    high = value.astype(jnp.bfloat16)
    low = (value - high.astype(jnp.float32)).astype(jnp.bfloat16)
    return high, low


def dot(a, b):
    return jnp.dot(a, b, preferred_element_type=jnp.float32)


def transmitted(delta, beta):
    u = delta - 0.5
    amp = jnp.exp(-beta)
    square = u * u
    return -amp * (u * series(square, SIN_TERMS)), -amp * series(square, COS_TERMS)


def body(
    depths, tiles, views, rows, cols, per_slab,
    incident_ref, delta_ref, beta_ref, rmat_ref, cmat_ref, out_ref,
    loads, first, volume, wave, trans, leaving, rmat_buf, cmat_buf,
    load_sem, first_send, first_recv, vol_send, vol_recv, rim_send, rim_recv, out_send, out_recv, go,
):
    half = HALF
    span = PAIR * rows
    slices = depths * per_slab
    blocks = cols // LANES
    edge = LANES // 2
    d = lax.axis_index("depth")
    t = lax.axis_index("tile")
    pair = t // PAIR
    q = t % PAIR
    pairs = tiles // PAIR
    mine = (d // 2) * PAIR + q
    works = (d % 2 == 0) & (mine < views)
    places = [((v // PAIR) * 2, v % PAIR) for v in range(views)]

    def at_worker(v):
        return (d == (v // PAIR) * 2) & (q == v % PAIR)

    def worker(v):
        return ((v // PAIR) * 2, pair * PAIR + v % PAIR)


    taps_in = [
        pltpu.make_async_copy(rmat_ref, rmat_buf, load_sem.at[0]),
        pltpu.make_async_copy(cmat_ref, cmat_buf, load_sem.at[1]),
    ]
    first_in = [
        pltpu.make_async_copy(incident_ref.at[0], loads.at[0], load_sem.at[2]),
        pltpu.make_async_copy(incident_ref.at[1], loads.at[1], load_sem.at[3]),
        pltpu.make_async_copy(delta_ref.at[:, 0], loads.at[2], load_sem.at[4]),
        pltpu.make_async_copy(beta_ref.at[:, 0], loads.at[3], load_sem.at[5]),
    ]

    @pl.when(d == 0)
    def _():
        for copy in first_in:
            copy.start()

    @pl.when(works)
    def _():
        for copy in taps_in:
            copy.start()

    barrier = pltpu.get_barrier_semaphore()
    for dd in range(depths):
        for qq in range(PAIR):
            here = (d == dd) & (q == qq)
            peer = (dd, pair * PAIR + qq)
            if (dd, qq) in places:

                @pl.when(jnp.logical_not(here))
                def _():
                    pl.semaphore_signal(barrier, inc=1, device_id=peer, device_id_type=MESH)
            else:

                @pl.when(works)
                def _():
                    pl.semaphore_signal(barrier, inc=1, device_id=peer, device_id_type=MESH)

    has_up = works & (pair > 0)
    has_down = works & (pair < pairs - 1)
    up = (d, jnp.maximum(t - PAIR, 0))
    down = (d, jnp.minimum(t + PAIR, tiles - 1))

    @pl.when(has_up)
    def _():
        pl.semaphore_signal(barrier, inc=1, device_id=up, device_id_type=MESH)

    @pl.when(has_down)
    def _():
        pl.semaphore_signal(barrier, inc=1, device_id=down, device_id_type=MESH)

    @pl.when(d == 0)
    def _():
        for copy in first_in:
            copy.wait()

        @pl.loop(0, views)
        def _(v):
            @pl.loop(0, rows // STRIP)
            def _(r):
                strip = pl.ds(pl.multiple_of(r * STRIP, STRIP), STRIP)
                real_part, imag_part = transmitted(loads[2, v, strip], loads[3, v, strip])
                wave_re, wave_im = loads[0, v, strip], loads[1, v, strip]
                first[v, 0, strip] = wave_re * real_part - wave_im * imag_part
                first[v, 1, strip] = wave_re * imag_part + wave_im * real_part

    peers = jnp.where(works, depths * PAIR - 1, views)
    pl.semaphore_wait(barrier, peers + has_up.astype(jnp.int32) + has_down.astype(jnp.int32))

    def piece_copy(i, c, v):
        return pltpu.make_async_remote_copy(
            src_ref=(delta_ref, beta_ref)[c].at[v, i],
            dst_ref=volume.at[d * per_slab + i, c, q],
            send_sem=vol_send.at[i, c, v],
            recv_sem=vol_recv.at[d * per_slab + i, c, q],
            device_id=worker(v),
            device_id_type=MESH,
        )

    def send_pieces(i, v):
        here = at_worker(v)

        @pl.when(here)
        def _():
            for c, ref in enumerate((delta_ref, beta_ref)):
                pltpu.make_async_copy(
                    ref.at[v, i], volume.at[d * per_slab + i, c, q], vol_recv.at[d * per_slab + i, c, q]
                ).start()

        @pl.when(jnp.logical_not(here))
        def _():
            for c in range(2):
                piece_copy(i, c, v).start()

    def first_copy(v):
        return pltpu.make_async_remote_copy(
            src_ref=first.at[v],
            dst_ref=wave.at[0, :, pl.ds(half + q * rows, rows)],
            send_sem=first_send.at[v],
            recv_sem=first_recv.at[q],
            device_id=worker(v),
            device_id_type=MESH,
        )

    @pl.when(d == 0)
    def _():
        @pl.loop(0, views)
        def _(v):
            here = at_worker(v)

            @pl.when(here)
            def _():
                pltpu.make_async_copy(
                    first.at[v], wave.at[0, :, pl.ds(half + q * rows, rows)], first_recv.at[q]
                ).start()

            @pl.when(jnp.logical_not(here))
            def _():
                first_copy(v).start()

        @pl.loop(0, views)
        def _(v):
            @pl.when(jnp.logical_not(at_worker(v)))
            def _():
                first_copy(v).wait_send()

        @pl.loop(0, (per_slab - 1) * views)
        def _(k):
            send_pieces(1 + k // views, k % views)

    @pl.when((d > 0) & jnp.logical_not(works))
    def _():
        @pl.loop(0, views)
        def _(v):
            pl.semaphore_wait(go.at[v], 1)

            @pl.loop(0, per_slab)
            def _(i):
                send_pieces(i, v)

    def out_copy(slab, qq):
        return pltpu.make_async_remote_copy(
            src_ref=leaving.at[slab, :, pl.ds(qq * rows, rows)],
            dst_ref=out_ref.at[:, mine, 0],
            send_sem=out_send.at[slab, qq],
            recv_sem=out_recv.at[mine],
            device_id=(slab, pair * PAIR + qq),
            device_id_type=MESH,
        )


    def rim_copy(s, side, h):
        first_row = half if side == 0 else span
        land = span + half if side == 0 else 0
        columns = pl.ds(h * LANES, LANES)
        return pltpu.make_async_remote_copy(
            src_ref=wave.at[s, :, pl.ds(first_row, half), columns],
            dst_ref=wave.at[s, :, pl.ds(land, half), columns],
            send_sem=rim_send.at[s, side, h],
            recv_sem=rim_recv.at[s, 1 - side, h],
            device_id=up if side == 0 else down,
            device_id_type=MESH,
        )

    def send_rims(s, first_block, last_block):
        @pl.when(has_up & (s < slices))
        def _():
            for h in range(first_block, last_block):
                rim_copy(s, 0, h).start()

        @pl.when(has_down & (s < slices))
        def _():
            for h in range(first_block, last_block):
                rim_copy(s, 1, h).start()

    def rim_arrival(s, side, h):
        land = 0 if side == 0 else span + half
        ref = wave.at[s, :, pl.ds(land, half), pl.ds(h * LANES, LANES)]
        return pltpu.make_async_copy(ref, ref, rim_recv.at[s, side, h])

    def transmission(s):
        for c in range(2):
            for qq in range(PAIR):
                ref = volume.at[s, c, qq]
                pltpu.make_async_copy(ref, ref, vol_recv.at[s, c, qq]).wait()
        for qq in range(PAIR):

            @pl.loop(0, rows // STRIP)
            def _(r):
                strip = pl.ds(pl.multiple_of(r * STRIP, STRIP), STRIP)
                land = pl.ds(pl.multiple_of(qq * rows + r * STRIP, STRIP), STRIP)
                real_part, imag_part = transmitted(volume[s, 0, qq, strip], volume[s, 1, qq, strip])
                trans[0, land] = real_part
                trans[1, land] = imag_part

    @pl.when(works)
    def _():
        def clear(first_row):
            @pl.loop(0, slices)
            def _(s):
                wave[s, :, first_row : first_row + half] = jnp.zeros((2, half, cols), jnp.float32)

        @pl.when(pair == 0)
        def _():
            clear(0)

        @pl.when(pair == pairs - 1)
        def _():
            clear(span + half)

        for copy in taps_in:
            copy.wait()
        for qq in range(PAIR):
            ref = wave.at[0, :, pl.ds(half + qq * rows, rows)]
            pltpu.make_async_copy(ref, ref, first_recv.at[qq]).wait()
        send_rims(0, 0, blocks)

        @pl.loop(0, slices)
        def _(s):
            for dd in range(1, depths):

                @pl.when(s == max(0, (dd - 1) * per_slab - 1))
                def _():
                    for qq in range(PAIR):
                        if (dd, qq) in places:

                            @pl.when((d == dd) & (q == qq))
                            def _():
                                @pl.loop(0, per_slab * views)
                                def _(k):
                                    send_pieces(k // views, k % views)
                        else:
                            pl.semaphore_signal(
                                go.at[mine], inc=1, device_id=(dd, pair * PAIR + qq), device_id_type=MESH
                            )

            @pl.when(s < slices - 1)
            def _():
                transmission(s + 1)

            count = 2 * span

            def rows_done(first_block, last_block):
                @pl.when(has_up)
                def _():
                    for h in range(first_block, last_block):
                        rim_arrival(s, 0, h).wait()

                @pl.when(has_down)
                def _():
                    for h in range(first_block, last_block):
                        rim_arrival(s, 1, h).wait()

                columns = slice(first_block * LANES, last_block * LANES)
                width = (last_block - first_block) * LANES
                high, low = split(wave[s, :, :, columns].reshape(2 * (span + 2 * half), width))
                both = dot(rmat_buf[...], high)
                return both[:count] + both[count:] + dot(rmat_buf[:count], low)

            def columns_done(first_block, last_block, pieces):
                high, low = split(pltpu.roll(pieces, pieces.shape[1] - edge, 1))

                def windows(value):
                    return [
                        jnp.concatenate(
                            [
                                value[:span, k * LANES : (k + 2) * LANES],
                                value[span:, k * LANES : (k + 2) * LANES],
                            ],
                            axis=1,
                        )
                        for k in range(last_block - first_block)
                    ]

                high, low = windows(high), windows(low)
                height = span * len(high)
                both = dot(jnp.concatenate(high + low, axis=0), cmat_buf[0])
                result = both[:height] + both[height:] + dot(jnp.concatenate(high, axis=0), cmat_buf[1])
                for k, block in enumerate(range(first_block, last_block)):
                    real_part, imag_part = [
                        result[k * span : (k + 1) * span, part * LANES : (part + 1) * LANES] for part in range(2)
                    ]
                    columns = slice(block * LANES, (block + 1) * LANES)
                    trans_re, trans_im = trans[0, :, columns], trans[1, :, columns]
                    wave[s + 1, 0, half : half + span, columns] = real_part * trans_re - imag_part * trans_im
                    wave[s + 1, 1, half : half + span, columns] = real_part * trans_im + imag_part * trans_re
                    leaving[s // per_slab, 0, :, columns] = real_part
                    leaving[s // per_slab, 1, :, columns] = imag_part

            outside = jnp.zeros((count, LANES), jnp.float32)
            made = []
            for first_block in range(0, blocks, GROUP):
                last_block = min(first_block + GROUP, blocks)
                for wanted in (last_block, min(last_block + 1, blocks)):
                    if len(made) < wanted:
                        joined = rows_done(len(made), wanted)
                        made += [joined[:, k : k + LANES] for k in range(0, joined.shape[1], LANES)]
                pieces = [
                    made[k] if 0 <= k < blocks else outside for k in range(first_block - 1, last_block + 1)
                ]
                columns_done(first_block, last_block, jnp.concatenate(pieces, axis=1))
                send_rims(s + 1, first_block, last_block)

            @pl.when(s % per_slab == per_slab - 1)
            def _():
                slab = s // per_slab
                for qq in range(PAIR):
                    here = (d == slab) & (q == qq)

                    @pl.when(here)
                    def _():
                        pltpu.make_async_copy(
                            leaving.at[slab, :, pl.ds(qq * rows, rows)], out_ref.at[:, mine, 0], out_recv.at[mine]
                        ).start()

                    @pl.when(jnp.logical_not(here))
                    def _():
                        out_copy(slab, qq).start()

    @pl.loop(0, per_slab * views)
    def _(k):
        i, v = k // views, k % views

        @pl.when(jnp.logical_not(at_worker(v)) & ((d > 0) | (i > 0)))
        def _():
            for c in range(2):
                piece_copy(i, c, v).wait_send()

    for v in range(views):
        ref = out_ref.at[:, v, 0]
        pltpu.make_async_copy(ref, ref, out_recv.at[v]).wait()

    @pl.when(works)
    def _():
        @pl.loop(0, slices)
        def _(s):
            @pl.loop(0, blocks)
            def _(h):
                @pl.when(has_up)
                def _():
                    rim_copy(s, 0, h).wait_send()

                @pl.when(has_down)
                def _():
                    rim_copy(s, 1, h).wait_send()

        @pl.loop(0, depths)
        def _(slab):
            for qq in range(PAIR):

                @pl.when(jnp.logical_not((d == slab) & (q == qq)))
                def _():
                    out_copy(slab, qq).wait_send()


def in_order(views, order_ref, value_ref, out_ref):
    for k in range(views):
        out_ref[:, k] = value_ref[:, order_ref[k]]


def per_device(depths, tiles, incident, delta, beta, view_order):
    half = HALF
    _, views, rows, cols = incident.shape
    per_slab = delta.shape[1]
    slices = per_slab * depths
    span = PAIR * rows
    edge = LANES // 2
    rmat = jnp.asarray(np.concatenate(in_two(row_matrix(span, half)), axis=0))
    cmat = jnp.asarray(np.stack(in_two(column_matrix(LANES, edge, half))))
    anywhere = pl.BlockSpec(memory_space=pl.ANY)
    hbm = pl.BlockSpec(memory_space=pltpu.HBM)
    vmem = pl.BlockSpec(memory_space=pltpu.VMEM)
    shape = jax.ShapeDtypeStruct((2, views, 1, rows, cols), jnp.float32)
    f32 = jnp.float32
    dma = pltpu.SemaphoreType.DMA
    by_view = pl.pallas_call(
        functools.partial(body, depths, tiles, views, rows, cols, per_slab),
        out_shape=shape,
        in_specs=[hbm] * 5,
        out_specs=anywhere,
        scratch_shapes=[
            pltpu.VMEM((4, views, rows, cols), f32),
            pltpu.VMEM((views, 2, rows, cols), f32),
            pltpu.VMEM((slices, 2, PAIR, rows, cols), f32),
            pltpu.VMEM((slices + 1, 2, span + 2 * half, cols), f32),
            pltpu.VMEM((2, span, cols), f32),
            pltpu.VMEM((depths, 2, span, cols), f32),
            pltpu.VMEM(rmat.shape, rmat.dtype),
            pltpu.VMEM(cmat.shape, cmat.dtype),
            dma((6,)),
            dma((views,)),
            dma((PAIR,)),
            dma((per_slab, 2, views)),
            dma((slices, 2, PAIR)),
            dma((slices, 2, cols // LANES)),
            dma((slices, 2, cols // LANES)),
            dma((depths, PAIR)),
            dma((views,)),
            pltpu.SemaphoreType.REGULAR((views,)),
        ],
        compiler_params=pltpu.CompilerParams(
            collective_id=0, has_side_effects=True, vmem_limit_bytes=63 * 1024 * 1024
        ),
        name="views_by_worker",
    )(incident, delta, beta, rmat, cmat)
    return pl.pallas_call(
        functools.partial(in_order, views),
        out_shape=shape,
        in_specs=[pl.BlockSpec(memory_space=pltpu.SMEM), vmem],
        out_specs=vmem,
        name="stored_order",
    )(view_order, by_view)


def solution(mesh):
    return jax.shard_map(
        functools.partial(per_device, mesh.shape["depth"], mesh.shape["tile"]),
        mesh=mesh,
        in_specs=(
            P(None, None, "tile", None),
            P(None, "depth", "tile", None),
            P(None, "depth", "tile", None),
            P(),
        ),
        out_specs=P(None, None, "depth", "tile", None),
        check_vma=False,
    )
```

```python
import functools

import jax
import jax.numpy as jnp
import ml_dtypes
import numpy as np
from jax import lax
from jax.experimental import pallas as pl
from jax.experimental.pallas import tpu as pltpu
from jax.sharding import PartitionSpec as P

HALF = 32
LANES = 128
PAIR = 2
GROUP = 1
STRIP = 8
MESH = pl.DeviceIdType.MESH

SIN_TERMS = (
    3.1415926535897931,
    -5.1677127800499694,
    2.5501640398773450,
    -0.59926452932079199,
    0.082145886611128236,
    -0.0073704309457143504,
    0.00046630280576761250,
)
COS_TERMS = (
    1.0,
    -4.9348022005446790,
    4.0587121264167676,
    -1.3352627688545893,
    0.23533063035889312,
    -0.025806891390014061,
    0.0019295743094039231,
    -0.00010463810492484570,
)


def series(square, terms):
    total = jnp.full_like(square, terms[-1])
    for term in terms[-2::-1]:
        total = total * square + term
    return total


def taps(offset, half):
    grid = np.arange(-half, half + 1, dtype=np.float64)
    norm = np.abs(
        np.sum((0.75 + 0.25 * np.cos(np.pi * grid / (half + 1))) * np.exp(1j * np.pi * grid**2 / (6.25 * half)))
    )
    place = offset.astype(np.float64)
    value = (0.75 + 0.25 * np.cos(np.pi * place / (half + 1))) * np.exp(1j * np.pi * place**2 / (6.25 * half))
    value = np.where(np.abs(offset) <= half, value / norm, 0.0)
    return value.real, value.imag


def in_two(matrix):
    matrix = matrix.astype(np.float32)
    high = matrix.astype(ml_dtypes.bfloat16)
    low = (matrix - high.astype(np.float32)).astype(ml_dtypes.bfloat16)
    return high, low


def row_matrix(rows, half):
    target, source = np.mgrid[0:rows, 0 : rows + 2 * half]
    real_part, imag_part = taps(source - half - target, half)
    return np.block([[real_part, -imag_part], [imag_part, real_part]])


def column_matrix(block, edge, half):
    source, target = np.mgrid[0 : block + 2 * edge, 0:block]
    real_part, imag_part = taps(source - edge - target, half)
    return np.block([[real_part, imag_part], [-imag_part, real_part]])


def split(value):
    high = value.astype(jnp.bfloat16)
    low = (value - high.astype(jnp.float32)).astype(jnp.bfloat16)
    return high, low


def dot(a, b):
    return jnp.dot(a, b, preferred_element_type=jnp.float32)


def transmitted(delta, beta):
    u = delta - 0.5
    amp = jnp.exp(-beta)
    square = u * u
    return -amp * (u * series(square, SIN_TERMS)), -amp * series(square, COS_TERMS)


def body(
    depths, tiles, views, rows, cols, per_slab,
    incident_ref, delta_ref, beta_ref, rmat_ref, cmat_ref, out_ref,
    loads, first, volume, wave, trans, leaving, rmat_buf, cmat_buf,
    load_sem, first_send, first_recv, vol_send, vol_recv, rim_send, rim_recv, out_send, out_recv, go,
):
    half = HALF
    span = PAIR * rows
    slices = depths * per_slab
    blocks = cols // LANES
    edge = LANES // 2
    d = lax.axis_index("depth")
    t = lax.axis_index("tile")
    pair = t // PAIR
    q = t % PAIR
    pairs = tiles // PAIR
    mine = (d // 2) * PAIR + q
    works = (d % 2 == 0) & (mine < views)
    places = [((v // PAIR) * 2, v % PAIR) for v in range(views)]

    def at_worker(v):
        return (d == (v // PAIR) * 2) & (q == v % PAIR)

    def worker(v):
        return ((v // PAIR) * 2, pair * PAIR + v % PAIR)


    taps_in = [
        pltpu.make_async_copy(rmat_ref, rmat_buf, load_sem.at[0]),
        pltpu.make_async_copy(cmat_ref, cmat_buf, load_sem.at[1]),
    ]
    first_in = [
        pltpu.make_async_copy(incident_ref.at[0], loads.at[0], load_sem.at[2]),
        pltpu.make_async_copy(incident_ref.at[1], loads.at[1], load_sem.at[3]),
        pltpu.make_async_copy(delta_ref.at[:, 0], loads.at[2], load_sem.at[4]),
        pltpu.make_async_copy(beta_ref.at[:, 0], loads.at[3], load_sem.at[5]),
    ]

    @pl.when(d == 0)
    def _():
        for copy in first_in:
            copy.start()

    @pl.when(works)
    def _():
        for copy in taps_in:
            copy.start()

    barrier = pltpu.get_barrier_semaphore()
    for dd in range(depths):
        for qq in range(PAIR):
            here = (d == dd) & (q == qq)
            peer = (dd, pair * PAIR + qq)
            if (dd, qq) in places:

                @pl.when(jnp.logical_not(here))
                def _():
                    pl.semaphore_signal(barrier, inc=1, device_id=peer, device_id_type=MESH)
            else:

                @pl.when(works)
                def _():
                    pl.semaphore_signal(barrier, inc=1, device_id=peer, device_id_type=MESH)

    has_up = works & (pair > 0)
    has_down = works & (pair < pairs - 1)
    up = (d, jnp.maximum(t - PAIR, 0))
    down = (d, jnp.minimum(t + PAIR, tiles - 1))

    @pl.when(has_up)
    def _():
        pl.semaphore_signal(barrier, inc=1, device_id=up, device_id_type=MESH)

    @pl.when(has_down)
    def _():
        pl.semaphore_signal(barrier, inc=1, device_id=down, device_id_type=MESH)

    @pl.when(d == 0)
    def _():
        for copy in first_in:
            copy.wait()

        @pl.loop(0, views)
        def _(v):
            @pl.loop(0, rows // STRIP)
            def _(r):
                strip = pl.ds(pl.multiple_of(r * STRIP, STRIP), STRIP)
                real_part, imag_part = transmitted(loads[2, v, strip], loads[3, v, strip])
                wave_re, wave_im = loads[0, v, strip], loads[1, v, strip]
                first[v, 0, strip] = wave_re * real_part - wave_im * imag_part
                first[v, 1, strip] = wave_re * imag_part + wave_im * real_part

    peers = jnp.where(works, depths * PAIR - 1, views)
    pl.semaphore_wait(barrier, peers + has_up.astype(jnp.int32) + has_down.astype(jnp.int32))

    def piece_copy(i, c, v):
        return pltpu.make_async_remote_copy(
            src_ref=(delta_ref, beta_ref)[c].at[v, i],
            dst_ref=volume.at[d * per_slab + i, c, q],
            send_sem=vol_send.at[i, c, v],
            recv_sem=vol_recv.at[d * per_slab + i, c, q],
            device_id=worker(v),
            device_id_type=MESH,
        )

    def send_pieces(i, v):
        here = at_worker(v)

        @pl.when(here)
        def _():
            for c, ref in enumerate((delta_ref, beta_ref)):
                pltpu.make_async_copy(
                    ref.at[v, i], volume.at[d * per_slab + i, c, q], vol_recv.at[d * per_slab + i, c, q]
                ).start()

        @pl.when(jnp.logical_not(here))
        def _():
            for c in range(2):
                piece_copy(i, c, v).start()

    def first_copy(v):
        return pltpu.make_async_remote_copy(
            src_ref=first.at[v],
            dst_ref=wave.at[0, :, pl.ds(half + q * rows, rows)],
            send_sem=first_send.at[v],
            recv_sem=first_recv.at[q],
            device_id=worker(v),
            device_id_type=MESH,
        )

    @pl.when(d == 0)
    def _():
        @pl.loop(0, views)
        def _(v):
            here = at_worker(v)

            @pl.when(here)
            def _():
                pltpu.make_async_copy(
                    first.at[v], wave.at[0, :, pl.ds(half + q * rows, rows)], first_recv.at[q]
                ).start()

            @pl.when(jnp.logical_not(here))
            def _():
                first_copy(v).start()

        @pl.loop(0, views)
        def _(v):
            @pl.when(jnp.logical_not(at_worker(v)))
            def _():
                first_copy(v).wait_send()

        @pl.loop(0, (per_slab - 1) * views)
        def _(k):
            send_pieces(1 + k // views, k % views)

    @pl.when((d > 0) & jnp.logical_not(works))
    def _():
        @pl.loop(0, views)
        def _(v):
            pl.semaphore_wait(go.at[v], 1)

            @pl.loop(0, per_slab)
            def _(i):
                send_pieces(i, v)

    def out_copy(slab, qq):
        return pltpu.make_async_remote_copy(
            src_ref=leaving.at[slab, :, pl.ds(qq * rows, rows)],
            dst_ref=out_ref.at[:, mine, 0],
            send_sem=out_send.at[slab, qq],
            recv_sem=out_recv.at[mine],
            device_id=(slab, pair * PAIR + qq),
            device_id_type=MESH,
        )


    def rim_copy(s, side, h):
        first_row = half if side == 0 else span
        land = span + half if side == 0 else 0
        columns = pl.ds(h * LANES, LANES)
        return pltpu.make_async_remote_copy(
            src_ref=wave.at[s, :, pl.ds(first_row, half), columns],
            dst_ref=wave.at[s, :, pl.ds(land, half), columns],
            send_sem=rim_send.at[s, side, h],
            recv_sem=rim_recv.at[s, 1 - side, h],
            device_id=up if side == 0 else down,
            device_id_type=MESH,
        )

    def send_rims(s, first_block, last_block):
        @pl.when(has_up & (s < slices))
        def _():
            for h in range(first_block, last_block):
                rim_copy(s, 0, h).start()

        @pl.when(has_down & (s < slices))
        def _():
            for h in range(first_block, last_block):
                rim_copy(s, 1, h).start()

    def rim_arrival(s, side, h):
        land = 0 if side == 0 else span + half
        ref = wave.at[s, :, pl.ds(land, half), pl.ds(h * LANES, LANES)]
        return pltpu.make_async_copy(ref, ref, rim_recv.at[s, side, h])

    def transmission(s):
        for c in range(2):
            for qq in range(PAIR):
                ref = volume.at[s, c, qq]
                pltpu.make_async_copy(ref, ref, vol_recv.at[s, c, qq]).wait()
        for qq in range(PAIR):

            @pl.loop(0, rows // STRIP)
            def _(r):
                strip = pl.ds(pl.multiple_of(r * STRIP, STRIP), STRIP)
                land = pl.ds(pl.multiple_of(qq * rows + r * STRIP, STRIP), STRIP)
                real_part, imag_part = transmitted(volume[s, 0, qq, strip], volume[s, 1, qq, strip])
                trans[0, land] = real_part
                trans[1, land] = imag_part

    @pl.when(works)
    def _():
        def clear(first_row):
            @pl.loop(0, slices)
            def _(s):
                wave[s, :, first_row : first_row + half] = jnp.zeros((2, half, cols), jnp.float32)

        @pl.when(pair == 0)
        def _():
            clear(0)

        @pl.when(pair == pairs - 1)
        def _():
            clear(span + half)

        for copy in taps_in:
            copy.wait()
        for qq in range(PAIR):
            ref = wave.at[0, :, pl.ds(half + qq * rows, rows)]
            pltpu.make_async_copy(ref, ref, first_recv.at[qq]).wait()
        send_rims(0, 0, blocks)

        @pl.loop(0, slices)
        def _(s):
            for dd in range(1, depths):

                @pl.when(s == max(0, (dd - 1) * per_slab - 1))
                def _():
                    for qq in range(PAIR):
                        if (dd, qq) in places:

                            @pl.when((d == dd) & (q == qq))
                            def _():
                                @pl.loop(0, per_slab * views)
                                def _(k):
                                    send_pieces(k // views, k % views)
                        else:
                            pl.semaphore_signal(
                                go.at[mine], inc=1, device_id=(dd, pair * PAIR + qq), device_id_type=MESH
                            )

            count = 2 * span

            def rows_done(first_block, last_block):
                @pl.when(has_up)
                def _():
                    for h in range(first_block, last_block):
                        rim_arrival(s, 0, h).wait()

                @pl.when(has_down)
                def _():
                    for h in range(first_block, last_block):
                        rim_arrival(s, 1, h).wait()

                columns = slice(first_block * LANES, last_block * LANES)
                width = (last_block - first_block) * LANES
                high, low = split(wave[s, :, :, columns].reshape(2 * (span + 2 * half), width))
                both = dot(rmat_buf[...], high)
                return both[:count] + both[count:] + dot(rmat_buf[:count], low)

            def columns_done(first_block, last_block, pieces):
                high, low = split(pltpu.roll(pieces, pieces.shape[1] - edge, 1))

                def windows(value):
                    return [
                        jnp.concatenate(
                            [
                                value[:span, k * LANES : (k + 2) * LANES],
                                value[span:, k * LANES : (k + 2) * LANES],
                            ],
                            axis=1,
                        )
                        for k in range(last_block - first_block)
                    ]

                high, low = windows(high), windows(low)
                height = span * len(high)
                both = dot(jnp.concatenate(high + low, axis=0), cmat_buf[0])
                result = both[:height] + both[height:] + dot(jnp.concatenate(high, axis=0), cmat_buf[1])
                for k, block in enumerate(range(first_block, last_block)):
                    real_part, imag_part = [
                        result[k * span : (k + 1) * span, part * LANES : (part + 1) * LANES] for part in range(2)
                    ]
                    columns = slice(block * LANES, (block + 1) * LANES)
                    trans_re, trans_im = trans[0, :, columns], trans[1, :, columns]
                    wave[s + 1, 0, half : half + span, columns] = real_part * trans_re - imag_part * trans_im
                    wave[s + 1, 1, half : half + span, columns] = real_part * trans_im + imag_part * trans_re
                    leaving[s // per_slab, 0, :, columns] = real_part
                    leaving[s // per_slab, 1, :, columns] = imag_part

            outside = jnp.zeros((count, LANES), jnp.float32)
            made = []
            for first_block in range(0, blocks, GROUP):
                last_block = min(first_block + GROUP, blocks)
                for wanted in (last_block, min(last_block + 1, blocks)):
                    if len(made) < wanted:
                        joined = rows_done(len(made), wanted)
                        made += [joined[:, k : k + LANES] for k in range(0, joined.shape[1], LANES)]
                if first_block == 0:

                    @pl.when(s < slices - 1)
                    def _():
                        transmission(s + 1)

                pieces = [
                    made[k] if 0 <= k < blocks else outside for k in range(first_block - 1, last_block + 1)
                ]
                columns_done(first_block, last_block, jnp.concatenate(pieces, axis=1))
                send_rims(s + 1, first_block, last_block)

            @pl.when(s % per_slab == per_slab - 1)
            def _():
                slab = s // per_slab
                for qq in range(PAIR):
                    here = (d == slab) & (q == qq)

                    @pl.when(here)
                    def _():
                        pltpu.make_async_copy(
                            leaving.at[slab, :, pl.ds(qq * rows, rows)], out_ref.at[:, mine, 0], out_recv.at[mine]
                        ).start()

                    @pl.when(jnp.logical_not(here))
                    def _():
                        out_copy(slab, qq).start()

    @pl.loop(0, per_slab * views)
    def _(k):
        i, v = k // views, k % views

        @pl.when(jnp.logical_not(at_worker(v)) & ((d > 0) | (i > 0)))
        def _():
            for c in range(2):
                piece_copy(i, c, v).wait_send()

    for v in range(views):
        ref = out_ref.at[:, v, 0]
        pltpu.make_async_copy(ref, ref, out_recv.at[v]).wait()

    @pl.when(works)
    def _():
        @pl.loop(0, slices)
        def _(s):
            @pl.loop(0, blocks)
            def _(h):
                @pl.when(has_up)
                def _():
                    rim_copy(s, 0, h).wait_send()

                @pl.when(has_down)
                def _():
                    rim_copy(s, 1, h).wait_send()

        @pl.loop(0, depths)
        def _(slab):
            for qq in range(PAIR):

                @pl.when(jnp.logical_not((d == slab) & (q == qq)))
                def _():
                    out_copy(slab, qq).wait_send()


def in_order(views, order_ref, value_ref, out_ref):
    for k in range(views):
        out_ref[:, k] = value_ref[:, order_ref[k]]


def per_device(depths, tiles, incident, delta, beta, view_order):
    half = HALF
    _, views, rows, cols = incident.shape
    per_slab = delta.shape[1]
    slices = per_slab * depths
    span = PAIR * rows
    edge = LANES // 2
    rmat = jnp.asarray(np.concatenate(in_two(row_matrix(span, half)), axis=0))
    cmat = jnp.asarray(np.stack(in_two(column_matrix(LANES, edge, half))))
    anywhere = pl.BlockSpec(memory_space=pl.ANY)
    hbm = pl.BlockSpec(memory_space=pltpu.HBM)
    vmem = pl.BlockSpec(memory_space=pltpu.VMEM)
    shape = jax.ShapeDtypeStruct((2, views, 1, rows, cols), jnp.float32)
    f32 = jnp.float32
    dma = pltpu.SemaphoreType.DMA
    by_view = pl.pallas_call(
        functools.partial(body, depths, tiles, views, rows, cols, per_slab),
        out_shape=shape,
        in_specs=[hbm] * 5,
        out_specs=anywhere,
        scratch_shapes=[
            pltpu.VMEM((4, views, rows, cols), f32),
            pltpu.VMEM((views, 2, rows, cols), f32),
            pltpu.VMEM((slices, 2, PAIR, rows, cols), f32),
            pltpu.VMEM((slices + 1, 2, span + 2 * half, cols), f32),
            pltpu.VMEM((2, span, cols), f32),
            pltpu.VMEM((depths, 2, span, cols), f32),
            pltpu.VMEM(rmat.shape, rmat.dtype),
            pltpu.VMEM(cmat.shape, cmat.dtype),
            dma((6,)),
            dma((views,)),
            dma((PAIR,)),
            dma((per_slab, 2, views)),
            dma((slices, 2, PAIR)),
            dma((slices, 2, cols // LANES)),
            dma((slices, 2, cols // LANES)),
            dma((depths, PAIR)),
            dma((views,)),
            pltpu.SemaphoreType.REGULAR((views,)),
        ],
        compiler_params=pltpu.CompilerParams(
            collective_id=0, has_side_effects=True, vmem_limit_bytes=63 * 1024 * 1024
        ),
        name="views_by_worker",
    )(incident, delta, beta, rmat, cmat)
    return pl.pallas_call(
        functools.partial(in_order, views),
        out_shape=shape,
        in_specs=[pl.BlockSpec(memory_space=pltpu.SMEM), vmem],
        out_specs=vmem,
        name="stored_order",
    )(view_order, by_view)


def solution(mesh):
    return jax.shard_map(
        functools.partial(per_device, mesh.shape["depth"], mesh.shape["tile"]),
        mesh=mesh,
        in_specs=(
            P(None, None, "tile", None),
            P(None, "depth", "tile", None),
            P(None, "depth", "tile", None),
            P(),
        ),
        out_specs=P(None, None, "depth", "tile", None),
        check_vma=False,
    )
```

```python
import functools

import jax
import jax.numpy as jnp
import ml_dtypes
import numpy as np
from jax import lax
from jax.experimental import pallas as pl
from jax.experimental.pallas import tpu as pltpu
from jax.sharding import PartitionSpec as P

HALF = 32
LANES = 128
PAIR = 2
GROUP = 1
STRIP = 8
MESH = pl.DeviceIdType.MESH

SIN_TERMS = (
    3.1415926535897931,
    -5.1677127800499694,
    2.5501640398773450,
    -0.59926452932079199,
    0.082145886611128236,
    -0.0073704309457143504,
    0.00046630280576761250,
)
COS_TERMS = (
    1.0,
    -4.9348022005446790,
    4.0587121264167676,
    -1.3352627688545893,
    0.23533063035889312,
    -0.025806891390014061,
    0.0019295743094039231,
    -0.00010463810492484570,
)


def series(square, terms):
    total = jnp.full_like(square, terms[-1])
    for term in terms[-2::-1]:
        total = total * square + term
    return total


def taps(offset, half):
    grid = np.arange(-half, half + 1, dtype=np.float64)
    norm = np.abs(
        np.sum((0.75 + 0.25 * np.cos(np.pi * grid / (half + 1))) * np.exp(1j * np.pi * grid**2 / (6.25 * half)))
    )
    place = offset.astype(np.float64)
    value = (0.75 + 0.25 * np.cos(np.pi * place / (half + 1))) * np.exp(1j * np.pi * place**2 / (6.25 * half))
    value = np.where(np.abs(offset) <= half, value / norm, 0.0)
    return value.real, value.imag


def in_two(matrix):
    matrix = matrix.astype(np.float32)
    high = matrix.astype(ml_dtypes.bfloat16)
    low = (matrix - high.astype(np.float32)).astype(ml_dtypes.bfloat16)
    return high, low


def row_matrix(rows, half):
    target, source = np.mgrid[0:rows, 0 : rows + 2 * half]
    real_part, imag_part = taps(source - half - target, half)
    return np.block([[real_part, -imag_part], [imag_part, real_part]])


def column_matrix(block, edge, half):
    source, target = np.mgrid[0 : block + 2 * edge, 0:block]
    real_part, imag_part = taps(source - edge - target, half)
    return np.block([[real_part, imag_part], [-imag_part, real_part]])


def split(value):
    high = value.astype(jnp.bfloat16)
    low = (value - high.astype(jnp.float32)).astype(jnp.bfloat16)
    return high, low


def dot(a, b):
    return jnp.dot(a, b, preferred_element_type=jnp.float32)


def transmitted(delta, beta):
    u = delta - 0.5
    amp = jnp.exp(-beta)
    square = u * u
    return -amp * (u * series(square, SIN_TERMS)), -amp * series(square, COS_TERMS)


def body(
    depths, tiles, views, rows, cols, per_slab,
    incident_ref, delta_ref, beta_ref, rmat_ref, cmat_ref, out_ref,
    loads, first, volume, wave, trans, leaving, rmat_buf, cmat_buf,
    load_sem, first_send, first_recv, vol_send, vol_recv, rim_send, rim_recv, out_send, out_recv, go,
):
    half = HALF
    span = PAIR * rows
    slices = depths * per_slab
    blocks = cols // LANES
    edge = LANES // 2
    d = lax.axis_index("depth")
    t = lax.axis_index("tile")
    pair = t // PAIR
    q = t % PAIR
    pairs = tiles // PAIR
    mine = (d // 2) * PAIR + q
    works = (d % 2 == 0) & (mine < views)
    places = [((v // PAIR) * 2, v % PAIR) for v in range(views)]

    def at_worker(v):
        return (d == (v // PAIR) * 2) & (q == v % PAIR)

    def worker(v):
        return ((v // PAIR) * 2, pair * PAIR + v % PAIR)


    taps_in = [
        pltpu.make_async_copy(rmat_ref, rmat_buf, load_sem.at[0]),
        pltpu.make_async_copy(cmat_ref, cmat_buf, load_sem.at[1]),
    ]
    first_in = [
        pltpu.make_async_copy(incident_ref.at[0], loads.at[0], load_sem.at[2]),
        pltpu.make_async_copy(incident_ref.at[1], loads.at[1], load_sem.at[3]),
        pltpu.make_async_copy(delta_ref.at[:, 0], loads.at[2], load_sem.at[4]),
        pltpu.make_async_copy(beta_ref.at[:, 0], loads.at[3], load_sem.at[5]),
    ]

    @pl.when(d == 0)
    def _():
        for copy in first_in:
            copy.start()

    @pl.when(works)
    def _():
        for copy in taps_in:
            copy.start()

    barrier = pltpu.get_barrier_semaphore()
    for dd in range(depths):
        for qq in range(PAIR):
            here = (d == dd) & (q == qq)
            peer = (dd, pair * PAIR + qq)
            if (dd, qq) in places:

                @pl.when(jnp.logical_not(here))
                def _():
                    pl.semaphore_signal(barrier, inc=1, device_id=peer, device_id_type=MESH)
            else:

                @pl.when(works)
                def _():
                    pl.semaphore_signal(barrier, inc=1, device_id=peer, device_id_type=MESH)

    has_up = works & (pair > 0)
    has_down = works & (pair < pairs - 1)
    up = (d, jnp.maximum(t - PAIR, 0))
    down = (d, jnp.minimum(t + PAIR, tiles - 1))

    @pl.when(has_up)
    def _():
        pl.semaphore_signal(barrier, inc=1, device_id=up, device_id_type=MESH)

    @pl.when(has_down)
    def _():
        pl.semaphore_signal(barrier, inc=1, device_id=down, device_id_type=MESH)

    @pl.when(d == 0)
    def _():
        for copy in first_in:
            copy.wait()

        @pl.loop(0, views)
        def _(v):
            @pl.loop(0, rows // STRIP)
            def _(r):
                strip = pl.ds(pl.multiple_of(r * STRIP, STRIP), STRIP)
                real_part, imag_part = transmitted(loads[2, v, strip], loads[3, v, strip])
                wave_re, wave_im = loads[0, v, strip], loads[1, v, strip]
                first[v, 0, strip] = wave_re * real_part - wave_im * imag_part
                first[v, 1, strip] = wave_re * imag_part + wave_im * real_part

    peers = jnp.where(works, depths * PAIR - 1, views)
    pl.semaphore_wait(barrier, peers + has_up.astype(jnp.int32) + has_down.astype(jnp.int32))

    def piece_copy(i, c, v):
        return pltpu.make_async_remote_copy(
            src_ref=(delta_ref, beta_ref)[c].at[v, i],
            dst_ref=volume.at[d * per_slab + i, c, q],
            send_sem=vol_send.at[i, c, v],
            recv_sem=vol_recv.at[d * per_slab + i, c, q],
            device_id=worker(v),
            device_id_type=MESH,
        )

    def send_pieces(i, v):
        here = at_worker(v)

        @pl.when(here)
        def _():
            for c, ref in enumerate((delta_ref, beta_ref)):
                pltpu.make_async_copy(
                    ref.at[v, i], volume.at[d * per_slab + i, c, q], vol_recv.at[d * per_slab + i, c, q]
                ).start()

        @pl.when(jnp.logical_not(here))
        def _():
            for c in range(2):
                piece_copy(i, c, v).start()

    def first_copy(v):
        return pltpu.make_async_remote_copy(
            src_ref=first.at[v],
            dst_ref=wave.at[0, :, pl.ds(half + q * rows, rows)],
            send_sem=first_send.at[v],
            recv_sem=first_recv.at[q],
            device_id=worker(v),
            device_id_type=MESH,
        )

    @pl.when(d == 0)
    def _():
        @pl.loop(0, views)
        def _(v):
            here = at_worker(v)

            @pl.when(here)
            def _():
                pltpu.make_async_copy(
                    first.at[v], wave.at[0, :, pl.ds(half + q * rows, rows)], first_recv.at[q]
                ).start()

            @pl.when(jnp.logical_not(here))
            def _():
                first_copy(v).start()

        @pl.loop(0, views)
        def _(v):
            @pl.when(jnp.logical_not(at_worker(v)))
            def _():
                first_copy(v).wait_send()

        @pl.loop(0, (per_slab - 1) * views)
        def _(k):
            send_pieces(1 + k // views, k % views)

    @pl.when((d > 0) & jnp.logical_not(works))
    def _():
        @pl.loop(0, views)
        def _(v):
            pl.semaphore_wait(go.at[v], 1)

            @pl.loop(0, per_slab)
            def _(i):
                send_pieces(i, v)

    def out_copy(slab, qq):
        return pltpu.make_async_remote_copy(
            src_ref=leaving.at[slab, :, pl.ds(qq * rows, rows)],
            dst_ref=out_ref.at[:, mine, 0],
            send_sem=out_send.at[slab, qq],
            recv_sem=out_recv.at[mine],
            device_id=(slab, pair * PAIR + qq),
            device_id_type=MESH,
        )


    def rim_copy(s, side, h):
        first_row = half if side == 0 else span
        land = span + half if side == 0 else 0
        columns = pl.ds(h * LANES, LANES)
        return pltpu.make_async_remote_copy(
            src_ref=wave.at[s, :, pl.ds(first_row, half), columns],
            dst_ref=wave.at[s, :, pl.ds(land, half), columns],
            send_sem=rim_send.at[s, side, h],
            recv_sem=rim_recv.at[s, 1 - side, h],
            device_id=up if side == 0 else down,
            device_id_type=MESH,
        )

    def send_rims(s, first_block, last_block):
        @pl.when(has_up & (s < slices))
        def _():
            for h in range(first_block, last_block):
                rim_copy(s, 0, h).start()

        @pl.when(has_down & (s < slices))
        def _():
            for h in range(first_block, last_block):
                rim_copy(s, 1, h).start()

    def rim_arrival(s, side, h):
        land = 0 if side == 0 else span + half
        ref = wave.at[s, :, pl.ds(land, half), pl.ds(h * LANES, LANES)]
        return pltpu.make_async_copy(ref, ref, rim_recv.at[s, side, h])

    def transmission(s):
        for c in range(2):
            for qq in range(PAIR):
                ref = volume.at[s, c, qq]
                pltpu.make_async_copy(ref, ref, vol_recv.at[s, c, qq]).wait()
        for qq in range(PAIR):

            @pl.loop(0, rows // STRIP)
            def _(r):
                strip = pl.ds(pl.multiple_of(r * STRIP, STRIP), STRIP)
                land = pl.ds(pl.multiple_of(qq * rows + r * STRIP, STRIP), STRIP)
                real_part, imag_part = transmitted(volume[s, 0, qq, strip], volume[s, 1, qq, strip])
                trans[0, land] = real_part
                trans[1, land] = imag_part

    @pl.when(works)
    def _():
        def clear(first_row):
            @pl.loop(0, slices)
            def _(s):
                wave[s, :, first_row : first_row + half] = jnp.zeros((2, half, cols), jnp.float32)

        @pl.when(pair == 0)
        def _():
            clear(0)

        @pl.when(pair == pairs - 1)
        def _():
            clear(span + half)

        for copy in taps_in:
            copy.wait()
        for qq in range(PAIR):
            ref = wave.at[0, :, pl.ds(half + qq * rows, rows)]
            pltpu.make_async_copy(ref, ref, first_recv.at[qq]).wait()
        send_rims(0, 0, blocks)

        @pl.loop(0, slices)
        def _(s):
            for dd in range(1, depths):

                @pl.when(s == max(0, (dd - 1) * per_slab - 1))
                def _():
                    for qq in range(PAIR):
                        if (dd, qq) in places:

                            @pl.when((d == dd) & (q == qq))
                            def _():
                                @pl.loop(0, per_slab * views)
                                def _(k):
                                    send_pieces(k // views, k % views)
                        else:
                            pl.semaphore_signal(
                                go.at[mine], inc=1, device_id=(dd, pair * PAIR + qq), device_id_type=MESH
                            )

            @pl.when(s < slices - 1)
            def _():
                transmission(s + 1)

            count = 2 * span

            def rows_done(first_block, last_block):
                @pl.when(has_up)
                def _():
                    for h in range(first_block, last_block):
                        rim_arrival(s, 0, h).wait()

                @pl.when(has_down)
                def _():
                    for h in range(first_block, last_block):
                        rim_arrival(s, 1, h).wait()

                columns = slice(first_block * LANES, last_block * LANES)
                width = (last_block - first_block) * LANES
                high, low = split(wave[s, :, :, columns].reshape(2 * (span + 2 * half), width))
                both = dot(rmat_buf[...], high)
                return both[:count] + both[count:] + dot(rmat_buf[:count], low)

            def columns_done(first_block, last_block, pieces):
                high, low = split(pltpu.roll(pieces, pieces.shape[1] - edge, 1))

                def windows(value):
                    return [
                        jnp.concatenate(
                            [
                                value[:span, k * LANES : (k + 2) * LANES],
                                value[span:, k * LANES : (k + 2) * LANES],
                            ],
                            axis=1,
                        )
                        for k in range(last_block - first_block)
                    ]

                high, low = windows(high), windows(low)
                height = span * len(high)
                both = dot(jnp.concatenate(high + low, axis=0), cmat_buf[0])
                result = both[:height] + both[height:] + dot(jnp.concatenate(high, axis=0), cmat_buf[1])
                for k, block in enumerate(range(first_block, last_block)):
                    real_part, imag_part = [
                        result[k * span : (k + 1) * span, part * LANES : (part + 1) * LANES] for part in range(2)
                    ]
                    columns = slice(block * LANES, (block + 1) * LANES)
                    trans_re, trans_im = trans[0, :, columns], trans[1, :, columns]
                    wave[s + 1, 0, half : half + span, columns] = real_part * trans_re - imag_part * trans_im
                    wave[s + 1, 1, half : half + span, columns] = real_part * trans_im + imag_part * trans_re
                    leaving[s // per_slab, 0, :, columns] = real_part
                    leaving[s // per_slab, 1, :, columns] = imag_part

            outside = jnp.zeros((count, LANES), jnp.float32)
            made = []
            for first_block in range(0, blocks, GROUP):
                last_block = min(first_block + GROUP, blocks)
                wanted = min(last_block + 1, blocks)
                if len(made) < wanted:
                    joined = rows_done(len(made), wanted)
                    made += [joined[:, k : k + LANES] for k in range(0, joined.shape[1], LANES)]
                pieces = [
                    made[k] if 0 <= k < blocks else outside for k in range(first_block - 1, last_block + 1)
                ]
                columns_done(first_block, last_block, jnp.concatenate(pieces, axis=1))
                send_rims(s + 1, first_block, last_block)

            @pl.when(s % per_slab == per_slab - 1)
            def _():
                slab = s // per_slab
                for qq in range(PAIR):
                    here = (d == slab) & (q == qq)

                    @pl.when(here)
                    def _():
                        pltpu.make_async_copy(
                            leaving.at[slab, :, pl.ds(qq * rows, rows)], out_ref.at[:, mine, 0], out_recv.at[mine]
                        ).start()

                    @pl.when(jnp.logical_not(here))
                    def _():
                        out_copy(slab, qq).start()

    @pl.loop(0, per_slab * views)
    def _(k):
        i, v = k // views, k % views

        @pl.when(jnp.logical_not(at_worker(v)) & ((d > 0) | (i > 0)))
        def _():
            for c in range(2):
                piece_copy(i, c, v).wait_send()

    for v in range(views):
        ref = out_ref.at[:, v, 0]
        pltpu.make_async_copy(ref, ref, out_recv.at[v]).wait()

    @pl.when(works)
    def _():
        @pl.loop(0, slices)
        def _(s):
            @pl.loop(0, blocks)
            def _(h):
                @pl.when(has_up)
                def _():
                    rim_copy(s, 0, h).wait_send()

                @pl.when(has_down)
                def _():
                    rim_copy(s, 1, h).wait_send()

        @pl.loop(0, depths)
        def _(slab):
            for qq in range(PAIR):

                @pl.when(jnp.logical_not((d == slab) & (q == qq)))
                def _():
                    out_copy(slab, qq).wait_send()


def in_order(views, order_ref, value_ref, out_ref):
    for k in range(views):
        out_ref[:, k] = value_ref[:, order_ref[k]]


def per_device(depths, tiles, incident, delta, beta, view_order):
    half = HALF
    _, views, rows, cols = incident.shape
    per_slab = delta.shape[1]
    slices = per_slab * depths
    span = PAIR * rows
    edge = LANES // 2
    rmat = jnp.asarray(np.concatenate(in_two(row_matrix(span, half)), axis=0))
    cmat = jnp.asarray(np.stack(in_two(column_matrix(LANES, edge, half))))
    anywhere = pl.BlockSpec(memory_space=pl.ANY)
    hbm = pl.BlockSpec(memory_space=pltpu.HBM)
    vmem = pl.BlockSpec(memory_space=pltpu.VMEM)
    shape = jax.ShapeDtypeStruct((2, views, 1, rows, cols), jnp.float32)
    f32 = jnp.float32
    dma = pltpu.SemaphoreType.DMA
    by_view = pl.pallas_call(
        functools.partial(body, depths, tiles, views, rows, cols, per_slab),
        out_shape=shape,
        in_specs=[hbm] * 5,
        out_specs=anywhere,
        scratch_shapes=[
            pltpu.VMEM((4, views, rows, cols), f32),
            pltpu.VMEM((views, 2, rows, cols), f32),
            pltpu.VMEM((slices, 2, PAIR, rows, cols), f32),
            pltpu.VMEM((slices + 1, 2, span + 2 * half, cols), f32),
            pltpu.VMEM((2, span, cols), f32),
            pltpu.VMEM((depths, 2, span, cols), f32),
            pltpu.VMEM(rmat.shape, rmat.dtype),
            pltpu.VMEM(cmat.shape, cmat.dtype),
            dma((6,)),
            dma((views,)),
            dma((PAIR,)),
            dma((per_slab, 2, views)),
            dma((slices, 2, PAIR)),
            dma((slices, 2, cols // LANES)),
            dma((slices, 2, cols // LANES)),
            dma((depths, PAIR)),
            dma((views,)),
            pltpu.SemaphoreType.REGULAR((views,)),
        ],
        compiler_params=pltpu.CompilerParams(
            collective_id=0, has_side_effects=True, vmem_limit_bytes=63 * 1024 * 1024
        ),
        name="views_by_worker",
    )(incident, delta, beta, rmat, cmat)
    return pl.pallas_call(
        functools.partial(in_order, views),
        out_shape=shape,
        in_specs=[pl.BlockSpec(memory_space=pltpu.SMEM), vmem],
        out_specs=vmem,
        name="stored_order",
    )(view_order, by_view)


def solution(mesh):
    return jax.shard_map(
        functools.partial(per_device, mesh.shape["depth"], mesh.shape["tile"]),
        mesh=mesh,
        in_specs=(
            P(None, None, "tile", None),
            P(None, "depth", "tile", None),
            P(None, "depth", "tile", None),
            P(),
        ),
        out_specs=P(None, None, "depth", "tile", None),
        check_vma=False,
    )
```
